32 devices in a mesh: dp: 8 (over y, x, core), mp: 4 (over z).
Axes of the slice: x: 2, y: 2, z: 4, core: 2. Of those that a mesh axis runs over, the one named last changes fastest.
Arguments:
- patches: bfloat16 [256, 14, 14, 256], P(('dp', 'mp')), may hold values from -6 to 6
- validity: int32 [256, 14, 14], P(('dp', 'mp')), may hold values from 0 to 1, as said below
- norm_gain: bfloat16 [2, 2, 256], P(None, None, 'mp'), may hold values from 0.099609375 to 1.8984375
- norm_shift: bfloat16 [2, 2, 256], P(None, None, 'mp'), may hold values from -3 to 3
- query_key_value_weight: bfloat16 [2, 256, 3, 256], P(None, None, None, 'mp'), may hold values from -0.375 to 0.375
- entry_bias: bfloat16 [2, 2, 256], P(None, None, 'mp'), may hold values from -3 to 3
- stencil: bfloat16 [2, 10, 256], P(None, None, 'mp'), may hold values from -2 to 2
- mixer_weight: bfloat16 [2, 256, 256], P(None, None, 'mp'), may hold values from -1 to 1
- branch_bias: bfloat16 [2, 2, 256], P(None, None, 'mp'), may hold values from -1.75 to 1.75
- expand_weight: bfloat16 [2, 256, 1024], P(None, None, 'mp'), may hold values from -0.375 to 0.375
- hidden_bias: bfloat16 [2, 1024], P(None, 'mp'), may hold values from -3 to 3
- reduce_weight: bfloat16 [2, 1024, 256], P(None, None, 'mp'), may hold values from -0.1875 to 0.1875
- cotangent: bfloat16 [256, 14, 14, 256], P(('dp', 'mp')), may hold values from -6 to 6
Outputs:
- output: bfloat16 [256, 14, 14, 256], P(('dp', 'mp'))
- patch_grad: bfloat16 [256, 14, 14, 256], P(('dp', 'mp'))
- gain_grad: float32 [2, 2, 256], P(None, None, 'mp')
- shift_grad: float32 [2, 2, 256], P(None, None, 'mp')
- packed_grad: float32 [2, 256, 3, 256], P(None, None, None, 'mp')
- entry_grad: float32 [2, 2, 256], P(None, None, 'mp')
- stencil_grad: float32 [2, 10, 256], P(None, None, 'mp')
- mixer_grad: float32 [2, 256, 256], P(None, None, 'mp')
- branch_grad: float32 [2, 2, 256], P(None, None, 'mp')
- expand_grad: float32 [2, 256, 1024], P(None, None, 'mp')
- hidden_grad: float32 [2, 1024], P(None, 'mp')
- reduce_grad: float32 [2, 1024, 256], P(None, None, 'mp')
The draws below stay inside these ranges and needn't reach their ends.
Inputs may be any that keep to these rules, and one draw needn't show every extreme that they name: validity is 1 on the patches of a crop whose row is below h and whose column is below w, 0 elsewhere, where h and w are whole numbers of 8 to 14 drawn for each crop.
All inputs are finite; a program needn't handle non-finite values.
Results may differ from the reference program's by a relative error of at most 0.025.
Values may be sent and summed in bfloat16 or wider, within the bound.
No kernel may reach another device: no remote copies, remote signals or barrier semaphores. Data moves between devices by JAX's collectives and lax.ppermute only.
A program may use at most 192 MiB of HBM per device.

```python
import jax
import jax.numpy as jnp
from jax import lax

D = 256
HEADS = 8
FF = 1024
GRID = 14
STRIPE = 7
LAYERS = 2
CROP_DEV = 8
CROPS = 256


def draw_validity(key, part):
    key = jax.random.fold_in(key, 7)
    height_key, width_key = jax.random.split(key)
    heights = jax.random.randint(height_key, (CROPS, 1, 1), 8, GRID + 1)
    widths = jax.random.randint(width_key, (CROPS, 1, 1), 8, GRID + 1)
    row_index = lax.broadcasted_iota(jnp.int32, (CROPS, GRID, GRID), 1)
    col_index = lax.broadcasted_iota(jnp.int32, (CROPS, GRID, GRID), 2)
    return ((row_index < heights) & (col_index < widths)).astype(jnp.int32)


def steps_of(own_key, dims, cuts, low, top_value):
    level, own = 1.0, jax.random.fold_in(own_key, 6)
    for axis_at, shards_of in cuts:
        steps = jnp.exp(jax.random.uniform(jax.random.fold_in(own, axis_at), (shards_of,), jnp.float32, low / len(cuts), top_value / len(cuts)))
        level = level * jnp.repeat(steps, dims[axis_at] // shards_of).reshape([-1 if axis == axis_at else 1 for axis in range(len(dims))])
    return level


def scatter_about(key, shape, scale, bound, cuts=(), held_as=jnp.bfloat16):
    loudness = steps_of(key, shape, cuts, -0.22, 0.18) if cuts else 1.0
    drawn = jax.random.normal(key, shape, jnp.float32) * scale * loudness
    return jnp.minimum(jnp.maximum(drawn, -bound), bound).astype(held_as)


def setup_inputs(seed: int = 0) -> dict:
    arg_keys = jax.random.split(jax.random.key(seed), 14)
    return {
        "patches": scatter_about(arg_keys[0], (CROPS, GRID, GRID, D), 1.0, 6.0, ((0, 32),)),
        "validity": draw_validity(jax.random.fold_in(arg_keys[13], 71), 0),
        "norm_gain": jnp.clip(1.0 + 0.18 * jax.random.normal(arg_keys[2], (LAYERS, 2, D), jnp.float32), 0.099609375, 1.8984375).astype(jnp.bfloat16),
        "norm_shift": scatter_about(arg_keys[3], (LAYERS, 2, D), 0.5, 3.0, ((2, 4),)),
        "query_key_value_weight": scatter_about(arg_keys[4], (LAYERS, D, 3, D), D ** -0.5, 0.375, ((3, 4),)),
        "entry_bias": scatter_about(arg_keys[5], (LAYERS, 2, D), 0.5, 3.0, ((2, 4),)),
        "stencil": scatter_about(arg_keys[6], (LAYERS, 10, D), 0.33, 2.0, ((2, 4),)),
        "mixer_weight": scatter_about(arg_keys[7], (LAYERS, D, D), (D // 8) ** -0.5, 1.0, ((2, 4),)),
        "branch_bias": scatter_about(arg_keys[8], (LAYERS, 2, D), 0.3, 1.75, ((2, 4),)),
        "expand_weight": scatter_about(arg_keys[9], (LAYERS, D, FF), D ** -0.5, 0.375, ((2, 4),)),
        "hidden_bias": scatter_about(arg_keys[10], (LAYERS, FF), 0.5, 3.0, ((1, 4),)),
        "reduce_weight": scatter_about(arg_keys[11], (LAYERS, FF, D), FF ** -0.5, 0.1875, ((2, 4),)),
        "cotangent": scatter_about(arg_keys[12], (CROPS, GRID, GRID, D), 1.0, 6.0, ((0, 32),)),
    }


@jax.custom_vjp
def low(v):
    return lax.optimization_barrier(v.astype(jnp.bfloat16)).astype(jnp.float32)

@jax.custom_vjp
def low_back(v):
    return v

def low_keep(v):
    return (low(v), None)

def low_pass(kept, grad):
    return (grad,)

def back_keep(v):
    return (v, None)

def back_low(kept, grad):
    return (low(grad),)
low.defvjp(low_keep, low_pass)
low_back.defvjp(back_keep, back_low)
norm_eps = 1e-05
masked_score = -1e+30
precision_highest_mode = lax.Precision.HIGHEST
root_half = 0.7071067811865476

def layer_norm(values, scales, offsets):
    center = values - lax.optimization_barrier(jnp.mean(values, axis=-1, keepdims=True))
    spread = lax.optimization_barrier(jnp.mean(center * center, axis=-1, keepdims=True))
    return center * lax.rsqrt(spread + norm_eps) * scales + offsets

def shifted(values, row_step, col_step):
    extent = values.shape[1]
    padded = jnp.pad(values, ((0, 0), (1, 1), (1, 1), (0, 0)))
    return padded[:, 1 + row_step:1 + row_step + extent, 1 + col_step:1 + col_step + extent, :]

def stripe_keep(row_step, col_step, channels):
    row_index = lax.broadcasted_iota(jnp.int32, (GRID, GRID), 0)
    col_index = lax.broadcasted_iota(jnp.int32, (GRID, GRID), 1)
    row_moved = row_index + row_step
    col_moved = col_index + col_step
    inside = (row_moved >= 0) & (row_moved < GRID) & (col_moved >= 0) & (col_moved < GRID)
    across = inside & (row_moved // STRIPE == row_index // STRIPE)
    downward = inside & (col_moved // STRIPE == col_index // STRIPE)
    channel = lax.broadcasted_iota(jnp.int32, (channels,), 0)
    return jnp.where(channel[None, None, :] < channels // 2, across[:, :, None], downward[:, :, None]).astype(jnp.float32)

def stencil_apply(valued, taps):
    channels = valued.shape[-1]
    running = jnp.zeros_like(valued) + taps[9]
    for row_step in (-1, 0, 1):
        for col_step in (-1, 0, 1):
            running = running + taps[3 * (row_step + 1) + col_step + 1] * shifted(valued, row_step, col_step) * stripe_keep(row_step, col_step, channels)
    return running

def gelu(values):
    return 0.5 * values * (1.0 + lax.erf(values * root_half))

def split_windows(values):
    crops_here = values.shape[0]
    half = values.shape[3] // 2
    heads = HEADS // 2
    across = values[..., :half].reshape(crops_here, GRID // STRIPE, STRIPE * GRID, heads, half // heads)
    downward = values[..., half:].reshape(crops_here, GRID, GRID // STRIPE, STRIPE, half).transpose(0, 2, 1, 3, 4)
    downward = downward.reshape(crops_here, GRID // STRIPE, GRID * STRIPE, heads, half // heads)
    return (across, downward)

def join_windows(across, downward):
    crops_here = across.shape[0]
    half = across.shape[3] * across.shape[4]
    upper = across.reshape(crops_here, GRID, GRID, half)
    lower = downward.reshape(crops_here, GRID // STRIPE, GRID, STRIPE, half).transpose(0, 2, 1, 3, 4).reshape(crops_here, GRID, GRID, half)
    return jnp.concatenate([upper, lower], axis=-1)

def key_windows(validity):
    crops_here = validity.shape[0]
    across = validity.reshape(crops_here, GRID // STRIPE, STRIPE * GRID)
    downward = validity.reshape(crops_here, GRID, GRID // STRIPE, STRIPE).transpose(0, 2, 1, 3).reshape(crops_here, GRID // STRIPE, GRID * STRIPE)
    return (across, downward)

def attend(query, keyed, valued, keeping):
    factor = query.shape[-1] ** (-0.5)
    scores = jnp.einsum('cwqhd,cwkhd->cwhqk', query, keyed, precision=precision_highest_mode) * factor
    scores = low_back(scores)
    scores = jnp.where(keeping[:, :, None, None, :] > 0, scores, masked_score)
    peak_score = lax.optimization_barrier(jnp.max(scores, axis=-1, keepdims=True))
    raised = jnp.exp(scores - peak_score)
    probs = low(raised / lax.optimization_barrier(jnp.sum(raised, axis=-1, keepdims=True)))
    return jnp.einsum('cwhqk,cwkhd->cwqhd', probs, valued, precision=precision_highest_mode)

def block_forward(state, masks, params):
    scales, offsets, query_key_value_weight, entry_bias, stencil, mixer_weight, branch_bias, expand_weight, hidden_bias, reduce_weight = params
    normalized_input = low(layer_norm(state, scales[0], offsets[0]))
    combined_projection = jnp.einsum('zaht,typ->zahyp', normalized_input, query_key_value_weight, precision=precision_highest_mode)
    query = low(low_back(combined_projection[..., 0, :] + entry_bias[0]))
    keyed = low(low_back(combined_projection[..., 1, :]))
    valued = low(low_back(combined_projection[..., 2, :] + entry_bias[1]))
    query_across, query_down = split_windows(query)
    key_across, key_down = split_windows(keyed)
    value_across, value_down = split_windows(valued)
    keep_across, keep_down = key_windows(masks)
    attended = join_windows(attend(query_across, key_across, value_across, keep_across), attend(query_down, key_down, value_down, keep_down))
    mixed = low(low_back(attended + stencil_apply(valued, stencil)))
    state = state + low_back(jnp.einsum('cijd,dk->cijk', mixed, mixer_weight, precision=precision_highest_mode) + branch_bias[0])
    normed_two = low(layer_norm(state, scales[1], offsets[1]))
    inner = low_back(jnp.einsum('cijd,df->cijf', normed_two, expand_weight, precision=precision_highest_mode) + hidden_bias)
    hidden = low(gelu(inner))
    return state + low_back(jnp.einsum('cijf,fd->cijd', hidden, reduce_weight, precision=precision_highest_mode) + branch_bias[1])

def forward(state, masks, params):
    for layer in range(LAYERS):
        state = block_forward(state, masks, tuple((member[layer] for member in params)))
    return state

def reference(patches, validity, norm_gain, norm_shift, query_key_value_weight, entry_bias, stencil, mixer_weight, branch_bias, expand_weight, hidden_bias, reduce_weight, cotangent):
    weights = tuple((member.astype(jnp.float32) for member in (norm_gain, norm_shift, query_key_value_weight, entry_bias, stencil, mixer_weight, branch_bias, expand_weight, hidden_bias, reduce_weight)))
    group_count = CROPS // CROP_DEV
    group_shape = (group_count, CROP_DEV, GRID, GRID, D)

    def visit(weight_sums, group_item):
        group_crops, group_masks, group_seeds = group_item

        def forward_group(state, params):
            return forward(state, group_masks, params)
        outcome, pullback = jax.vjp(forward_group, group_crops.astype(jnp.float32), weights)
        state_grad, weight_grads = pullback(group_seeds.astype(jnp.float32))
        weight_sums = tuple((running + addend for running, addend in zip(weight_sums, weight_grads)))
        return (weight_sums, (outcome.astype(jnp.bfloat16), state_grad.astype(jnp.bfloat16)))
    zero_grads = tuple((jnp.zeros_like(member) for member in weights))
    weight_sums, (outcomes, state_grads) = lax.scan(visit, zero_grads, (patches.reshape(group_shape), validity.reshape(group_count, CROP_DEV, GRID, GRID), cotangent.reshape(group_shape)))
    full_shape = patches.shape
    return (outcomes.reshape(full_shape), state_grads.reshape(full_shape), weight_sums[0], weight_sums[1], weight_sums[2], weight_sums[3], weight_sums[4], weight_sums[5], weight_sums[6], weight_sums[7], weight_sums[8], weight_sums[9])
```

```python
import functools

import jax
import jax.numpy as jnp
from jax import lax
from jax.experimental import pallas as pl
from jax.experimental.pallas import tpu as pltpu
from jax.sharding import PartitionSpec as P

GRID = 14
STRIPE = 7
MINOR = 16
TOK = GRID * MINOR
WIN = STRIPE * MINOR
HALF_HEADS = 4
HEAD = 32
D = 256
FF = 1024
CB = 2

norm_eps = 1e-05
masked_score = -1e30
root_half = 0.7071067811865476
inverse_root_tau = 0.3989422804014327
log2_e = 1.4426950408889634
factor = HEAD**-0.5

f32 = jnp.float32
bf16 = jnp.bfloat16

ATTN_ROWS = 288
FF_ROWS = 512
GRAD_ATTN_ROWS = 320
GAIN, SHIFT, ENTRY, TAPS, BRANCH, HIDDEN = 0, 2, 4, 6, 16, 18


def dot(a, b):
    return lax.dot_general(a, b, (((1,), (0,)), ((), ())), preferred_element_type=f32)


def dot_nt(a, b):
    return lax.dot_general(a, b, (((1,), (1,)), ((), ())), preferred_element_type=f32)


def dot_tn(a, b):
    return lax.dot_general(a, b, (((0,), (0,)), ((), ())), preferred_element_type=f32)


def norm(x):
    center = x - jnp.mean(x, axis=-1, keepdims=True)
    spread = jnp.mean(center * center, axis=-1, keepdims=True)
    inverse = lax.rsqrt(spread + norm_eps)
    return center * inverse, inverse


def norm_back(grad, normal, inverse, gain):
    scaled = grad * gain
    return inverse * (
        scaled
        - jnp.mean(scaled, axis=-1, keepdims=True)
        - normal * jnp.mean(scaled * normal, axis=-1, keepdims=True)
    )


def column_sum(x):
    return jnp.sum(x, axis=0, keepdims=True)


def grid_transpose():
    row = lax.broadcasted_iota(jnp.int32, (TOK, TOK), 0)
    col = lax.broadcasted_iota(jnp.int32, (TOK, TOK), 1)
    hit = (row // MINOR == col % MINOR) & (row % MINOR == col // MINOR)
    return hit.astype(f32).astype(bf16)


def minor_inside(rows, lanes):
    cell = lax.broadcasted_iota(jnp.int32, (rows, lanes), 0) % MINOR
    return cell < GRID


def key_bias(major_end, minor_end, window):
    row = lax.broadcasted_iota(jnp.int32, (WIN, 128), 0)
    major = row // MINOR + window * STRIPE
    minor = row % MINOR
    return jnp.where((major < major_end) & (minor < minor_end), 0.0, masked_score)


def heads_apart(x):
    lane = lax.broadcasted_iota(jnp.int32, (WIN, 128), 1) // HEAD
    wide = x.astype(f32)
    rest = jnp.zeros((128 - WIN, 128), bf16)
    blocks = []
    for head in range(HALF_HEADS):
        blocks.append(jnp.where(lane == head, wide, 0.0).astype(bf16))
        blocks.append(rest)
    return jnp.concatenate(blocks, axis=0)


def by_head(flat, probs):
    turned = flat.astype(f32).T.astype(bf16)
    parts = []
    for head in range(HALF_HEADS):
        parts.append(
            dot(turned[head * HEAD : (head + 1) * HEAD], probs[:, head * 128 : (head + 1) * 128])
        )
    return jnp.concatenate(parts, axis=0).T[:WIN]


def attend(query, key, value, bias):
    scores = dot_nt(key, heads_apart(query)) * (factor * log2_e)
    scores = scores + jnp.concatenate([bias] * HALF_HEADS, axis=1)
    raised = jnp.exp2(scores - jnp.max(scores, axis=0, keepdims=True))
    probs = (raised * (1.0 / jnp.sum(raised, axis=0, keepdims=True))).astype(bf16)
    return by_head(value, probs), probs


def attend_back(grad, query, key, value, probs):
    grad_apart = heads_apart(grad)
    grad_probs = dot_nt(value, grad_apart)
    wide = probs.astype(f32)
    inner = jnp.sum(grad_probs * wide, axis=0, keepdims=True)
    grad_scores = (wide * (grad_probs - inner)).astype(bf16)
    grad_value = dot(probs, grad_apart)
    grad_key = dot(grad_scores, heads_apart(query)) * factor
    grad_query = by_head(key, grad_scores) * factor
    return grad_query, grad_key, grad_value


def tap_of(taps, orient, major_step, minor_step):
    if orient == 0:
        return taps[3 * (major_step + 1) + minor_step + 1]
    return taps[3 * (minor_step + 1) + major_step + 1]


def tap_index(orient, major_step, minor_step):
    if orient == 0:
        return 3 * (major_step + 1) + minor_step + 1
    return 3 * (minor_step + 1) + major_step + 1


def minor_shifts(x):
    rows = x.shape[0]
    return {-1: pltpu.roll(x, 1, 0), 0: x, 1: pltpu.roll(x, rows - 1, 0)}


def major_shift(x, step):
    if step == 0:
        return x
    zeros = jnp.zeros((MINOR, x.shape[1]), x.dtype)
    if step == 1:
        return jnp.concatenate([x[MINOR:], zeros], axis=0)
    return jnp.concatenate([zeros, x[:-MINOR]], axis=0)


def stencil(value_shifts, taps, orient):
    out = None
    for major_step in (-1, 0, 1):
        line = None
        for minor_step in (-1, 0, 1):
            term = value_shifts[minor_step] * tap_of(taps, orient, major_step, minor_step)
            line = term if line is None else line + term
        line = major_shift(line, major_step)
        out = line if out is None else out + line
    return out + taps[9]


def stencil_back(grad_shifts, taps, orient):
    out = None
    for major_step in (-1, 0, 1):
        line = None
        for minor_step in (-1, 0, 1):
            term = grad_shifts[-minor_step] * tap_of(taps, orient, major_step, minor_step)
            line = term if line is None else line + term
        line = major_shift(line, -major_step)
        out = line if out is None else out + line
    return out


def stencil_tap_grads(grad, value_shifts, orient):
    sums = [None] * 9
    for major_step in (-1, 0, 1):
        for minor_step in (-1, 0, 1):
            shifted = value_shifts[minor_step]
            if major_step == 1:
                product = grad[:-MINOR] * shifted[MINOR:]
            elif major_step == -1:
                product = grad[MINOR:] * shifted[:-MINOR]
            else:
                product = grad * shifted
            sums[tap_index(orient, major_step, minor_step)] = column_sum(product)
    sums.append(column_sum(grad))
    return jnp.concatenate(sums, axis=0)


def assemble_attn(me, core, own, near, far, wqkv, wm, sm):
    half = ATTN_ROWS // 2
    for k in range(4):
        shard = lax.rem(me + 4 - k, 4)
        orient, part = lax.div(shard, 2), lax.rem(shard, 2)
        if k == 0:
            unit = own[...]
        else:
            first = jnp.where(core == 0, near[k - 1][...], far[k - 1][...])
            second = jnp.where(core == 0, far[k - 1][...], near[k - 1][...])
            unit = jnp.concatenate([first, second], axis=0)
        for p in range(3):
            at = pl.multiple_of(orient * 384 + p * 128 + part * 64, 64)
            wqkv[pl.ds(at, 64), :] = unit[p * 64 : (p + 1) * 64]
        wm[pl.ds(pl.multiple_of(shard * 64, 64), 64), :] = unit[192:256]
        vectors = unit[256:288].astype(f32)
        if k == 0:
            sm[...] = vectors
        else:
            sm[...] += vectors


def assemble_ff(me, core, own, near, far, we, wr):
    for k in range(4):
        shard = lax.rem(me + 4 - k, 4)
        if k == 0:
            first, second = own[:256], own[256:]
        else:
            first = jnp.where(core == 0, near[k - 1][...], far[k - 1][...])
            second = jnp.where(core == 0, far[k - 1][...], near[k - 1][...])
        we[shard] = first
        at = pl.multiple_of(shard * 64, 64)
        for c in range(4):
            wr[pl.ds(at, 64), c * 256 : (c + 1) * 256] = second[c * 64 : (c + 1) * 64]


def attn_forward(x, hw, crop0, turn, wqkv, wm, sm, a_ref, qkv_ref, probs_ref, mixed_ref):
    normal, _ = norm(x)
    a = (normal * sm[GAIN : GAIN + 1] + sm[SHIFT : SHIFT + 1]).astype(bf16)
    a_ref[...] = a
    entry = sm[ENTRY : ENTRY + 2]
    taps_all = sm[TAPS : TAPS + 10]
    inside = minor_inside(TOK, 128)
    for i in range(CB):
        rows = slice(i * TOK, (i + 1) * TOK)
        height, width = hw[2 * (crop0 + i)], hw[2 * (crop0 + i) + 1]
        a_here = a[rows]
        mixed_halves = []
        for orient in range(2):
            lanes = slice(orient * 128, (orient + 1) * 128)
            source = a_here if orient == 0 else dot(turn, a_here).astype(bf16)
            packed = dot_nt(source, wqkv[orient * 384 : (orient + 1) * 384])
            query = (packed[:, :128] + entry[0:1, lanes]).astype(bf16)
            key = packed[:, 128:256].astype(bf16)
            value = jnp.where(inside, packed[:, 256:] + entry[1:2, lanes], 0.0).astype(bf16)
            base = orient * 384
            qkv_ref[rows, base : base + 128] = query
            qkv_ref[rows, base + 128 : base + 256] = key
            qkv_ref[rows, base + 256 : base + 384] = value
            shifts = minor_shifts(value.astype(f32))
            taps = [taps_all[t : t + 1, lanes] for t in range(10)]
            major_end, minor_end = (height, width) if orient == 0 else (width, height)
            outs = []
            for window in range(2):
                win = slice(window * WIN, (window + 1) * WIN)
                bias = key_bias(major_end, minor_end, window)
                out, probs = attend(query[win], key[win], value[win], bias)
                probs_ref[i, 2 * orient + window] = probs
                out = out + stencil({s: v[win] for s, v in shifts.items()}, taps, orient)
                outs.append(out.astype(bf16))
            half = jnp.concatenate(outs, axis=0)
            if orient == 1:
                half = dot(turn, half).astype(bf16)
            mixed_halves.append(half)
        mixed_ref[rows, :] = jnp.concatenate(mixed_halves, axis=1)
    return x + (dot_nt(mixed_ref[...], wm[...]) + sm[BRANCH : BRANCH + 1])


def ff_forward(middle, we, wr, sm, a2_ref, g_ref, slope_ref):
    normal, _ = norm(middle)
    a2 = (normal * sm[GAIN + 1 : GAIN + 2] + sm[SHIFT + 1 : SHIFT + 2]).astype(bf16)
    a2_ref[...] = a2
    for s in range(4):
        u = dot(a2, we[s]) + sm[HIDDEN + s : HIDDEN + s + 1]
        phi = 0.5 + 0.5 * lax.erf(u * root_half)
        g_ref[:, s * 256 : (s + 1) * 256] = (u * phi).astype(bf16)
        slope_ref[:, s * 256 : (s + 1) * 256] = (
            phi + u * jnp.exp(-0.5 * u * u) * inverse_root_tau
        ).astype(bf16)
    return middle + (dot_nt(g_ref[...], wr[...]) + sm[BRANCH + 1 : BRANCH + 2])


def ff_backward(grad, middle, a2_ref, g_ref, slope_ref, we, wr, sm, acc_e, acc_r, vec):
    ey = grad.astype(bf16)
    vec[BRANCH + 1 : BRANCH + 2] += column_sum(grad)
    a2 = a2_ref[...]
    back = None
    for s in range(4):
        cols = slice(s * 256, (s + 1) * 256)
        acc_r[s] += dot_tn(ey, g_ref[:, cols])
        eu_wide = dot(ey, wr[:, cols]) * slope_ref[:, cols].astype(f32)
        vec[HIDDEN + s : HIDDEN + s + 1] += column_sum(eu_wide)
        eu = eu_wide.astype(bf16)
        acc_e[s] += dot_tn(a2, eu)
        term = dot_nt(eu, we[s])
        back = term if back is None else back + term
    normal, inverse = norm(middle)
    vec[GAIN + 1 : GAIN + 2] += column_sum(back * normal)
    vec[SHIFT + 1 : SHIFT + 2] += column_sum(back)
    return grad + norm_back(back, normal, inverse, sm[GAIN + 1 : GAIN + 2])


def attn_backward(grad, x, turn, a_ref, qkv_ref, probs_ref, mixed_ref, wqkv, wm, sm, e_ref, acc_q, acc_m, vec):
    eo = grad.astype(bf16)
    vec[BRANCH : BRANCH + 1] += column_sum(grad)
    acc_m[...] += dot_tn(eo, mixed_ref[...])
    em_all = dot(eo, wm[...]).astype(bf16)
    taps_all = sm[TAPS : TAPS + 10]
    inside = minor_inside(TOK, 128)
    for i in range(CB):
        rows = slice(i * TOK, (i + 1) * TOK)
        for orient in range(2):
            lanes = slice(orient * 128, (orient + 1) * 128)
            em = em_all[rows, lanes]
            if orient == 1:
                em = dot(turn, em).astype(bf16)
            base = orient * 384
            query = qkv_ref[rows, base : base + 128]
            key = qkv_ref[rows, base + 128 : base + 256]
            value = qkv_ref[rows, base + 256 : base + 384]
            taps = [taps_all[t : t + 1, lanes] for t in range(10)]
            em_wide = em.astype(f32)
            grad_shifts = minor_shifts(em_wide)
            value_shifts = minor_shifts(value.astype(f32))
            tap_grads = None
            got = [[], [], []]
            for window in range(2):
                win = slice(window * WIN, (window + 1) * WIN)
                dq, dk, dv = attend_back(em[win], query[win], key[win], value[win], probs_ref[i, 2 * orient + window])
                dv = dv + stencil_back({s: v[win] for s, v in grad_shifts.items()}, taps, orient)
                here = stencil_tap_grads(em_wide[win], {s: v[win] for s, v in value_shifts.items()}, orient)
                tap_grads = here if tap_grads is None else tap_grads + here
                got[0].append(dq)
                got[1].append(dk)
                got[2].append(dv)
            vec[TAPS : TAPS + 10, lanes] += tap_grads
            eq = jnp.concatenate(got[0], axis=0)
            ek = jnp.concatenate(got[1], axis=0)
            ev = jnp.where(inside, jnp.concatenate(got[2], axis=0), 0.0)
            vec[ENTRY : ENTRY + 1, lanes] += column_sum(eq)
            vec[ENTRY + 1 : ENTRY + 2, lanes] += column_sum(ev)
            e = jnp.concatenate([eq, ek, ev], axis=1).astype(bf16)
            if orient == 1:
                e = dot(turn, e).astype(bf16)
            e_ref[rows, base : base + 384] = e
    e = e_ref[...]
    acc_q[...] += dot_tn(e, a_ref[...])
    back = dot(e, wqkv[...])
    normal, inverse = norm(x)
    vec[GAIN : GAIN + 1] += column_sum(back * normal)
    vec[SHIFT : SHIFT + 1] += column_sum(back)
    return grad + norm_back(back, normal, inverse, sm[GAIN : GAIN + 1])


def write_ff_grads(out, acc_e, acc_r):
    for s in range(4):
        out[s, 0:256] = acc_e[s].astype(out.dtype)
        for c in range(4):
            out[s, 256 + 64 * c : 320 + 64 * c] = acc_r[c, 64 * s : 64 * (s + 1)].astype(out.dtype)


def write_attn_grads(out, acc_q, acc_m, vec):
    for s in range(4):
        for p in range(3):
            at = (s // 2) * 384 + p * 128 + (s % 2) * 64
            out[s, p * 64 : (p + 1) * 64] = acc_q[at : at + 64].astype(out.dtype)
        out[s, 192:256] = acc_m[64 * s : 64 * (s + 1)].astype(out.dtype)
        out[s, 256:288] = vec[...].astype(out.dtype)
        out[s, 288:320] = jnp.zeros((32, D), out.dtype)


def load_cells(ref, spread):
    spread[:, GRID:MINOR, :] = jnp.zeros((CB * GRID, MINOR - GRID, D), f32)
    spread[:, 0:GRID, :] = ref[...].reshape(CB * GRID, GRID, D).astype(f32)
    return spread[...].reshape(CB * TOK, D)


def store_cells(ref, x):
    cells = x.astype(ref.dtype).reshape(CB * GRID, MINOR, D)[:, 0:GRID, :]
    ref[...] = cells.reshape(CB, GRID, GRID, D)


def first_step(fn):
    pl.when(pl.program_id(0) == 0)(fn)


def last_step(fn):
    pl.when(pl.program_id(0) == pl.num_programs(0) - 1)(fn)


def attn_fwd_kernel(place, x, *refs):
    own, near, far = refs[0], refs[1:4], refs[4:7]
    mid, a, qkv, probs, mixed, wqkv, wm, sm, spread, turn = refs[7:]

    @first_step
    def _():
        assemble_attn(place[0], place[1], own, near, far, wqkv, wm, sm)
        turn[...] = grid_transpose()

    state = load_cells(x, spread)
    mid[...] = attn_forward(state, place, pl.program_id(0) * CB + 1, turn[...], wqkv, wm, sm, a, qkv, probs, mixed)


def ff_fwd_kernel(place, middle, sm, *refs):
    own, near, far = refs[0], refs[1:4], refs[4:7]
    out, a2, g, slope, we, wr = refs[7:]

    @first_step
    def _():
        assemble_ff(place[0], place[1], own, near, far, we, wr)

    out[...] = ff_forward(middle[...], we, wr, sm, a2, g, slope)


def top_kernel(place, x, cotangent, *refs):
    attn_in, ff_in = refs[0:7], refs[7:14]
    (output, grad_out, grads_a, grads_f) = refs[14:18]
    (wqkv, wm, sm, we, wr, turn, spread, middle, a, qkv, probs, mixed, a2, g, slope, e,
     acc_e, acc_r, acc_q, acc_m, vec) = refs[18:]

    @first_step
    def _():
        assemble_attn(place[0], place[1], attn_in[0], attn_in[1:4], attn_in[4:7], wqkv, wm, sm)
        assemble_ff(place[0], place[1], ff_in[0], ff_in[1:4], ff_in[4:7], we, wr)
        turn[...] = grid_transpose()
        for ref in (acc_e, acc_r, acc_q, acc_m, vec):
            ref[...] = jnp.zeros_like(ref)

    flip = turn[...]
    middle[...] = attn_forward(x[...], place, pl.program_id(0) * CB + 1, flip, wqkv, wm, sm, a, qkv, probs, mixed)
    store_cells(output, ff_forward(middle[...], we, wr, sm, a2, g, slope))
    grad = load_cells(cotangent, spread)
    grad_mid = ff_backward(grad, middle[...], a2, g, slope, we, wr, sm, acc_e, acc_r, vec)
    grad_out[...] = attn_backward(grad_mid, x[...], flip, a, qkv, probs, mixed, wqkv, wm, sm, e, acc_q, acc_m, vec)

    @last_step
    def _():
        write_ff_grads(grads_f, acc_e, acc_r)
        write_attn_grads(grads_a, acc_q, acc_m, vec)


def ff_bwd_kernel(grad, middle, a2, g, slope, we, wr, sm, grad_mid, grads_f, vec, acc_e, acc_r):
    @first_step
    def _():
        for ref in (acc_e, acc_r, vec):
            ref[...] = jnp.zeros_like(ref)

    grad_mid[...] = ff_backward(grad[...], middle[...], a2, g, slope, we, wr, sm, acc_e, acc_r, vec)

    @last_step
    def _():
        write_ff_grads(grads_f, acc_e, acc_r)


def attn_bwd_kernel(grad, x, a, qkv, probs, mixed, wqkv, wm, sm, vec_in, patch_grad, grads_a, spread, turn, e, acc_q, acc_m, vec):
    @first_step
    def _():
        for ref in (acc_q, acc_m):
            ref[...] = jnp.zeros_like(ref)
        vec[...] = vec_in[...]
        turn[...] = grid_transpose()

    state = load_cells(x, spread)
    store_cells(
        patch_grad,
        attn_backward(grad[...], state, turn[...], a, qkv, probs, mixed, wqkv, wm, sm, e, acc_q, acc_m, vec),
    )

    @last_step
    def _():
        write_attn_grads(grads_a, acc_q, acc_m, vec)


def whole(shape):
    return pl.BlockSpec(shape, lambda i, *_: (0,) * len(shape))


def rows_of(lanes):
    return pl.BlockSpec((CB * TOK, lanes), lambda i, *_: (i, 0))


def cells():
    return pl.BlockSpec((CB, GRID, GRID, D), lambda i, *_: (i, 0, 0, 0))


def probs_spec():
    return pl.BlockSpec((CB, 4, WIN, 512), lambda i, *_: (i, 0, 0, 0))


def unit_specs(rows):
    return [whole((rows, D))] + [whole((rows // 2, D))] * 6


def shape(dims, dtype=bf16):
    return jax.ShapeDtypeStruct(dims, dtype)


params = dict(
    compiler_params=pltpu.CompilerParams(
        vmem_limit_bytes=56 * 1024 * 1024, dimension_semantics=("arbitrary",)
    )
)


def attn_fwd_call(place, patches, unit):
    crops = patches.shape[0]
    n = crops * TOK
    return pl.pallas_call(
        attn_fwd_kernel,
        grid_spec=pltpu.PrefetchScalarGridSpec(
            num_scalar_prefetch=1,
            grid=(crops // CB,),
            in_specs=[cells()] + unit_specs(ATTN_ROWS),
            out_specs=[rows_of(D), rows_of(D), rows_of(768), probs_spec(), rows_of(D), whole((768, D)), whole((D, D)), whole((32, D))],
            scratch_shapes=[pltpu.VMEM((CB * GRID, MINOR, D), f32), pltpu.VMEM((TOK, TOK), bf16)],
        ),
        out_shape=[shape((n, D), f32), shape((n, D)), shape((n, 768)), shape((crops, 4, WIN, 512)), shape((n, D)), shape((768, D)), shape((D, D)), shape((32, D), f32)],
        name="attn_fwd",
        **params,
    )(place, patches, *unit)


def ff_fwd_call(place, middle, sm, unit):
    n = middle.shape[0]
    return pl.pallas_call(
        ff_fwd_kernel,
        grid_spec=pltpu.PrefetchScalarGridSpec(
            num_scalar_prefetch=1,
            grid=(n // (CB * TOK),),
            in_specs=[rows_of(D), whole((32, D))] + unit_specs(FF_ROWS),
            out_specs=[rows_of(D), rows_of(D), rows_of(FF), rows_of(FF), whole((4, D, D)), whole((D, FF))],
        ),
        out_shape=[shape((n, D), f32), shape((n, D)), shape((n, FF)), shape((n, FF)), shape((4, D, D)), shape((D, FF))],
        name="ff_fwd",
        **params,
    )(place, middle, sm, *unit)


def top_call(place, x, cotangent, attn_unit, ff_unit):
    n = x.shape[0]
    crops = n // TOK
    r = CB * TOK
    v = pltpu.VMEM
    return pl.pallas_call(
        top_kernel,
        grid_spec=pltpu.PrefetchScalarGridSpec(
            num_scalar_prefetch=1,
            grid=(crops // CB,),
            in_specs=[rows_of(D), cells()] + unit_specs(ATTN_ROWS) + unit_specs(FF_ROWS),
            out_specs=[cells(), rows_of(D), whole((4, GRAD_ATTN_ROWS, D)), whole((4, FF_ROWS, D))],
            scratch_shapes=[
                v((768, D), bf16), v((D, D), bf16), v((32, D), f32), v((4, D, D), bf16), v((D, FF), bf16),
                v((TOK, TOK), bf16), v((CB * GRID, MINOR, D), f32), v((r, D), f32), v((r, D), bf16), v((r, 768), bf16),
                v((CB, 4, WIN, 512), bf16), v((r, D), bf16), v((r, D), bf16), v((r, FF), bf16), v((r, FF), bf16), v((r, 768), bf16),
                v((4, D, D), f32), v((4, D, D), f32), v((768, D), f32), v((D, D), f32), v((32, D), f32),
            ],
        ),
        out_shape=[shape((crops, GRID, GRID, D)), shape((n, D), f32), shape((4, GRAD_ATTN_ROWS, D)), shape((4, FF_ROWS, D))],
        name="top_block",
        **params,
    )(place, x, cotangent, *attn_unit, *ff_unit)


def ff_bwd_call(grad, middle, a2, g, slope, we, wr, sm):
    n = grad.shape[0]
    return pl.pallas_call(
        ff_bwd_kernel,
        grid=(n // (CB * TOK),),
        in_specs=[rows_of(D), rows_of(D), rows_of(D), rows_of(FF), rows_of(FF), whole((4, D, D)), whole((D, FF)), whole((32, D))],
        out_specs=[rows_of(D), whole((4, FF_ROWS, D)), whole((32, D))],
        scratch_shapes=[pltpu.VMEM((4, D, D), f32), pltpu.VMEM((4, D, D), f32)],
        out_shape=[shape((n, D), f32), shape((4, FF_ROWS, D)), shape((32, D), f32)],
        name="ff_bwd",
        **params,
    )(grad, middle, a2, g, slope, we, wr, sm)


def attn_bwd_call(grad, patches, a, qkv, probs, mixed, wqkv, wm, sm, vec):
    crops = patches.shape[0]
    v = pltpu.VMEM
    return pl.pallas_call(
        attn_bwd_kernel,
        grid=(crops // CB,),
        in_specs=[rows_of(D), cells(), rows_of(D), rows_of(768), probs_spec(), rows_of(D), whole((768, D)), whole((D, D)), whole((32, D)), whole((32, D))],
        out_specs=[cells(), whole((4, GRAD_ATTN_ROWS, D))],
        scratch_shapes=[v((CB * GRID, MINOR, D), f32), v((TOK, TOK), bf16), v((CB * TOK, 768), bf16), v((768, D), f32), v((D, D), f32), v((32, D), f32)],
        out_shape=[shape(patches.shape), shape((4, GRAD_ATTN_ROWS, D))],
        name="attn_bwd",
        **params,
    )(grad, patches, a, qkv, probs, mixed, wqkv, wm, sm, vec)


def compute(place, patches, cotangent, attn_units, ff_units):
    mid, a, qkv, probs, mixed, wqkv, wm, sm = attn_fwd_call(place, patches, attn_units[0])
    state, a2, g, slope, we, wr = ff_fwd_call(place, mid, sm, ff_units[0])
    output, grad, grads_a1, grads_f1 = top_call(place, state, cotangent, attn_units[1], ff_units[1])
    grad_mid, grads_f0, vec = ff_bwd_call(grad, mid, a2, g, slope, we, wr, sm)
    patch_grad, grads_a0 = attn_bwd_call(grad_mid, patches, a, qkv, probs, mixed, wqkv, wm, sm, vec)
    return output, patch_grad, grads_a0, grads_f0, grads_a1, grads_f1


def pack_units(norm_gain, norm_shift, qkv_weight, entry_bias, stencil_taps, mixer_weight, branch_bias, expand_weight, hidden_bias, reduce_weight):
    layers = qkv_weight.shape[0]
    me = lax.axis_index("mp")
    qkv = jnp.transpose(qkv_weight, (0, 2, 3, 1)).reshape(layers, 192, D)
    mixer = jnp.transpose(mixer_weight, (0, 2, 1))
    vectors = jnp.concatenate([norm_gain, norm_shift, entry_bias, stencil_taps, branch_bias], axis=1)
    lane_shard = lax.broadcasted_iota(jnp.int32, (1, 1, D), 2) // 64
    vectors = jnp.where(lane_shard == me, jnp.tile(vectors, (1, 1, 4)), jnp.zeros((), bf16))
    row = lax.broadcasted_iota(jnp.int32, (1, 14, 1), 1)
    hidden = jnp.where(row == me, hidden_bias[:, None, :], jnp.zeros((), bf16))
    attn = jnp.concatenate([qkv, mixer, vectors, hidden], axis=1)
    reduce = jnp.transpose(reduce_weight, (0, 2, 1)).reshape(layers, 64, 4, D)
    reduce = jnp.transpose(reduce, (0, 2, 1, 3)).reshape(layers, D, D)
    ff = jnp.concatenate([expand_weight, reduce], axis=1)
    return [attn[i] for i in range(layers)], [ff[i] for i in range(layers)]


def turn_mp(x, k):
    n = lax.axis_size("mp")
    return lax.ppermute(x, "mp", [(i, (i + k) % n) for i in range(n)])


def swap_dp(x, bit):
    n = lax.axis_size("dp")
    return lax.ppermute(x, "dp", [(i, i ^ bit) for i in range(n)])


def gather_unit(unit, core):
    half = unit.shape[0] // 2
    mine = lax.dynamic_slice_in_dim(unit, core * half, half, 0)
    near = [turn_mp(mine, k) for k in (1, 2, 3)]
    far = [swap_dp(x, 1) for x in near]
    return [unit] + near + far


def sum_grads(grads, dtype=bf16):
    dp, me_dp, me = lax.axis_size("dp"), lax.axis_index("dp"), lax.axis_index("mp")
    rows = grads.shape[1]
    held = grads.reshape(4, dp, rows // dp, D)
    bit = 1
    held = grads.reshape(4, dp, rows // dp, D)
    while bit < dp:
        pairs = held.reshape(4, held.shape[1] // 2, 2, rows // dp, D)
        mine_at = (me_dp // bit) % 2
        keep = lax.dynamic_index_in_dim(pairs, mine_at, 2, keepdims=False)
        give = lax.dynamic_index_in_dim(pairs, 1 - mine_at, 2, keepdims=False)
        held = (keep.astype(f32) + swap_dp(give, bit).astype(f32)).astype(dtype)
        bit *= 2
    piece = held[:, 0]
    total = lax.dynamic_index_in_dim(piece, me, 0, keepdims=False).astype(f32)
    for k in (1, 2, 3):
        give = lax.dynamic_index_in_dim(piece, (me + k) % 4, 0, keepdims=False)
        total = total + turn_mp(give, k).astype(f32)
    return lax.all_gather(total, "dp", axis=0, tiled=True)


def piece_order(dp):
    return list(range(dp))


def unpack(attn, ff, me):
    layers = attn.shape[0]
    packed = jnp.transpose(attn[:, :192].reshape(layers, 3, 64, D), (0, 3, 1, 2))
    mixer = jnp.transpose(attn[:, 192:256], (0, 2, 1))
    vec = lax.dynamic_slice_in_dim(attn[:, 256:274], me * 64, 64, 2)
    hidden = lax.dynamic_index_in_dim(attn[:, 256 + HIDDEN : 256 + HIDDEN + 4], me, 1, keepdims=False)
    expand = ff[:, :256]
    reduce = jnp.transpose(ff[:, 256:].reshape(layers, 4, 64, D), (0, 1, 3, 2)).reshape(layers, FF, 64)
    return (
        vec[:, GAIN : GAIN + 2], vec[:, SHIFT : SHIFT + 2], packed, vec[:, ENTRY : ENTRY + 2], vec[:, TAPS : TAPS + 10],
        mixer, vec[:, BRANCH : BRANCH + 2], expand, hidden, reduce,
    )


def body(patches, validity, *rest):
    weights, cotangent = rest[:-1], rest[-1]
    me, core = lax.axis_index("mp"), lax.axis_index("dp") % 2
    heights = jnp.sum(validity[:, :, 0], axis=1)
    widths = jnp.sum(validity[:, 0, :], axis=1)
    place = jnp.concatenate([jnp.stack([me, core]), jnp.stack([heights, widths], axis=1).reshape(-1)]).astype(jnp.int32)
    attn, ff = pack_units(*weights)
    attn_units = [gather_unit(x, core) for x in attn]
    ff_units = [gather_unit(x, core) for x in ff]
    output, patch_grad, grads_a0, grads_f0, grads_a1, grads_f1 = compute(place, patches, cotangent, attn_units, ff_units)
    attn_sums = jnp.stack([sum_grads(grads_a0), sum_grads(grads_a1)])
    ff_sums = jnp.stack([sum_grads(grads_f0), sum_grads(grads_f1)])
    return (output, patch_grad) + unpack(attn_sums, ff_sums, me)


def solution(mesh):
    crops = P(("dp", "mp"), None, None, None)
    lanes = P(None, None, "mp")
    deep = P(None, None, None, "mp")
    return jax.shard_map(
        body,
        mesh=mesh,
        in_specs=(crops, P(("dp", "mp"), None, None), lanes, lanes, deep, lanes, lanes, lanes, lanes, lanes, P(None, "mp"), lanes, crops),
        out_specs=(crops, crops, lanes, lanes, deep, lanes, lanes, lanes, lanes, lanes, P(None, "mp"), lanes),
        check_vma=False,
    )
```

```python
import functools

import jax
import jax.numpy as jnp
from jax import lax
from jax.experimental import pallas as pl
from jax.experimental.pallas import tpu as pltpu
from jax.sharding import PartitionSpec as P

GRID = 14
STRIPE = 7
CELLS = GRID * GRID
CROPS = 8
ROWS = CELLS * CROPS
LINE = GRID * CROPS
HELD = ROWS + 112
WIN = 112
HALF_HEADS = 4
HEAD = 32
D = 256
FF = 1024
STEP_CROPS = 4
CHUNK = 784

norm_eps = 1e-05
masked_score = -1e30
root_half = 0.7071067811865476
inverse_root_tau = 0.3989422804014327
log2_e = 1.4426950408889634
factor = HEAD**-0.5

f32 = jnp.float32
bf16 = jnp.bfloat16

ATTN_ROWS = 288
FF_ROWS = 512
TOP_ROWS = 832
LOW_ROWS = 288
GAIN, SHIFT, ENTRY, TAPS, BRANCH, HIDDEN = 0, 2, 4, 6, 16, 18


def dot(a, b):
    return lax.dot_general(a, b, (((1,), (0,)), ((), ())), preferred_element_type=f32)


def dot_nt(a, b):
    return lax.dot_general(a, b, (((1,), (1,)), ((), ())), preferred_element_type=f32)


def dot_tn(a, b):
    return lax.dot_general(a, b, (((0,), (0,)), ((), ())), preferred_element_type=f32)


def norm(x):
    center = x - jnp.mean(x, axis=-1, keepdims=True)
    spread = jnp.mean(center * center, axis=-1, keepdims=True)
    inverse = lax.rsqrt(spread + norm_eps)
    return center * inverse, inverse


def norm_back(grad, normal, inverse, gain):
    scaled = grad * gain
    return inverse * (
        scaled
        - jnp.mean(scaled, axis=-1, keepdims=True)
        - normal * jnp.mean(scaled * normal, axis=-1, keepdims=True)
    )


def column_sum(x):
    return jnp.sum(x.reshape(x.shape[0] // CROPS, CROPS, x.shape[1]), axis=0)


def window_row_inside(orient):
    row = lax.broadcasted_iota(jnp.int32, (WIN, 128), 0)
    return row < 98 if orient == 0 else row % 8 < STRIPE


def key_bias(orient, window, height, width):
    row = lax.broadcasted_iota(jnp.int32, (WIN, 128), 0)
    if orient == 0:
        line, column = row // GRID + window * STRIPE, row % GRID
    else:
        line, column = row // 8, row % 8 + window * STRIPE
    valid = window_row_inside(orient) & (line < height) & (column < width)
    return jnp.where(valid, 0.0, masked_score)


def load_window(ref, block, crop, orient, window):
    if orient == 0:
        return ref[block, pl.ds(98 * CROPS * window + crop, WIN, stride=CROPS), :]
    parts = [
        ref[block, pl.ds((line * GRID + window * STRIPE) * CROPS + crop, 8, stride=CROPS), :]
        for line in range(GRID)
    ]
    return jnp.concatenate(parts, axis=0)


def store_window(ref, block, crop, orient, window, x):
    if orient == 0:
        ref[block, pl.ds(98 * CROPS * window + crop, 98, stride=CROPS), :] = x[:98]
        return
    for line in range(GRID):
        at = (line * GRID + window * STRIPE) * CROPS + crop
        ref[block, pl.ds(at, STRIPE, stride=CROPS), :] = x[line * 8 : line * 8 + STRIPE]


def heads_apart(x, inside=None):
    lane = lax.broadcasted_iota(jnp.int32, (WIN, 128), 1) // HEAD
    rest = jnp.zeros((128 - WIN, 128), bf16)
    blocks = []
    for head in range(HALF_HEADS):
        keep = lane == head
        if inside is not None:
            keep = keep & inside
        blocks.append(jnp.where(keep, x, 0.0).astype(bf16))
        blocks.append(rest)
    return jnp.concatenate(blocks, axis=0)


def by_head(flat_turned, probs):
    parts = []
    for head in range(HALF_HEADS):
        parts.append(
            dot(flat_turned[head * HEAD : (head + 1) * HEAD], probs[:, head * 128 : (head + 1) * 128])
        )
    return jnp.concatenate(parts, axis=0)


def attend(queries, keys, values, biases):
    apart = [heads_apart(x) for x in queries]
    value_turned = [x.T.astype(bf16) for x in values]
    scores = [dot_nt(k.astype(bf16), q) for k, q in zip(keys, apart)]
    scores = [s * (factor * log2_e) + jnp.concatenate([b] * HALF_HEADS, axis=1) for s, b in zip(scores, biases)]
    peaks = [jnp.max(s, axis=0, keepdims=True) for s in scores]
    raised = [jnp.exp2(s - p) for s, p in zip(scores, peaks)]
    shares = [1.0 / jnp.sum(r, axis=0, keepdims=True) for r in raised]
    probs = [(r * s).astype(bf16) for r, s in zip(raised, shares)]
    outs = [by_head(v, p) for v, p in zip(value_turned, probs)]
    return [o.T[:WIN] for o in outs], probs


def attend_back(grads, queries, keys, values, probs, insides):
    grad_apart = [heads_apart(x, i) for x, i in zip(grads, insides)]
    grad_probs = [dot_nt(v, g) for v, g in zip(values, grad_apart)]
    key_turned = [x.astype(f32).T.astype(bf16) for x in keys]
    grad_value = [dot(p, g) for p, g in zip(probs, grad_apart)]
    wide = [p.astype(f32) for p in probs]
    inner = [jnp.sum(g * w, axis=0, keepdims=True) for g, w in zip(grad_probs, wide)]
    grad_scores = [(w * (g - i)).astype(bf16) for w, g, i in zip(wide, grad_probs, inner)]
    apart = [heads_apart(x) for x in queries]
    grad_key = [dot(s, q) * factor for s, q in zip(grad_scores, apart)]
    grad_query = [by_head(k, s) for k, s in zip(key_turned, grad_scores)]
    grad_query = [g.T[:WIN] * factor for g in grad_query]
    return grad_query, grad_key, grad_value


WINDOWS = [(orient, window) for orient in range(2) for window in range(2)]


def steps_along(x, orient):
    zero = jnp.zeros((CROPS, x.shape[1]), x.dtype)
    if orient == 0:
        return {-1: jnp.concatenate([zero, x[:-CROPS]], axis=0), 0: x, 1: jnp.concatenate([x[CROPS:], zero], axis=0)}
    half = LINE // 2
    left, right = x[:half], x[half:]
    return {
        -1: jnp.concatenate([zero, left[:-CROPS], zero, right[:-CROPS]], axis=0),
        0: x,
        1: jnp.concatenate([left[CROPS:], zero, right[CROPS:], zero], axis=0),
    }


def line_reaches(line, step, orient):
    if step == 0:
        return None
    stops = (GRID, STRIPE) if orient == 0 else (GRID,)
    edges = [(stop - 1) if step == 1 else (stop % GRID) for stop in stops]
    ok = line != edges[0]
    for edge in edges[1:]:
        ok = ok & (line != edge)
    return jnp.where(ok, 1.0, 0.0).astype(f32)


def line_at(ref, block, line):
    held = jnp.clip(line, 0, GRID - 1)
    return ref[block, pl.ds(pl.multiple_of(held * LINE, LINE), LINE), :]


def stencil_line(ref, block, taps, line, orient, back):
    total = None
    for step in (-1, 0, 1):
        moved = steps_along(line_at(ref, block, line + (-step if back else step)).astype(f32), orient)
        reach = line_reaches(line, -step if back else step, orient)
        for side in (-1, 0, 1):
            tap = taps[3 * (step + 1) + side + 1]
            if reach is not None:
                tap = tap * reach
            term = moved[-side if back else side] * tap
            total = term if total is None else total + term
    return total


def stencil_line_taps(ref, block, grad, line, orient):
    sums = []
    for step in (-1, 0, 1):
        moved = steps_along(line_at(ref, block, line + step).astype(f32), orient)
        reach = line_reaches(line, step, orient)
        for side in (-1, 0, 1):
            part = column_sum(grad * moved[side])
            sums.append(part if reach is None else part * reach)
    sums.append(column_sum(grad))
    return sums


def assemble_attn(me, core, own, near, far, wqkv, wm, sm):
    for k in range(4):
        shard = lax.rem(me + 4 - k, 4)
        orient, part = lax.div(shard, 2), lax.rem(shard, 2)
        if k == 0:
            unit = own[...]
        else:
            first = jnp.where(core == 0, near[k - 1][...], far[k - 1][...])
            second = jnp.where(core == 0, far[k - 1][...], near[k - 1][...])
            unit = jnp.concatenate([first, second], axis=0)
        for p in range(3):
            at = pl.multiple_of(orient * 384 + p * 128 + part * 64, 64)
            wqkv[pl.ds(at, 64), :] = unit[p * 64 : (p + 1) * 64]
        wm[pl.ds(pl.multiple_of(shard * 64, 64), 64), :] = unit[192:256]
        vectors = unit[256:288].astype(f32)
        if k == 0:
            sm[...] = vectors
        else:
            sm[...] += vectors


def assemble_ff(me, core, own, near, far, we, wr):
    for k in range(4):
        shard = lax.rem(me + 4 - k, 4)
        if k == 0:
            first, second = own[:256], own[256:]
        else:
            first = jnp.where(core == 0, near[k - 1][...], far[k - 1][...])
            second = jnp.where(core == 0, far[k - 1][...], near[k - 1][...])
        we[shard] = first
        at = pl.multiple_of(shard * 64, 64)
        for c in range(4):
            wr[pl.ds(at, 64), c * 256 : (c + 1) * 256] = second[c * 64 : (c + 1) * 64]


def chunks():
    return [slice(at, at + CHUNK) for at in range(0, ROWS, CHUNK)]


def put_blocks(ref, rows, x):
    for block in range(x.shape[1] // 128):
        ref[block, rows, :] = x[:, block * 128 : (block + 1) * 128]


def project(x, wqkv, sm, qkv):
    zero = jnp.zeros((1, 128), f32)
    query_bias, value_bias = sm[ENTRY : ENTRY + 1], sm[ENTRY + 1 : ENTRY + 2]
    bias = jnp.concatenate(
        [query_bias[:, :128], zero, value_bias[:, :128], query_bias[:, 128:], zero, value_bias[:, 128:]], axis=1
    )
    for rows in chunks():
        normal, _ = norm(x[rows, :].astype(f32))
        a = (normal * sm[GAIN : GAIN + 1] + sm[SHIFT : SHIFT + 1]).astype(bf16)
        put_blocks(qkv, rows, dot_nt(a, wqkv[...]) + bias)
    qkv[:, ROWS:HELD, :] = jnp.zeros((6, HELD - ROWS, 128), f32)


def attend_crops(place, crops, slots, qkv, packed, probs_ref, out):
    at, lists = [], ([], [], [], [])
    for crop, slot in zip(crops, slots):
        height, width = place[2 + 2 * crop], place[3 + 2 * crop]
        for n, (orient, window) in enumerate(WINDOWS):
            three = [load_window(qkv, orient * 3 + p, crop, orient, window) for p in range(3)]
            packed[slot, n] = jnp.concatenate(three, axis=1).astype(bf16)
            entries = (*three, key_bias(orient, window, height, width))
            for held, new in zip(lists, entries):
                held.append(new)
            at.append((crop, slot, n, orient, window))
    outs, probs = attend(*lists)
    for (crop, slot, n, orient, window), o, p in zip(at, outs, probs):
        probs_ref[slot, n] = p
        store_window(out, orient, crop, orient, window, o)


def attend_crops_back(crops, slots, em, packed, probs_ref, e):
    at, lists = [], ([], [], [], [], [], [])
    for crop, slot in zip(crops, slots):
        for n, (orient, window) in enumerate(WINDOWS):
            grad = load_window(em, orient, crop, orient, window)
            entries = (
                grad, packed[slot, n, :, :128], packed[slot, n, :, 128:256], packed[slot, n, :, 256:],
                probs_ref[slot, n], window_row_inside(orient),
            )
            for held, new in zip(lists, entries):
                held.append(new)
            at.append((crop, orient, window))
    for (crop, orient, window), dq, dk, dv in zip(at, *attend_back(*lists)):
        for p, part in enumerate((dq, dk, dv)):
            store_window(e, orient * 3 + p, crop, orient, window, part)


def taps_of(sm, orient):
    lanes = slice(orient * 128, (orient + 1) * 128)
    return [sm[TAPS + t : TAPS + t + 1, lanes] for t in range(10)]


def mix(out, value, value_at, sm, mixed):
    taps = [taps_of(sm, orient) for orient in range(2)]

    def line(i, _):
        rows = pl.ds(pl.multiple_of(i * LINE, LINE), LINE)
        for orient in range(2):
            e_v = stencil_line(value, value_at[orient], taps[orient], i, orient, False) + taps[orient][9]
            mixed[rows, orient * 128 : (orient + 1) * 128] = (out[orient, rows, :] + e_v).astype(bf16)
        return 0

    lax.fori_loop(0, GRID, line, 0)


def mixer(x, mixed, wm, sm, middle):
    for rows in chunks():
        middle[rows, :] = x[rows, :].astype(f32) + (dot_nt(mixed[rows, :], wm[...]) + sm[BRANCH : BRANCH + 1])


def hidden(a2, we, sm, s):
    u = dot(a2, we[s]) + sm[HIDDEN + s : HIDDEN + s + 1]
    phi = 0.5 + 0.5 * lax.erf(u * root_half)
    return u, phi


def slope_of(u, phi):
    return phi + u * jnp.exp(-0.5 * u * u) * inverse_root_tau


def second_norm(middle, sm):
    normal, inverse = norm(middle)
    a2 = (normal * sm[GAIN + 1 : GAIN + 2] + sm[SHIFT + 1 : SHIFT + 2]).astype(bf16)
    return normal, inverse, a2


def ff_forward(middle, we, wr, sm, g_out=None, slope_out=None):
    _, _, a2 = second_norm(middle, sm)
    gs = []
    for s in range(4):
        u, phi = hidden(a2, we, sm, s)
        gs.append((u * phi).astype(bf16))
        if g_out is not None:
            g_out[s], slope_out[s] = gs[-1], slope_of(u, phi).astype(bf16)
    return middle + (dot_nt(jnp.concatenate(gs, axis=1), wr[...]) + sm[BRANCH + 1 : BRANCH + 2])


def ff_backward(grad, middle, we, wr, sm, acc_e, acc_r, vec, held=None):
    ey = grad.astype(bf16)
    vec[BRANCH + 1] += column_sum(grad)
    normal, inverse, a2 = second_norm(middle, sm)
    eus = []
    for s in range(4):
        if held is None:
            u, phi = hidden(a2, we, sm, s)
            g, slope = (u * phi).astype(bf16), slope_of(u, phi)
        else:
            g, slope = held(s)
        acc_r[s] += dot_tn(ey, g)
        eu_wide = dot(ey, wr[:, s * 256 : (s + 1) * 256]) * slope.astype(f32)
        vec[HIDDEN + s] += column_sum(eu_wide)
        eu = eu_wide.astype(bf16)
        acc_e[s] += dot_tn(a2, eu)
        eus.append(eu)
    back = None
    for s in range(4):
        term = dot_nt(eus[s], we[s])
        back = term if back is None else back + term
    vec[GAIN + 1] += column_sum(back * normal)
    vec[SHIFT + 1] += column_sum(back)
    return grad + norm_back(back, normal, inverse, sm[GAIN + 1 : GAIN + 2])


def mixer_back(grad, mixed, wm, acc_m, vec, em):
    for rows in chunks():
        here = grad[rows, :]
        eo = here.astype(bf16)
        vec[BRANCH] += column_sum(here)
        acc_m[...] += dot_tn(eo, mixed[rows, :])
        put_blocks(em, rows, dot(eo, wm[...]))
    em[:, ROWS:HELD, :] = jnp.zeros((2, HELD - ROWS, 128), f32)


def mix_back(em, value, value_at, sm, e, e_low, vec):
    taps = [taps_of(sm, orient) for orient in range(2)]

    def line(i, _):
        rows = pl.ds(pl.multiple_of(i * LINE, LINE), LINE)
        for orient in range(2):
            lanes = slice(orient * 128, (orient + 1) * 128)
            base = orient * 384
            eq, ek, ev = [e[orient * 3 + p, rows, :] for p in range(3)]
            ev = ev + stencil_line(em, orient, taps[orient], i, orient, True)
            e_low[rows, base : base + 384] = jnp.concatenate([eq, ek, ev], axis=1).astype(bf16)
            vec[ENTRY, :, lanes] += column_sum(eq)
            vec[ENTRY + 1, :, lanes] += column_sum(ev)
            for t, part in enumerate(stencil_line_taps(value, value_at[orient], em[orient, rows, :], i, orient)):
                vec[TAPS + t, :, lanes] += part
        return 0

    lax.fori_loop(0, GRID, line, 0)


def project_back(grad, x, e_low, wqkv, sm, acc_q, vec, out):
    for rows in chunks():
        normal, inverse = norm(x[rows, :].astype(f32))
        a = (normal * sm[GAIN : GAIN + 1] + sm[SHIFT : SHIFT + 1]).astype(bf16)
        e = e_low[rows, :]
        acc_q[...] += dot_tn(e, a)
        back = dot(e, wqkv[...])
        vec[GAIN] += column_sum(back * normal)
        vec[SHIFT] += column_sum(back)
        out[rows, :] = (grad[rows, :] + norm_back(back, normal, inverse, sm[GAIN : GAIN + 1])).astype(out.dtype)


def attn_pieces(acc_q, acc_m, sums):
    def qkv(s, p, lo, hi):
        at = (s // 2) * 384 + p * 128 + (s % 2) * 64
        return acc_q[at + lo : at + hi]

    return [(64, lambda s, lo, hi, p=p: qkv(s, p, lo, hi)) for p in range(3)] + [
        (64, lambda s, lo, hi: acc_m[64 * s + lo : 64 * s + hi]),
        (32, lambda s, lo, hi: sums[lo:hi]),
    ]


def ff_pieces(acc_e, acc_r):
    return [(256, lambda s, lo, hi: acc_e[s, lo:hi])] + [
        (64, lambda s, lo, hi, c=c: acc_r[c, 64 * s + lo : 64 * s + hi]) for c in range(4)
    ]


def half_rows(rows, planes):
    return -(-rows // (32 * planes)) * 16 * planes


def unused(rows):
    return [(rows, lambda s, lo, hi: jnp.zeros((hi - lo, D), f32))]


def write_halves(core, pieces, keep, give):
    half = keep.shape[1]

    def write(which, ref):
        for s in range(4):
            at = 0
            for rows, get in pieces:
                lo, hi = max(at, which * half), min(at + rows, (which + 1) * half)
                if lo < hi:
                    ref[s, lo - which * half : hi - which * half] = get(s, lo - at, hi - at).astype(ref.dtype)
                at += rows
            if at < (which + 1) * half:
                ref[s, max(at - which * half, 0) : half] = jnp.zeros((min(half, (which + 1) * half - at), D), ref.dtype)

    for mine in range(2):

        @pl.when(core == mine)
        def _(mine=mine):
            write(mine, keep)
            write(1 - mine, give)


def clear(*refs):
    for ref in refs:
        ref[...] = jnp.zeros_like(ref)


def first_step(fn):
    pl.when(pl.program_id(0) == 0)(fn)


def last_step(fn):
    pl.when(pl.program_id(0) == pl.num_programs(0) - 1)(fn)


def attn_fwd_kernel(place, x, *refs):
    own, near, far = refs[0], refs[1:4], refs[4:7]
    middle, packed, probs, mixed, value, wqkv, wm, sm, qkv, out = refs[7:]

    @first_step
    def _():
        assemble_attn(place[0], place[1], own, near, far, wqkv, wm, sm)
        project(x, wqkv, sm, qkv)

    crops = [pl.program_id(0) * STEP_CROPS + i for i in range(STEP_CROPS)]
    attend_crops(place, crops, range(STEP_CROPS), qkv, packed, probs, out)

    @last_step
    def _():
        mix(out, qkv, (2, 5), sm, mixed)
        for orient in range(2):
            value[orient] = qkv[orient * 3 + 2, :ROWS, :].astype(bf16)
        mixer(x, mixed, wm, sm, middle)


def ff_fwd_kernel(place, middle, sm, *refs):
    own, near, far = refs[0], refs[1:4], refs[4:7]
    out, we, wr = refs[7:]

    @first_step
    def _():
        assemble_ff(place[0], place[1], own, near, far, we, wr)

    out[...] = ff_forward(middle[...], we, wr, sm)


def top_kernel(place, x, cotangent, *refs):
    attn_in, ff_in = refs[0:7], refs[7:14]
    (output, grad_out, keep, give) = refs[14:18]
    (wqkv, wm, sm, we, wr, qkv, out, packed, probs, mixed, middle, g, slope, em, e, e_low,
     acc_e, acc_r, acc_q, acc_m, vec) = refs[18:]

    assemble_attn(place[0], place[1], attn_in[0], attn_in[1:4], attn_in[4:7], wqkv, wm, sm)
    assemble_ff(place[0], place[1], ff_in[0], ff_in[1:4], ff_in[4:7], we, wr)
    clear(acc_e, acc_r, acc_q, acc_m, vec)
    project(x, wqkv, sm, qkv)

    def ahead(i, _):
        crops = [i * STEP_CROPS + j for j in range(STEP_CROPS)]
        attend_crops(place, crops, crops, qkv, packed, probs, out)
        return 0

    lax.fori_loop(0, CROPS // STEP_CROPS, ahead, 0)
    mix(out, qkv, (2, 5), sm, mixed)
    mixer(x, mixed, wm, sm, middle)
    for rows in chunks():
        gs, slopes = {}, {}
        output[rows, :] = ff_forward(middle[rows, :], we, wr, sm, gs, slopes).astype(bf16)
        for s in range(4):
            g[rows, s * 256 : (s + 1) * 256] = gs[s]
            slope[rows, s * 256 : (s + 1) * 256] = slopes[s]
    for rows in chunks():
        held = lambda s: (g[rows, s * 256 : (s + 1) * 256], slope[rows, s * 256 : (s + 1) * 256])
        middle_here = middle[rows, :]
        middle[rows, :] = ff_backward(cotangent[rows, :].astype(f32), middle_here, we, wr, sm, acc_e, acc_r, vec, held)
    mixer_back(middle, mixed, wm, acc_m, vec, em)

    def behind(i, _):
        crops = [i * STEP_CROPS + j for j in range(STEP_CROPS)]
        attend_crops_back(crops, crops, em, packed, probs, e)
        return 0

    lax.fori_loop(0, CROPS // STEP_CROPS, behind, 0)
    mix_back(em, qkv, (2, 5), sm, e, e_low, vec)
    project_back(middle, x, e_low, wqkv, sm, acc_q, vec, grad_out)
    pieces = attn_pieces(acc_q, acc_m, jnp.sum(vec[...], axis=1)) + unused(32) + ff_pieces(acc_e, acc_r)
    write_halves(place[1], pieces, keep, give)


def ff_bwd_kernel(place, grad, middle, we, wr, sm, grad_mid, keep, give, vec, acc_e, acc_r):
    @first_step
    def _():
        clear(acc_e, acc_r, vec)

    grad_mid[...] = ff_backward(grad[...], middle[...], we, wr, sm, acc_e, acc_r, vec)

    @last_step
    def _():
        write_halves(place[1], ff_pieces(acc_e, acc_r), keep, give)


def attn_bwd_kernel(grad, packed, probs, mixed, wm, vec_in, e, em, acc_m, vec):
    @first_step
    def _():
        clear(acc_m)
        vec[...] = vec_in[...]
        mixer_back(grad, mixed, wm, acc_m, vec, em)

    crops = [pl.program_id(0) * STEP_CROPS + i for i in range(STEP_CROPS)]
    attend_crops_back(crops, range(STEP_CROPS), em, packed, probs, e)


def entry_bwd_kernel(place, grad, x, e, em, value, wqkv, sm, acc_m, vec_in, patch_grad, keep, give, e_low, acc_q, vec):
    clear(acc_q)
    vec[...] = vec_in[...]
    mix_back(em, value, (0, 1), sm, e, e_low, vec)
    project_back(grad, x, e_low, wqkv, sm, acc_q, vec, patch_grad)
    write_halves(place[1], attn_pieces(acc_q, acc_m, jnp.sum(vec[...], axis=1)), keep, give)


def whole(shape):
    return pl.BlockSpec(shape, lambda i, *_: (0,) * len(shape))


def rows_of(lanes, rows=CHUNK):
    return pl.BlockSpec((rows, lanes), lambda i, *_: (i, 0))


def crop_spec(*dims):
    return pl.BlockSpec((STEP_CROPS, 4) + dims, lambda i, *_: (i, 0, 0, 0))


def unit_specs(rows):
    return [whole((rows, D))] + [whole((rows // 2, D))] * 6


def shape(dims, dtype=bf16):
    return jax.ShapeDtypeStruct(dims, dtype)


def params(micros):
    return dict(
        compiler_params=pltpu.CompilerParams(
            vmem_limit_bytes=58 * 1024 * 1024, dimension_semantics=("arbitrary",)
        ),
        cost_estimate=pl.CostEstimate(flops=int(micros * 1e9), bytes_accessed=1 << 20, transcendentals=0),
    )


v = pltpu.VMEM


def attn_fwd_call(place, x, unit):
    return pl.pallas_call(
        attn_fwd_kernel,
        grid_spec=pltpu.PrefetchScalarGridSpec(
            num_scalar_prefetch=1,
            grid=(CROPS // STEP_CROPS,),
            in_specs=[whole((ROWS, D))] + unit_specs(ATTN_ROWS),
            out_specs=[whole((ROWS, D)), crop_spec(WIN, 384), crop_spec(WIN, 512), whole((ROWS, D)), whole((2, ROWS, 128)), whole((768, D)), whole((D, D)), whole((32, D))],
            scratch_shapes=[v((6, HELD, 128), f32), v((2, HELD, 128), f32)],
        ),
        out_shape=[shape((ROWS, D), f32), shape((CROPS, 4, WIN, 384)), shape((CROPS, 4, WIN, 512)), shape((ROWS, D)), shape((2, ROWS, 128)), shape((768, D)), shape((D, D)), shape((32, D), f32)],
        name="attn_fwd",
        **params(10),
    )(place, x, *unit)


def ff_fwd_call(place, middle, sm, unit):
    return pl.pallas_call(
        ff_fwd_kernel,
        grid_spec=pltpu.PrefetchScalarGridSpec(
            num_scalar_prefetch=1,
            grid=(ROWS // CHUNK,),
            in_specs=[rows_of(D), whole((32, D))] + unit_specs(FF_ROWS),
            out_specs=[rows_of(D), whole((4, D, D)), whole((D, FF))],
        ),
        out_shape=[shape((ROWS, D), f32), shape((4, D, D)), shape((D, FF))],
        name="ff_fwd",
        **params(6),
    )(place, middle, sm, *unit)


def top_call(place, x, cotangent, attn_unit, ff_unit, half):
    return pl.pallas_call(
        top_kernel,
        grid_spec=pltpu.PrefetchScalarGridSpec(
            num_scalar_prefetch=1,
            grid=(1,),
            in_specs=[whole((ROWS, D)), whole((ROWS, D))] + unit_specs(ATTN_ROWS) + unit_specs(FF_ROWS),
            out_specs=[whole((ROWS, D)), whole((ROWS, D))] + [whole((4, half, D))] * 2,
            scratch_shapes=[
                v((768, D), bf16), v((D, D), bf16), v((32, D), f32), v((4, D, D), bf16), v((D, FF), bf16),
                v((6, HELD, 128), f32), v((2, HELD, 128), f32), v((CROPS, 4, WIN, 384), bf16), v((CROPS, 4, WIN, 512), bf16),
                v((ROWS, D), bf16), v((ROWS, D), f32), v((ROWS, FF), bf16), v((ROWS, FF), bf16),
                v((2, HELD, 128), f32), v((6, HELD, 128), f32), v((ROWS, 768), bf16),
                v((4, D, D), f32), v((4, D, D), f32), v((768, D), f32), v((D, D), f32), v((32, CROPS, D), f32),
            ],
        ),
        out_shape=[shape((ROWS, D)), shape((ROWS, D), f32)] + [shape((4, half, D))] * 2,
        name="top_block",
        **params(30),
    )(place, x, cotangent, *attn_unit, *ff_unit)


def ff_bwd_call(place, grad, middle, we, wr, sm, half):
    return pl.pallas_call(
        ff_bwd_kernel,
        grid_spec=pltpu.PrefetchScalarGridSpec(
            num_scalar_prefetch=1,
            grid=(ROWS // CHUNK,),
            in_specs=[rows_of(D), rows_of(D), whole((4, D, D)), whole((D, FF)), whole((32, D))],
            out_specs=[rows_of(D)] + [whole((4, half, D))] * 2 + [whole((32, CROPS, D))],
            scratch_shapes=[v((4, D, D), f32), v((4, D, D), f32)],
        ),
        out_shape=[shape((ROWS, D), f32)] + [shape((4, half, D))] * 2 + [shape((32, CROPS, D), f32)],
        name="ff_bwd",
        **params(10),
    )(place, grad, middle, we, wr, sm)


def attn_bwd_call(grad, packed, probs, mixed, wm, vec):
    return pl.pallas_call(
        attn_bwd_kernel,
        grid=(CROPS // STEP_CROPS,),
        in_specs=[whole((ROWS, D)), crop_spec(WIN, 384), crop_spec(WIN, 512), whole((ROWS, D)), whole((D, D)), whole((32, CROPS, D))],
        out_specs=[whole((6, HELD, 128)), whole((2, HELD, 128)), whole((D, D)), whole((32, CROPS, D))],
        out_shape=[shape((6, HELD, 128), f32), shape((2, HELD, 128), f32), shape((D, D), f32), shape((32, CROPS, D), f32)],
        name="attn_bwd",
        **params(9),
    )(grad, packed, probs, mixed, wm, vec)


def entry_bwd_call(place, grad, x, e, em, value, wqkv, sm, acc_m, vec):
    return pl.pallas_call(
        entry_bwd_kernel,
        grid_spec=pltpu.PrefetchScalarGridSpec(
            num_scalar_prefetch=1,
            grid=(1,),
            in_specs=[whole((ROWS, D)), whole((ROWS, D)), whole((6, HELD, 128)), whole((2, HELD, 128)), whole((2, ROWS, 128)), whole((768, D)), whole((32, D)), whole((D, D)), whole((32, CROPS, D))],
            out_specs=[whole((ROWS, D))] + [whole((4, LOW_ROWS // 2, D))] * 2,
            scratch_shapes=[v((ROWS, 768), bf16), v((768, D), f32), v((32, CROPS, D), f32)],
        ),
        out_shape=[shape((ROWS, D))] + [shape((4, LOW_ROWS // 2, D))] * 2,
        name="entry_bwd",
        **params(8),
    )(place, grad, x, e, em, value, wqkv, sm, acc_m, vec)


def to_rows(x):
    return jnp.transpose(x, (1, 2, 0, 3)).reshape(ROWS, D)


def from_rows(x):
    return jnp.transpose(x.reshape(GRID, GRID, CROPS, D), (2, 0, 1, 3))


def pack_attn_kernel(layer, place, qkv, mixer_t, gain, shift, entry, taps, branch, hidden_bias, own, mine):
    me, core = place[0], place[1]
    own[0:192] = qkv[0]
    own[192:256] = mixer_t[0]
    rows = jnp.concatenate(
        [ref[layer].astype(f32) for ref in (gain, shift, entry)] + [taps[:, layer].astype(f32), branch[layer].astype(f32)], axis=0
    )
    lane = lax.broadcasted_iota(jnp.int32, (18, D), 1)
    vectors = jnp.where(lane // 64 == me, jnp.concatenate([rows] * 4, axis=1), 0.0)
    row = lax.broadcasted_iota(jnp.int32, (14, D), 0)
    hidden_rows = jnp.where(row == me, hidden_bias[layer : layer + 1].astype(f32), 0.0)
    own[256:288] = jnp.concatenate([vectors, hidden_rows], axis=0).astype(bf16)
    mine[...] = own[pl.ds(pl.multiple_of(core * (ATTN_ROWS // 2), 16), ATTN_ROWS // 2)]


def pack_ff_kernel(place, expand, reduce_t, own, mine):
    own[0:256] = expand[0]
    for c in range(4):
        own[256 + 64 * c : 320 + 64 * c] = reduce_t[0, :, c * 256 : (c + 1) * 256]
    mine[...] = own[pl.ds(pl.multiple_of(place[1] * (FF_ROWS // 2), 16), FF_ROWS // 2)]


def of_layer(layer, *dims):
    return pl.BlockSpec((1,) + dims, lambda i, *_: (layer,) + (0,) * len(dims))


def local_call(kernel, name, place, arrays, outs, in_specs=None):
    return pl.pallas_call(
        kernel,
        grid_spec=pltpu.PrefetchScalarGridSpec(
            num_scalar_prefetch=1,
            grid=(1,),
            in_specs=[whole(x.shape) for x in arrays] if in_specs is None else in_specs,
            out_specs=[whole(dims) for dims, _ in outs],
        ),
        out_shape=[shape(dims, dtype) for dims, dtype in outs],
        name=name,
        **params(1),
    )(place, *arrays)


def pack_attn(place, layer, qkv_t, mixer_t, vectors):
    specs = [of_layer(layer, 192, D), of_layer(layer, 64, D)] + [whole(x.shape) for x in vectors]
    return local_call(
        functools.partial(pack_attn_kernel, layer), "pack_attn", place, [qkv_t, mixer_t, *vectors],
        [((ATTN_ROWS, D), bf16), ((ATTN_ROWS // 2, D), bf16)], specs,
    )


def pack_ff(place, layer, expand, reduce_t):
    return local_call(
        pack_ff_kernel, "pack_ff", place, [expand, reduce_t],
        [((FF_ROWS, D), bf16), ((FF_ROWS // 2, D), bf16)], [of_layer(layer, D, D), of_layer(layer, 64, FF)],
    )


def turn_mp(x, k):
    n = lax.axis_size("mp")
    return lax.ppermute(x, "mp", [(i, (i + k) % n) for i in range(n)])


def swap_dp(x, bits):
    n = lax.axis_size("dp")
    return lax.ppermute(x, "dp", [(i, i ^ bits) for i in range(n)])


def turn_all(x):
    return [turn_mp(x, k) for k in (1, 2, 3)]


def swap_core(xs):
    return [swap_dp(x, 1) for x in xs]


def after(xs, *others):
    return lax.optimization_barrier((xs, others))[0]


def add_up(refs, index):
    total = refs[0][index].astype(f32)
    for ref in refs[1:]:
        total = total + ref[index].astype(f32)
    return total


def spread_kernel(planes, place, keep, got, *outs):
    for b in range(planes):
        at = place[2] ^ b
        for s in range(4):
            outs[b][s] = add_up((keep, got), (s, at)).astype(bf16)


def spread(place, planes, keep, got):
    r = keep.shape[1] // planes
    split = [x.reshape(4, planes, r, D) for x in (keep, got)]
    return local_call(functools.partial(spread_kernel, planes), "spread", place, split, [((4, r, D), bf16)] * planes)


def shards_kernel(place, *refs):
    ins, outs = refs[:-4], refs[-4:]
    for k in range(4):
        at = lax.rem(place[0] + k, 4)
        outs[k][...] = add_up(ins, at).astype(outs[k].dtype)


def shards(place, parts):
    r = parts[0].shape[1]
    return local_call(shards_kernel, "shards", place, parts, [((r, D), f32)] + [((r, D), bf16)] * 3)


def low_shards_kernel(count, place, *refs):
    attn, ff, outs = refs[:2], refs[2 : 2 + count], refs[2 + count :]
    cut = attn[0].shape[1]
    for k in range(4):
        at = lax.rem(place[0] + k, 4)
        outs[k][:cut] = add_up(attn, at).astype(outs[k].dtype)
        outs[k][cut:] = add_up(ff, at).astype(outs[k].dtype)


def low_shards(place, attn, ff):
    r = attn[0].shape[1] + ff[0].shape[1]
    return local_call(
        functools.partial(low_shards_kernel, len(ff)), "low_shards", place, [*attn, *ff], [((r, D), f32)] + [((r, D), bf16)] * 3
    )


def share_kernel(place, *refs):
    low, top, (out,) = refs[:4], refs[4:8], refs[8:]
    cut = low[0].shape[0]
    out[:cut] = add_up(low, slice(None)).astype(out.dtype)
    out[cut:] = add_up(top, slice(None)).astype(out.dtype)


def share(place, low, top):
    r = low[0].shape[0] + top[0].shape[0]
    return local_call(share_kernel, "share", place, [*low, *top], [((r, D), bf16)])[0]


def half_kernel(planes, cut_a, cut_f, place, *refs):
    parts, out = refs[:-1], refs[-1]
    r_f, r_t = cut_f - cut_a, parts[0].shape[0] - cut_f
    out[:cut_a] = add_up(parts, slice(0, cut_a)).astype(out.dtype)
    for b in range(planes):
        at = place[2] ^ b
        out[pl.ds(pl.multiple_of(cut_a + at * r_f, 16), r_f)] = parts[b][cut_a:cut_f]
        out[pl.ds(pl.multiple_of(cut_a + planes * r_f + at * r_t, 16), r_t)] = parts[b][cut_f:]


def unpack_kernel(cut_f, cut_t, place, mine, other, packed, mixer_g, expand, reduce_g, gain, shift, entry, taps, branch, hidden_g):
    me, core = place[0], place[1]
    half_a, half_f, half_t = cut_f, cut_t - cut_f, mine.shape[0] - cut_t

    def rows(which, lo, hi):
        start, half = which
        out = []
        for c in range(2):
            a, b = max(lo, c * half), min(hi, (c + 1) * half)
            if a < b:
                at = slice(start + a - c * half, start + b - c * half)
                out.append(jnp.where(core == c, mine[at].astype(f32), other[at].astype(f32)))
        return out[0] if len(out) == 1 else jnp.concatenate(out, axis=0)

    low_a, low_f, top = (0, half_a), (cut_f, half_f), (cut_t, half_t)
    for layer, attn, ff, ff_at in ((0, low_a, low_f, 0), (1, top, top, 320)):
        packed[layer] = rows(attn, 0, 192)
        mixer_g[layer] = rows(attn, 192, 256)
        expand[layer] = rows(ff, ff_at, ff_at + 256)
        for c in range(4):
            at = ff_at + 256 + 64 * c
            reduce_g[layer, :, c * 256 : (c + 1) * 256] = rows(ff, at, at + 64)
        vectors = rows(attn, 256, 288)
        mine_lanes = vectors[:, :64]
        for s in range(1, 4):
            mine_lanes = jnp.where(me == s, vectors[:, 64 * s : 64 * (s + 1)], mine_lanes)
        gain[layer] = mine_lanes[GAIN : GAIN + 2]
        shift[layer] = mine_lanes[SHIFT : SHIFT + 2]
        entry[layer] = mine_lanes[ENTRY : ENTRY + 2]
        branch[layer] = mine_lanes[BRANCH : BRANCH + 2]
        for t in range(10):
            taps[t, layer : layer + 1] = mine_lanes[TAPS + t : TAPS + t + 1]
        row = vectors[HIDDEN : HIDDEN + 1]
        for s in range(1, 4):
            row = jnp.where(me == s, vectors[HIDDEN + s : HIDDEN + s + 1], row)
        hidden_g[layer : layer + 1] = row


def body(patches, validity, norm_gain, norm_shift, qkv_weight, entry_bias, stencil, mixer_weight, branch_bias, expand_weight, hidden_bias, reduce_weight, cotangent):
    dp = lax.axis_size("dp")
    planes = dp // 2
    me, at_dp = lax.axis_index("mp"), lax.axis_index("dp")
    heights = jnp.sum(validity[:, :, 0], axis=1)
    widths = jnp.sum(validity[:, 0, :], axis=1)
    place = jnp.stack([me, at_dp % 2, at_dp // 2]).astype(jnp.int32)
    sizes = jnp.concatenate([jnp.stack([me, at_dp % 2]), jnp.stack([heights, widths], axis=1).reshape(-1)]).astype(jnp.int32)

    qkv_t = jnp.transpose(qkv_weight, (0, 2, 3, 1)).reshape(2, 192, D)
    mixer_t = jnp.transpose(mixer_weight, (0, 2, 1))
    reduce_t = jnp.transpose(reduce_weight, (0, 2, 1))
    vectors = (norm_gain, norm_shift, entry_bias, jnp.transpose(stencil, (1, 0, 2)), branch_bias, hidden_bias)

    own_a0, half_a0 = pack_attn(place, 0, qkv_t, mixer_t, vectors)
    near_a0 = turn_all(half_a0)
    own_f0, half_f0 = pack_ff(place, 0, expand_weight, reduce_t)
    near_f0 = turn_all(half_f0)
    own_a1, half_a1 = pack_attn(place, 1, qkv_t, mixer_t, vectors)
    own_f1, half_f1 = pack_ff(place, 1, expand_weight, reduce_t)
    far_a0 = swap_core(near_a0)

    x, top_grad = to_rows(patches), to_rows(cotangent)
    middle, packed, probs, mixed, value, wqkv, wm, sm = attn_fwd_call(sizes, x, [own_a0] + near_a0 + far_a0)
    near_f0, middle, half_a1, half_f1 = lax.optimization_barrier((near_f0, middle, half_a1, half_f1))
    far_f0 = swap_core(near_f0)
    near_a1, near_f1 = turn_all(half_a1), turn_all(half_f1)
    state, we, wr = ff_fwd_call(sizes, middle, sm, [own_f0] + near_f0 + far_f0)
    near_a1, near_f1, state = lax.optimization_barrier((near_a1, near_f1, state))
    far_a1, far_f1 = swap_core(near_a1), swap_core(near_f1)
    output, grad, keep_1, give_1 = top_call(sizes, state, top_grad, [own_a1] + near_a1 + far_a1, [own_f1] + near_f1 + far_f1, half_rows(TOP_ROWS, planes))

    got_1 = swap_dp(give_1, 1)
    grad_mid, keep_f, give_f, vec = ff_bwd_call(place, grad, middle, we, wr, sm, half_rows(FF_ROWS, planes))
    got_1, grad_mid, keep_f, give_f = lax.optimization_barrier((got_1, grad_mid, keep_f, give_f))

    got_f = swap_dp(give_f, 1)
    parts_1 = spread(place, planes, keep_1, got_1)
    grad_mid, parts_1 = lax.optimization_barrier((grad_mid, parts_1))
    planes_1 = [parts_1[0]] + [swap_dp(parts_1[b], 2 * b) for b in range(1, planes)]
    e, em, acc_m, vec = attn_bwd_call(grad_mid, packed, probs, mixed, wm, vec)
    planes_1, got_f, e = lax.optimization_barrier((planes_1, got_f, e))

    shards_1 = shards(place, planes_1)
    parts_f = spread(place, planes, keep_f, got_f)
    e, shards_1, parts_f = lax.optimization_barrier((e, shards_1, parts_f))
    mp_1 = [shards_1[0]] + [turn_mp(shards_1[k], k) for k in (1, 2, 3)]
    planes_f = [parts_f[0]] + [swap_dp(parts_f[b], 2 * b) for b in range(1, planes)]
    patch_grad, keep_a, give_a = entry_bwd_call(place, grad_mid, x, e, em, value, wqkv, sm, acc_m, vec)

    got_a = swap_dp(give_a, 1)
    shards_0 = low_shards(place, [keep_a, got_a], planes_f)
    mp_0 = [shards_0[0]] + [turn_mp(shards_0[k], k) for k in (1, 2, 3)]
    both = share(place, mp_0, mp_1)
    held = [both] + [swap_dp(both, 2 * b) for b in range(1, planes)]
    cut_a, cut_f = LOW_ROWS // 2, shards_0[0].shape[0]
    cut_t = cut_a + planes * (cut_f - cut_a)
    total = cut_t + planes * (both.shape[0] - cut_f)
    mine = local_call(functools.partial(half_kernel, planes, cut_a, cut_f), "half", place, held, [((total, D), bf16)])[0]
    other = swap_dp(mine, 1)
    outs = [(2, 192, D), (2, 64, D), (2, D, D), (2, 64, FF), (2, 2, 64), (2, 2, 64), (2, 2, 64), (10, 2, 64), (2, 2, 64), (2, D)]
    packed_g, mixer_g, expand_g, reduce_g, gain_g, shift_g, entry_g, taps_g, branch_g, hidden_g = local_call(
        functools.partial(unpack_kernel, cut_a, cut_t), "unpack", place, [mine, other], [(dims, f32) for dims in outs]
    )
    return (
        from_rows(output), from_rows(patch_grad), gain_g, shift_g,
        jnp.transpose(packed_g.reshape(2, 3, 64, D), (0, 3, 1, 2)), entry_g, jnp.transpose(taps_g, (1, 0, 2)),
        jnp.transpose(mixer_g, (0, 2, 1)), branch_g, expand_g, hidden_g, jnp.transpose(reduce_g, (0, 2, 1)),
    )


def solution(mesh):
    crops = P(("dp", "mp"), None, None, None)
    lanes = P(None, None, "mp")
    deep = P(None, None, None, "mp")
    return jax.shard_map(
        body,
        mesh=mesh,
        in_specs=(crops, P(("dp", "mp"), None, None), lanes, lanes, deep, lanes, lanes, lanes, lanes, lanes, P(None, "mp"), lanes, crops),
        out_specs=(crops, crops, lanes, lanes, deep, lanes, lanes, lanes, lanes, lanes, P(None, "mp"), lanes),
        check_vma=False,
    )
```

```python
import functools

import jax
import jax.numpy as jnp
from jax import lax
from jax.experimental import pallas as pl
from jax.experimental.pallas import tpu as pltpu
from jax.sharding import PartitionSpec as P

GRID = 14
STRIPE = 7
CELLS = GRID * GRID
CROPS = 8
ROWS = CELLS * CROPS
LINE = GRID * CROPS
HELD = ROWS + 112
WIN = 112
HALF_HEADS = 4
HEAD = 32
D = 256
FF = 1024
STEP_CROPS = 4
CHUNK = 784

norm_eps = 1e-05
masked_score = -1e30
root_half = 0.7071067811865476
inverse_root_tau = 0.3989422804014327
log2_e = 1.4426950408889634
factor = HEAD**-0.5

f32 = jnp.float32
bf16 = jnp.bfloat16

HALF_ATTN = 144
HALF_FF = 256
FF_ROWS = 512
TOP_ROWS = 832
LOW_ROWS = 288
GAIN, SHIFT, ENTRY, TAPS, BRANCH, HIDDEN = 0, 2, 4, 6, 16, 18


def dot(a, b):
    return lax.dot_general(a, b, (((1,), (0,)), ((), ())), preferred_element_type=f32)


def dot_nt(a, b):
    return lax.dot_general(a, b, (((1,), (1,)), ((), ())), preferred_element_type=f32)


def dot_tn(a, b):
    return lax.dot_general(a, b, (((0,), (0,)), ((), ())), preferred_element_type=f32)


def norm(x):
    center = x - jnp.mean(x, axis=-1, keepdims=True)
    spread = jnp.mean(center * center, axis=-1, keepdims=True)
    inverse = lax.rsqrt(spread + norm_eps)
    return center * inverse, inverse


def norm_back(grad, normal, inverse, gain):
    scaled = grad * gain
    return inverse * (
        scaled
        - jnp.mean(scaled, axis=-1, keepdims=True)
        - normal * jnp.mean(scaled * normal, axis=-1, keepdims=True)
    )


def column_sum(x):
    return jnp.sum(x.reshape(x.shape[0] // CROPS, CROPS, x.shape[1]), axis=0)


def window_row_inside(orient):
    row = lax.broadcasted_iota(jnp.int32, (WIN, 128), 0)
    return row < 98 if orient == 0 else row % 8 < STRIPE


def key_bias(orient, window, height, width):
    row = lax.broadcasted_iota(jnp.int32, (WIN, 128), 0)
    if orient == 0:
        line, column = row // GRID + window * STRIPE, row % GRID
    else:
        line, column = row // 8, row % 8 + window * STRIPE
    valid = window_row_inside(orient) & (line < height) & (column < width)
    return jnp.where(valid, 0.0, masked_score)


def load_window(ref, block, crop, orient, window):
    if orient == 0:
        return ref[block, pl.ds(98 * CROPS * window + crop, WIN, stride=CROPS), :]
    parts = [
        ref[block, pl.ds((line * GRID + window * STRIPE) * CROPS + crop, 8, stride=CROPS), :]
        for line in range(GRID)
    ]
    return jnp.concatenate(parts, axis=0)


def store_window(ref, block, crop, orient, window, x):
    if orient == 0:
        ref[block, pl.ds(98 * CROPS * window + crop, 98, stride=CROPS), :] = x[:98]
        return
    for line in range(GRID):
        at = (line * GRID + window * STRIPE) * CROPS + crop
        ref[block, pl.ds(at, STRIPE, stride=CROPS), :] = x[line * 8 : line * 8 + STRIPE]


def heads_apart(x, inside=None):
    lane = lax.broadcasted_iota(jnp.int32, (WIN, 128), 1) // HEAD
    rest = jnp.zeros((128 - WIN, 128), bf16)
    blocks = []
    for head in range(HALF_HEADS):
        keep = lane == head
        if inside is not None:
            keep = keep & inside
        blocks.append(jnp.where(keep, x, 0.0).astype(bf16))
        blocks.append(rest)
    return jnp.concatenate(blocks, axis=0)


def by_head(flat_turned, probs):
    parts = []
    for head in range(HALF_HEADS):
        parts.append(
            dot(flat_turned[head * HEAD : (head + 1) * HEAD], probs[:, head * 128 : (head + 1) * 128])
        )
    return jnp.concatenate(parts, axis=0)


def attend(queries, keys, values, biases):
    apart = [heads_apart(x) for x in queries]
    value_turned = [x.T.astype(bf16) for x in values]
    scores = [dot_nt(k.astype(bf16), q) for k, q in zip(keys, apart)]
    scores = [s * (factor * log2_e) + jnp.concatenate([b] * HALF_HEADS, axis=1) for s, b in zip(scores, biases)]
    peaks = [jnp.max(s, axis=0, keepdims=True) for s in scores]
    raised = [jnp.exp2(s - p) for s, p in zip(scores, peaks)]
    shares = [1.0 / jnp.sum(r, axis=0, keepdims=True) for r in raised]
    probs = [(r * s).astype(bf16) for r, s in zip(raised, shares)]
    outs = [by_head(v, p) for v, p in zip(value_turned, probs)]
    return [o.T[:WIN] for o in outs], probs


def attend_back(grads, queries, keys, values, probs, insides):
    grad_apart = [heads_apart(x, i) for x, i in zip(grads, insides)]
    grad_probs = [dot_nt(v, g) for v, g in zip(values, grad_apart)]
    key_turned = [x.astype(f32).T.astype(bf16) for x in keys]
    grad_value = [dot(p, g) for p, g in zip(probs, grad_apart)]
    wide = [p.astype(f32) for p in probs]
    inner = [jnp.sum(g * w, axis=0, keepdims=True) for g, w in zip(grad_probs, wide)]
    grad_scores = [(w * (g - i)).astype(bf16) for w, g, i in zip(wide, grad_probs, inner)]
    apart = [heads_apart(x) for x in queries]
    grad_key = [dot(s, q) * factor for s, q in zip(grad_scores, apart)]
    grad_query = [by_head(k, s) for k, s in zip(key_turned, grad_scores)]
    grad_query = [g.T[:WIN] * factor for g in grad_query]
    return grad_query, grad_key, grad_value


WINDOWS = [(orient, window) for orient in range(2) for window in range(2)]


def steps_along(x, orient):
    zero = jnp.zeros((CROPS, x.shape[1]), x.dtype)
    if orient == 0:
        return {-1: jnp.concatenate([zero, x[:-CROPS]], axis=0), 0: x, 1: jnp.concatenate([x[CROPS:], zero], axis=0)}
    half = LINE // 2
    left, right = x[:half], x[half:]
    return {
        -1: jnp.concatenate([zero, left[:-CROPS], zero, right[:-CROPS]], axis=0),
        0: x,
        1: jnp.concatenate([left[CROPS:], zero, right[CROPS:], zero], axis=0),
    }


def line_reaches(line, step, orient):
    if step == 0:
        return None
    stops = (GRID, STRIPE) if orient == 0 else (GRID,)
    edges = [(stop - 1) if step == 1 else (stop % GRID) for stop in stops]
    ok = line != edges[0]
    for edge in edges[1:]:
        ok = ok & (line != edge)
    return jnp.where(ok, 1.0, 0.0).astype(f32)


def line_at(ref, block, line):
    held = jnp.clip(line, 0, GRID - 1)
    return ref[block, pl.ds(pl.multiple_of(held * LINE, LINE), LINE), :]


def stencil_line(ref, block, taps, line, orient, back):
    total = None
    for step in (-1, 0, 1):
        moved = steps_along(line_at(ref, block, line + (-step if back else step)).astype(f32), orient)
        reach = line_reaches(line, -step if back else step, orient)
        for side in (-1, 0, 1):
            tap = taps[3 * (step + 1) + side + 1]
            if reach is not None:
                tap = tap * reach
            term = moved[-side if back else side] * tap
            total = term if total is None else total + term
    return total


def stencil_line_taps(ref, block, grad, line, orient):
    sums = []
    for step in (-1, 0, 1):
        moved = steps_along(line_at(ref, block, line + step).astype(f32), orient)
        reach = line_reaches(line, step, orient)
        for side in (-1, 0, 1):
            part = column_sum(grad * moved[side])
            sums.append(part if reach is None else part * reach)
    sums.append(column_sum(grad))
    return sums


def assemble_attn(layer, me, core, own, near, far, wqkv, wm, sm):
    qkv, mixer_t, vec = own

    def put(shard, blocks, at, mixer_rows, mixer_at):
        orient, part = lax.div(shard, 2), lax.rem(shard, 2)
        for i, block in enumerate(blocks):
            j = at + i
            row = orient * 384 + lax.div(j, 2) * 128 + part * 64 + lax.rem(j, 2) * 32
            wqkv[pl.ds(pl.multiple_of(row, 32), 32), :] = block
        wm[pl.ds(pl.multiple_of(shard * 64 + mixer_at, 32), mixer_rows.shape[0]), :] = mixer_rows

    put(me, [qkv[0, 32 * i : 32 * (i + 1)] for i in range(6)], jnp.int32(0), mixer_t[0], 0)
    sm[...] = vec[layer].astype(f32)
    for halves, which in ((near, core), (far, 1 - core)):
        for k, half in enumerate(halves, 1):
            shard = lax.rem(me + 4 - k, 4)
            put(shard, [half[32 * i : 32 * (i + 1)] for i in range(3)], 3 * which, half[96:128], 32 * which)
            sm[pl.ds(pl.multiple_of(16 * which, 16), 16), :] += half[128:144].astype(f32)


def assemble_ff(first, me, core, own, near, far, we, wr):
    expand, reduce_t = own
    we[me] = expand[0]
    wr[pl.ds(pl.multiple_of(me * 64, 64), 64), :] = reduce_t[0]
    for halves, which in ((near, core), (far, 1 - core)):
        for k, half in enumerate(halves, 1):
            shard = lax.rem(me + 4 - k, 4)
            we[shard, pl.ds(pl.multiple_of(128 * which, 128), 128), :] = half[first : first + 128]
            row = pl.multiple_of(shard * 64 + 32 * which, 32)
            for c in range(4):
                at = first + 128 + 32 * c
                wr[pl.ds(row, 32), c * 256 : (c + 1) * 256] = half[at : at + 32]


def chunks():
    return [slice(at, at + CHUNK) for at in range(0, ROWS, CHUNK)]


def put_blocks(ref, rows, x):
    for block in range(x.shape[1] // 128):
        ref[block, rows, :] = x[:, block * 128 : (block + 1) * 128]


def project(x, wqkv, sm, qkv):
    zero = jnp.zeros((1, 128), f32)
    query_bias, value_bias = sm[ENTRY : ENTRY + 1], sm[ENTRY + 1 : ENTRY + 2]
    bias = jnp.concatenate(
        [query_bias[:, :128], zero, value_bias[:, :128], query_bias[:, 128:], zero, value_bias[:, 128:]], axis=1
    )
    for rows in chunks():
        normal, _ = norm(x[rows, :].astype(f32))
        a = (normal * sm[GAIN : GAIN + 1] + sm[SHIFT : SHIFT + 1]).astype(bf16)
        put_blocks(qkv, rows, dot_nt(a, wqkv[...]) + bias)
    qkv[:, ROWS:HELD, :] = jnp.zeros((6, HELD - ROWS, 128), f32)


def attend_crops(place, crops, slots, qkv, packed, probs_ref, out):
    at, lists = [], ([], [], [], [])
    for crop, slot in zip(crops, slots):
        height, width = place[2 + 2 * crop], place[3 + 2 * crop]
        for n, (orient, window) in enumerate(WINDOWS):
            three = [load_window(qkv, orient * 3 + p, crop, orient, window) for p in range(3)]
            packed[slot, n] = jnp.concatenate(three, axis=1).astype(bf16)
            entries = (*three, key_bias(orient, window, height, width))
            for held, new in zip(lists, entries):
                held.append(new)
            at.append((crop, slot, n, orient, window))
    outs, probs = attend(*lists)
    for (crop, slot, n, orient, window), o, p in zip(at, outs, probs):
        probs_ref[slot, n] = p
        store_window(out, orient, crop, orient, window, o)


def attend_crops_back(crops, slots, em, packed, probs_ref, e):
    at, lists = [], ([], [], [], [], [], [])
    for crop, slot in zip(crops, slots):
        for n, (orient, window) in enumerate(WINDOWS):
            grad = load_window(em, orient, crop, orient, window)
            entries = (
                grad, packed[slot, n, :, :128], packed[slot, n, :, 128:256], packed[slot, n, :, 256:],
                probs_ref[slot, n], window_row_inside(orient),
            )
            for held, new in zip(lists, entries):
                held.append(new)
            at.append((crop, orient, window))
    for (crop, orient, window), dq, dk, dv in zip(at, *attend_back(*lists)):
        for p, part in enumerate((dq, dk, dv)):
            store_window(e, orient * 3 + p, crop, orient, window, part)


def taps_of(sm, orient):
    lanes = slice(orient * 128, (orient + 1) * 128)
    return [sm[TAPS + t : TAPS + t + 1, lanes] for t in range(10)]


def mix(out, value, value_at, sm, mixed):
    taps = [taps_of(sm, orient) for orient in range(2)]

    def line(i, _):
        rows = pl.ds(pl.multiple_of(i * LINE, LINE), LINE)
        for orient in range(2):
            e_v = stencil_line(value, value_at[orient], taps[orient], i, orient, False) + taps[orient][9]
            mixed[rows, orient * 128 : (orient + 1) * 128] = (out[orient, rows, :] + e_v).astype(bf16)
        return 0

    lax.fori_loop(0, GRID, line, 0)


def mixer(x, mixed, wm, sm, middle):
    for rows in chunks():
        middle[rows, :] = x[rows, :].astype(f32) + (dot_nt(mixed[rows, :], wm[...]) + sm[BRANCH : BRANCH + 1])


def hidden(a2, we, sm, s):
    u = dot(a2, we[s]) + sm[HIDDEN + s : HIDDEN + s + 1]
    phi = 0.5 + 0.5 * lax.erf(u * root_half)
    return u, phi


def slope_of(u, phi):
    return phi + u * jnp.exp(-0.5 * u * u) * inverse_root_tau


def second_norm(middle, sm):
    normal, inverse = norm(middle)
    a2 = (normal * sm[GAIN + 1 : GAIN + 2] + sm[SHIFT + 1 : SHIFT + 2]).astype(bf16)
    return normal, inverse, a2


def ff_forward(middle, we, wr, sm, g_out=None, slope_out=None):
    _, _, a2 = second_norm(middle, sm)
    gs = []
    for s in range(4):
        u, phi = hidden(a2, we, sm, s)
        gs.append((u * phi).astype(bf16))
        if g_out is not None:
            g_out[s], slope_out[s] = gs[-1], slope_of(u, phi).astype(bf16)
    return middle + (dot_nt(jnp.concatenate(gs, axis=1), wr[...]) + sm[BRANCH + 1 : BRANCH + 2])


def ff_backward(grad, middle, we, wr, sm, acc_e, acc_r, vec, held=None):
    ey = grad.astype(bf16)
    vec[BRANCH + 1] += column_sum(grad)
    normal, inverse, a2 = second_norm(middle, sm)
    eus = []
    for s in range(4):
        if held is None:
            u, phi = hidden(a2, we, sm, s)
            g, slope = (u * phi).astype(bf16), slope_of(u, phi)
        else:
            g, slope = held(s)
        acc_r[s] += dot_tn(ey, g)
        eu_wide = dot(ey, wr[:, s * 256 : (s + 1) * 256]) * slope.astype(f32)
        vec[HIDDEN + s] += column_sum(eu_wide)
        eu = eu_wide.astype(bf16)
        acc_e[s] += dot_tn(a2, eu)
        eus.append(eu)
    back = None
    for s in range(4):
        term = dot_nt(eus[s], we[s])
        back = term if back is None else back + term
    vec[GAIN + 1] += column_sum(back * normal)
    vec[SHIFT + 1] += column_sum(back)
    return grad + norm_back(back, normal, inverse, sm[GAIN + 1 : GAIN + 2])


def mixer_back(grad, mixed, wm, acc_m, vec, em):
    for rows in chunks():
        here = grad[rows, :]
        eo = here.astype(bf16)
        vec[BRANCH] += column_sum(here)
        acc_m[...] += dot_tn(eo, mixed[rows, :])
        put_blocks(em, rows, dot(eo, wm[...]))
    em[:, ROWS:HELD, :] = jnp.zeros((2, HELD - ROWS, 128), f32)


def mix_back(em, value, value_at, sm, e, e_low, vec):
    taps = [taps_of(sm, orient) for orient in range(2)]

    def line(i, _):
        rows = pl.ds(pl.multiple_of(i * LINE, LINE), LINE)
        for orient in range(2):
            lanes = slice(orient * 128, (orient + 1) * 128)
            base = orient * 384
            eq, ek, ev = [e[orient * 3 + p, rows, :] for p in range(3)]
            ev = ev + stencil_line(em, orient, taps[orient], i, orient, True)
            e_low[rows, base : base + 384] = jnp.concatenate([eq, ek, ev], axis=1).astype(bf16)
            vec[ENTRY, :, lanes] += column_sum(eq)
            vec[ENTRY + 1, :, lanes] += column_sum(ev)
            for t, part in enumerate(stencil_line_taps(value, value_at[orient], em[orient, rows, :], i, orient)):
                vec[TAPS + t, :, lanes] += part
        return 0

    lax.fori_loop(0, GRID, line, 0)


def project_back(grad, x, e_low, wqkv, sm, acc_q, vec, out):
    for rows in chunks():
        normal, inverse = norm(x[rows, :].astype(f32))
        a = (normal * sm[GAIN : GAIN + 1] + sm[SHIFT : SHIFT + 1]).astype(bf16)
        e = e_low[rows, :]
        acc_q[...] += dot_tn(e, a)
        back = dot(e, wqkv[...])
        vec[GAIN] += column_sum(back * normal)
        vec[SHIFT] += column_sum(back)
        out[rows, :] = (grad[rows, :] + norm_back(back, normal, inverse, sm[GAIN : GAIN + 1])).astype(out.dtype)


def attn_pieces(acc_q, acc_m, sums):
    def qkv(s, p, lo, hi):
        at = (s // 2) * 384 + p * 128 + (s % 2) * 64
        return acc_q[at + lo : at + hi]

    return [(64, lambda s, lo, hi, p=p: qkv(s, p, lo, hi)) for p in range(3)] + [
        (64, lambda s, lo, hi: acc_m[64 * s + lo : 64 * s + hi]),
        (32, lambda s, lo, hi: sums[lo:hi]),
    ]


def ff_pieces(acc_e, acc_r):
    return [(256, lambda s, lo, hi: acc_e[s, lo:hi])] + [
        (64, lambda s, lo, hi, c=c: acc_r[c, 64 * s + lo : 64 * s + hi]) for c in range(4)
    ]


def part_rows(rows, planes):
    return -(-rows // (32 * planes)) * 16


def unused(rows):
    return [(rows, lambda s, lo, hi: jnp.zeros((hi - lo, D), f32))]


def write_halves(core, pieces, keep, give):
    parts, _, r, _ = keep.shape

    def write(which, ref):
        for s in range(4):
            at = 0
            for rows, get in pieces + [(2 * parts * r, None)]:
                for part in range(parts):
                    start = (which * parts + part) * r
                    lo, hi = max(at, start), min(at + rows, start + r)
                    if lo < hi:
                        new = jnp.zeros((hi - lo, D), f32) if get is None else get(s, lo - at, hi - at)
                        ref[part, s, lo - start : hi - start] = new.astype(ref.dtype)
                at += rows

    for mine in range(2):

        @pl.when(core == mine)
        def _(mine=mine):
            write(mine, keep)
            write(1 - mine, give)


def clear(*refs):
    for ref in refs:
        ref[...] = jnp.zeros_like(ref)


def first_step(fn):
    pl.when(pl.program_id(0) == 0)(fn)


def last_step(fn):
    pl.when(pl.program_id(0) == pl.num_programs(0) - 1)(fn)


def attn_fwd_kernel(place, x, *refs):
    own, near, far = refs[0:3], refs[3:6], refs[6:9]
    middle, packed, probs, mixed, value, wqkv, wm, sm, qkv, out = refs[9:]

    @first_step
    def _():
        assemble_attn(0, place[0], place[1], own, near, far, wqkv, wm, sm)
        project(x, wqkv, sm, qkv)

    crops = [pl.program_id(0) * STEP_CROPS + i for i in range(STEP_CROPS)]
    attend_crops(place, crops, range(STEP_CROPS), qkv, packed, probs, out)

    @last_step
    def _():
        mix(out, qkv, (2, 5), sm, mixed)
        for orient in range(2):
            value[orient] = qkv[orient * 3 + 2, :ROWS, :].astype(bf16)
        mixer(x, mixed, wm, sm, middle)


def ff_fwd_kernel(place, middle, sm, *refs):
    own, near, far = refs[0:2], refs[2:5], refs[5:8]
    out, we, wr = refs[8:]

    @first_step
    def _():
        assemble_ff(0, place[0], place[1], own, near, far, we, wr)

    out[...] = ff_forward(middle[...], we, wr, sm)


def top_kernel(place, x, cotangent, *refs):
    attn_own, ff_own, near, far = refs[0:3], refs[3:5], refs[5:8], refs[8:11]
    (output, grad_out, keep, give) = refs[11:15]
    (wqkv, wm, sm, we, wr, qkv, out, packed, probs, mixed, middle, g, slope, em, e, e_low,
     acc_e, acc_r, acc_q, acc_m, vec) = refs[15:]

    assemble_attn(1, place[0], place[1], attn_own, near, far, wqkv, wm, sm)
    assemble_ff(HALF_ATTN, place[0], place[1], ff_own, near, far, we, wr)
    clear(acc_e, acc_r, acc_q, acc_m, vec)
    project(x, wqkv, sm, qkv)

    def ahead(i, _):
        crops = [i * STEP_CROPS + j for j in range(STEP_CROPS)]
        attend_crops(place, crops, crops, qkv, packed, probs, out)
        return 0

    lax.fori_loop(0, CROPS // STEP_CROPS, ahead, 0)
    mix(out, qkv, (2, 5), sm, mixed)
    mixer(x, mixed, wm, sm, middle)
    for rows in chunks():
        gs, slopes = {}, {}
        output[rows, :] = ff_forward(middle[rows, :], we, wr, sm, gs, slopes).astype(bf16)
        for s in range(4):
            g[rows, s * 256 : (s + 1) * 256] = gs[s]
            slope[rows, s * 256 : (s + 1) * 256] = slopes[s]
    for rows in chunks():
        held = lambda s: (g[rows, s * 256 : (s + 1) * 256], slope[rows, s * 256 : (s + 1) * 256])
        middle_here = middle[rows, :]
        middle[rows, :] = ff_backward(cotangent[rows, :].astype(f32), middle_here, we, wr, sm, acc_e, acc_r, vec, held)
    mixer_back(middle, mixed, wm, acc_m, vec, em)

    def behind(i, _):
        crops = [i * STEP_CROPS + j for j in range(STEP_CROPS)]
        attend_crops_back(crops, crops, em, packed, probs, e)
        return 0

    lax.fori_loop(0, CROPS // STEP_CROPS, behind, 0)
    mix_back(em, qkv, (2, 5), sm, e, e_low, vec)
    project_back(middle, x, e_low, wqkv, sm, acc_q, vec, grad_out)
    pieces = attn_pieces(acc_q, acc_m, jnp.sum(vec[...], axis=1)) + unused(32) + ff_pieces(acc_e, acc_r)
    write_halves(place[1], pieces, keep, give)


def ff_bwd_kernel(place, grad, middle, we, wr, sm, grad_mid, keep, give, vec, acc_e, acc_r):
    @first_step
    def _():
        clear(acc_e, acc_r, vec)

    grad_mid[...] = ff_backward(grad[...], middle[...], we, wr, sm, acc_e, acc_r, vec)

    @last_step
    def _():
        write_halves(place[1], ff_pieces(acc_e, acc_r), keep, give)


def attn_bwd_kernel(place, grad, x, packed, probs, mixed, value, wqkv, wm, sm, vec_in, patch_grad, keep, give, em, e, e_low, acc_q, acc_m, vec):
    @first_step
    def _():
        clear(acc_q, acc_m)
        vec[...] = vec_in[...]
        mixer_back(grad, mixed, wm, acc_m, vec, em)

    crops = [pl.program_id(0) * STEP_CROPS + i for i in range(STEP_CROPS)]
    attend_crops_back(crops, range(STEP_CROPS), em, packed, probs, e)

    @last_step
    def _():
        mix_back(em, value, (0, 1), sm, e, e_low, vec)
        project_back(grad, x, e_low, wqkv, sm, acc_q, vec, patch_grad)
        write_halves(place[1], attn_pieces(acc_q, acc_m, jnp.sum(vec[...], axis=1)), keep, give)


def whole(shape):
    return pl.BlockSpec(shape, lambda i, *_: (0,) * len(shape))


def rows_of(lanes, rows=CHUNK):
    return pl.BlockSpec((rows, lanes), lambda i, *_: (i, 0))


def crop_spec(*dims):
    return pl.BlockSpec((STEP_CROPS, 4) + dims, lambda i, *_: (i, 0, 0, 0))


def of_layer(layer, *dims):
    return pl.BlockSpec((1,) + dims, lambda i, *_: (layer,) + (0,) * len(dims))


def attn_specs(layer):
    return [of_layer(layer, 192, D), of_layer(layer, 64, D), whole((2, 32, D))]


def ff_specs(layer):
    return [of_layer(layer, D, D), of_layer(layer, 64, FF)]


def half_specs(rows):
    return [whole((rows, D))] * 6


def shape(dims, dtype=bf16):
    return jax.ShapeDtypeStruct(dims, dtype)


def params(micros):
    return dict(
        compiler_params=pltpu.CompilerParams(
            vmem_limit_bytes=58 * 1024 * 1024, dimension_semantics=("arbitrary",)
        ),
        cost_estimate=pl.CostEstimate(flops=int(micros * 1e9), bytes_accessed=1 << 20, transcendentals=0),
    )


v = pltpu.VMEM


def attn_fwd_call(place, x, unit):
    return pl.pallas_call(
        attn_fwd_kernel,
        grid_spec=pltpu.PrefetchScalarGridSpec(
            num_scalar_prefetch=1,
            grid=(CROPS // STEP_CROPS,),
            in_specs=[whole((ROWS, D))] + attn_specs(0) + half_specs(HALF_ATTN),
            out_specs=[whole((ROWS, D)), crop_spec(WIN, 384), crop_spec(WIN, 512), whole((ROWS, D)), whole((2, ROWS, 128)), whole((768, D)), whole((D, D)), whole((32, D))],
            scratch_shapes=[v((6, HELD, 128), f32), v((2, HELD, 128), f32)],
        ),
        out_shape=[shape((ROWS, D), f32), shape((CROPS, 4, WIN, 384)), shape((CROPS, 4, WIN, 512)), shape((ROWS, D)), shape((2, ROWS, 128)), shape((768, D)), shape((D, D)), shape((32, D), f32)],
        name="attn_fwd",
        **params(10),
    )(place, x, *unit)


def ff_fwd_call(place, middle, sm, unit):
    return pl.pallas_call(
        ff_fwd_kernel,
        grid_spec=pltpu.PrefetchScalarGridSpec(
            num_scalar_prefetch=1,
            grid=(ROWS // CHUNK,),
            in_specs=[rows_of(D), whole((32, D))] + ff_specs(0) + half_specs(HALF_FF),
            out_specs=[rows_of(D), whole((4, D, D)), whole((D, FF))],
        ),
        out_shape=[shape((ROWS, D), f32), shape((4, D, D)), shape((D, FF))],
        name="ff_fwd",
        **params(6),
    )(place, middle, sm, *unit)


def top_call(place, x, cotangent, weights, parts, r):
    return pl.pallas_call(
        top_kernel,
        grid_spec=pltpu.PrefetchScalarGridSpec(
            num_scalar_prefetch=1,
            grid=(1,),
            in_specs=[whole((ROWS, D)), whole((ROWS, D))] + attn_specs(1) + ff_specs(1) + half_specs(HALF_ATTN + HALF_FF),
            out_specs=[whole((ROWS, D)), whole((ROWS, D))] + [whole((parts, 4, r, D))] * 2,
            scratch_shapes=[
                v((768, D), bf16), v((D, D), bf16), v((32, D), f32), v((4, D, D), bf16), v((D, FF), bf16),
                v((6, HELD, 128), f32), v((2, HELD, 128), f32), v((CROPS, 4, WIN, 384), bf16), v((CROPS, 4, WIN, 512), bf16),
                v((ROWS, D), bf16), v((ROWS, D), f32), v((ROWS, FF), bf16), v((ROWS, FF), bf16),
                v((2, HELD, 128), f32), v((6, HELD, 128), f32), v((ROWS, 768), bf16),
                v((4, D, D), f32), v((4, D, D), f32), v((768, D), f32), v((D, D), f32), v((32, CROPS, D), f32),
            ],
        ),
        out_shape=[shape((ROWS, D)), shape((ROWS, D), f32)] + [shape((parts, 4, r, D))] * 2,
        name="top_block",
        **params(30),
    )(place, x, cotangent, *weights)


def ff_bwd_call(place, grad, middle, we, wr, sm, parts, r):
    return pl.pallas_call(
        ff_bwd_kernel,
        grid_spec=pltpu.PrefetchScalarGridSpec(
            num_scalar_prefetch=1,
            grid=(ROWS // CHUNK,),
            in_specs=[rows_of(D), rows_of(D), whole((4, D, D)), whole((D, FF)), whole((32, D))],
            out_specs=[rows_of(D)] + [whole((parts, 4, r, D))] * 2 + [whole((32, CROPS, D))],
            scratch_shapes=[v((4, D, D), f32), v((4, D, D), f32)],
        ),
        out_shape=[shape((ROWS, D), f32)] + [shape((parts, 4, r, D))] * 2 + [shape((32, CROPS, D), f32)],
        name="ff_bwd",
        **params(10),
    )(place, grad, middle, we, wr, sm)


def attn_bwd_call(place, grad, x, packed, probs, mixed, value, wqkv, wm, sm, vec):
    return pl.pallas_call(
        attn_bwd_kernel,
        grid_spec=pltpu.PrefetchScalarGridSpec(
            num_scalar_prefetch=1,
            grid=(CROPS // STEP_CROPS,),
            in_specs=[whole((ROWS, D)), whole((ROWS, D)), crop_spec(WIN, 384), crop_spec(WIN, 512), whole((ROWS, D)), whole((2, ROWS, 128)), whole((768, D)), whole((D, D)), whole((32, D)), whole((32, CROPS, D))],
            out_specs=[whole((ROWS, D))] + [whole((1, 4, LOW_ROWS // 2, D))] * 2,
            scratch_shapes=[v((2, HELD, 128), f32), v((6, HELD, 128), f32), v((ROWS, 768), bf16), v((768, D), f32), v((D, D), f32), v((32, CROPS, D), f32)],
        ),
        out_shape=[shape((ROWS, D))] + [shape((1, 4, LOW_ROWS // 2, D))] * 2,
        name="attn_bwd",
        **params(16),
    )(place, grad, x, packed, probs, mixed, value, wqkv, wm, sm, vec)


def to_rows(x):
    return jnp.transpose(x, (1, 2, 0, 3)).reshape(ROWS, D)


def from_rows(x):
    return jnp.transpose(x.reshape(GRID, GRID, CROPS, D), (2, 0, 1, 3))


def pack_kernel(place, qkv, mixer_t, gain, shift, entry, taps, branch, hidden_bias, expand, reduce_t, half_a, half_f, half_1, vec):
    me, core = place[0], place[1]
    lane = lax.broadcasted_iota(jnp.int32, (18, D), 1)
    row = lax.broadcasted_iota(jnp.int32, (14, D), 0)
    for layer, attn, ff, first in ((0, half_a, half_f, 0), (1, half_1, half_1, HALF_ATTN)):
        rows = jnp.concatenate(
            [ref[layer].astype(f32) for ref in (gain, shift, entry)] + [taps[:, layer].astype(f32), branch[layer].astype(f32)], axis=0
        )
        vectors = jnp.where(lane // 64 == me, jnp.concatenate([rows] * 4, axis=1), 0.0)
        hidden_rows = jnp.where(row == me, hidden_bias[layer : layer + 1].astype(f32), 0.0)
        vec[layer] = jnp.concatenate([vectors, hidden_rows], axis=0).astype(bf16)
        attn[0:96] = qkv[layer, pl.ds(pl.multiple_of(96 * core, 32), 96)]
        attn[96:128] = mixer_t[layer, pl.ds(pl.multiple_of(32 * core, 32), 32)]
        attn[128:144] = vec[layer, pl.ds(pl.multiple_of(16 * core, 16), 16)]
        ff[first : first + 128] = expand[layer, pl.ds(pl.multiple_of(128 * core, 128), 128)]
        for c in range(4):
            at = first + 128 + 32 * c
            ff[at : at + 32] = reduce_t[layer, pl.ds(pl.multiple_of(32 * core, 32), 32), c * 256 : (c + 1) * 256]


def local_call(kernel, name, place, arrays, outs, scratch=()):
    return pl.pallas_call(
        kernel,
        grid_spec=pltpu.PrefetchScalarGridSpec(
            num_scalar_prefetch=1,
            grid=(1,),
            in_specs=[whole(x.shape) for x in arrays],
            out_specs=[whole(dims) for dims, _ in outs],
            scratch_shapes=list(scratch),
        ),
        out_shape=[shape(dims, dtype) for dims, dtype in outs],
        name=name,
        **params(1),
    )(place, *arrays)


def turn_mp(x, k):
    n = lax.axis_size("mp")
    return lax.ppermute(x, "mp", [(i, (i + k) % n) for i in range(n)])


def swap_dp(x, bits):
    n = lax.axis_size("dp")
    return lax.ppermute(x, "dp", [(i, i ^ bits) for i in range(n)])


def turn_all(x):
    return [turn_mp(x, k) for k in (1, 2, 3)]


def swap_core(xs):
    return [swap_dp(x, 1) for x in xs]


def pick(x, at):
    return lax.dynamic_index_in_dim(x, at, 0, keepdims=False)


def add_up(xs):
    total = xs[0].astype(f32)
    for x in xs[1:]:
        total = total + x.astype(f32)
    return total


def to_planes(keep, got, at):
    total = add_up([keep, got]).astype(bf16)
    return [pick(total, at ^ b) for b in range(keep.shape[0])]


def swap_planes(parts):
    return [parts[0]] + [swap_dp(part, 2 * b) for b, part in enumerate(parts) if b]


def to_shards(xs, me):
    total = add_up(xs)
    low = total.astype(bf16)
    return [pick(total, me)] + [pick(low, (me + k) % 4) for k in (1, 2, 3)]


def turn_shards(parts):
    return [parts[0]] + [turn_mp(part, k) for k, part in enumerate(parts) if k]


def unpack_kernel(planes, cut_f, cut_t, place, *refs):
    mine, other = refs[:planes], refs[planes : 2 * planes]
    packed, mixer_g, expand, reduce_g, gain, shift, entry, taps, branch, hidden_g, held = refs[2 * planes :]
    me, core = place[0], place[1]
    r_f, r_t = cut_t - cut_f, mine[0].shape[0] - cut_t
    start_t = cut_f + planes * r_f
    for which, parts in ((core, mine), (1 - core, other)):
        total = parts[0][:cut_f].astype(f32)
        for part in parts[1:]:
            total = total + part[:cut_f].astype(f32)
        held[which, :cut_f] = total
        for b in range(planes):
            at = place[2] ^ b
            held[which, pl.ds(pl.multiple_of(cut_f + at * r_f, 16), r_f)] = parts[b][cut_f:cut_t].astype(f32)
            held[which, pl.ds(pl.multiple_of(start_t + at * r_t, 16), r_t)] = parts[b][cut_t:].astype(f32)

    def rows(which, lo, hi):
        start, half = which
        out = []
        for c in range(2):
            a, b = max(lo, c * half), min(hi, (c + 1) * half)
            if a < b:
                out.append(held[c, start + a - c * half : start + b - c * half])
        return out[0] if len(out) == 1 else jnp.concatenate(out, axis=0)

    low_a, low_f, top = (0, cut_f), (cut_f, planes * r_f), (start_t, planes * r_t)
    for layer, attn, ff, ff_at in ((0, low_a, low_f, 0), (1, top, top, 320)):
        packed[layer] = rows(attn, 0, 192)
        mixer_g[layer] = rows(attn, 192, 256)
        expand[layer] = rows(ff, ff_at, ff_at + 256)
        for c in range(4):
            at = ff_at + 256 + 64 * c
            reduce_g[layer, :, c * 256 : (c + 1) * 256] = rows(ff, at, at + 64)
        vectors = rows(attn, 256, 288)
        mine_lanes = vectors[:, :64]
        for s in range(1, 4):
            mine_lanes = jnp.where(me == s, vectors[:, 64 * s : 64 * (s + 1)], mine_lanes)
        gain[layer] = mine_lanes[GAIN : GAIN + 2]
        shift[layer] = mine_lanes[SHIFT : SHIFT + 2]
        entry[layer] = mine_lanes[ENTRY : ENTRY + 2]
        branch[layer] = mine_lanes[BRANCH : BRANCH + 2]
        for t in range(10):
            taps[t, layer : layer + 1] = mine_lanes[TAPS + t : TAPS + t + 1]
        row = vectors[HIDDEN : HIDDEN + 1]
        for s in range(1, 4):
            row = jnp.where(me == s, vectors[HIDDEN + s : HIDDEN + s + 1], row)
        hidden_g[layer : layer + 1] = row


def body(patches, validity, norm_gain, norm_shift, qkv_weight, entry_bias, stencil, mixer_weight, branch_bias, expand_weight, hidden_bias, reduce_weight, cotangent):
    dp = lax.axis_size("dp")
    planes = dp // 2
    me, at_dp = lax.axis_index("mp"), lax.axis_index("dp")
    heights = jnp.sum(validity[:, :, 0], axis=1)
    widths = jnp.sum(validity[:, 0, :], axis=1)
    place = jnp.stack([me, at_dp % 2, at_dp // 2]).astype(jnp.int32)
    sizes = jnp.concatenate([jnp.stack([me, at_dp % 2]), jnp.stack([heights, widths], axis=1).reshape(-1)]).astype(jnp.int32)

    qkv_t = jnp.transpose(qkv_weight, (0, 2, 3, 1)).reshape(2, 192, D)
    mixer_t = jnp.transpose(mixer_weight, (0, 2, 1))
    reduce_t = jnp.transpose(reduce_weight, (0, 2, 1))
    vectors = (norm_gain, norm_shift, entry_bias, jnp.transpose(stencil, (1, 0, 2)), branch_bias, hidden_bias)

    arrays = [qkv_t, mixer_t, norm_gain, norm_shift, entry_bias, jnp.transpose(stencil, (1, 0, 2)), branch_bias, hidden_bias, expand_weight, reduce_t]
    outs = [(HALF_ATTN, D), (HALF_FF, D), (HALF_ATTN + HALF_FF, D), (2, 32, D)]
    half_a0, half_f0, half_1, vec = local_call(pack_kernel, "pack", place, arrays, [(dims, bf16) for dims in outs])
    attn_own, ff_own = [qkv_t, mixer_t, vec], [expand_weight, reduce_t]

    near_a0 = turn_all(half_a0)
    near_f0 = turn_all(half_f0)
    near_1 = turn_all(half_1)
    far_a0 = swap_core(near_a0)
    x, top_grad = to_rows(patches), to_rows(cotangent)
    middle, packed, probs, mixed, value, wqkv, wm, sm = attn_fwd_call(sizes, x, attn_own + near_a0 + far_a0)
    near_f0, middle = lax.optimization_barrier((near_f0, middle))
    far_f0 = swap_core(near_f0)
    state, we, wr = ff_fwd_call(sizes, middle, sm, ff_own + near_f0 + far_f0)
    near_1, state = lax.optimization_barrier((near_1, state))
    far_1 = swap_core(near_1)
    r_t, r_f = part_rows(TOP_ROWS, planes), part_rows(FF_ROWS, planes)
    output, grad, keep_1, give_1 = top_call(sizes, state, top_grad, attn_own + ff_own + near_1 + far_1, planes, r_t)

    got_1 = swap_dp(give_1, 1)
    grad_mid, keep_f, give_f, vec = ff_bwd_call(place, grad, middle, we, wr, sm, planes, r_f)
    got_1, grad_mid, keep_f, give_f = lax.optimization_barrier((got_1, grad_mid, keep_f, give_f))

    got_f = swap_dp(give_f, 1)
    parts_1 = to_planes(keep_1, got_1, place[2])
    grad_mid, parts_1 = lax.optimization_barrier((grad_mid, parts_1))
    planes_1 = swap_planes(parts_1)
    patch_grad, keep_a, give_a = attn_bwd_call(place, grad_mid, x, packed, probs, mixed, value, wqkv, wm, sm, vec)
    planes_1, got_f, keep_a, give_a = lax.optimization_barrier((planes_1, got_f, keep_a, give_a))

    got_a = swap_dp(give_a, 1)
    planes_f = swap_planes(to_planes(keep_f, got_f, place[2]))
    mp_1 = turn_shards(to_shards(planes_1, me))
    mp_a = turn_shards(to_shards([keep_a[0], got_a[0]], me))
    mp_f = turn_shards(to_shards(planes_f, me))
    share = jnp.concatenate([add_up(mp_a), add_up(mp_f), add_up(mp_1)], axis=0).astype(bf16)
    mine = swap_planes([share] * planes)
    other = swap_core(mine)
    outs = [(2, 192, D), (2, 64, D), (2, D, D), (2, 64, FF), (2, 2, 64), (2, 2, 64), (2, 2, 64), (10, 2, 64), (2, 2, 64), (2, D)]
    cut_f = LOW_ROWS // 2
    cut_t = cut_f + r_f
    held = v((2, cut_f + planes * (r_f + r_t), D), f32)
    packed_g, mixer_g, expand_g, reduce_g, gain_g, shift_g, entry_g, taps_g, branch_g, hidden_g = local_call(
        functools.partial(unpack_kernel, planes, cut_f, cut_t), "unpack", place, mine + other, [(dims, f32) for dims in outs], [held]
    )
    return (
        from_rows(output), from_rows(patch_grad), gain_g, shift_g,
        jnp.transpose(packed_g.reshape(2, 3, 64, D), (0, 3, 1, 2)), entry_g, jnp.transpose(taps_g, (1, 0, 2)),
        jnp.transpose(mixer_g, (0, 2, 1)), branch_g, expand_g, hidden_g, jnp.transpose(reduce_g, (0, 2, 1)),
    )


def solution(mesh):
    crops = P(("dp", "mp"), None, None, None)
    lanes = P(None, None, "mp")
    deep = P(None, None, None, "mp")
    return jax.shard_map(
        body,
        mesh=mesh,
        in_specs=(crops, P(("dp", "mp"), None, None), lanes, lanes, deep, lanes, lanes, lanes, lanes, lanes, P(None, "mp"), lanes, crops),
        out_specs=(crops, crops, lanes, lanes, deep, lanes, lanes, lanes, lanes, lanes, P(None, "mp"), lanes),
        check_vma=False,
    )
```

```python
import functools

import jax
import jax.numpy as jnp
from jax import lax
from jax.experimental import pallas as pl
from jax.experimental.pallas import tpu as pltpu
from jax.sharding import PartitionSpec as P

GRID = 14
STRIPE = 7
CELLS = GRID * GRID
CROPS = 8
ROWS = CELLS * CROPS
LINE = GRID * CROPS
HELD = ROWS + 112
WIN = 112
HALF_HEADS = 4
HEAD = 32
D = 256
FF = 1024
STEP_CROPS = 2
CHUNK = 784

norm_eps = 1e-05
masked_score = -1e30
root_half = 0.7071067811865476
inverse_root_tau = 0.3989422804014327
log2_e = 1.4426950408889634
factor = HEAD**-0.5

f32 = jnp.float32
bf16 = jnp.bfloat16

HALF_ATTN = 144
HALF_FF = 256
FF_ROWS = 512
UNIT = 800
LOW_ROWS = 288
GAIN, SHIFT, ENTRY, TAPS, BRANCH, HIDDEN = 0, 2, 4, 6, 16, 18


def dot(a, b):
    return lax.dot_general(a, b, (((1,), (0,)), ((), ())), preferred_element_type=f32)


def dot_nt(a, b):
    return lax.dot_general(a, b, (((1,), (1,)), ((), ())), preferred_element_type=f32)


def dot_tn(a, b):
    return lax.dot_general(a, b, (((0,), (0,)), ((), ())), preferred_element_type=f32)


def norm(x):
    center = x - jnp.mean(x, axis=-1, keepdims=True)
    spread = jnp.mean(center * center, axis=-1, keepdims=True)
    inverse = lax.rsqrt(spread + norm_eps)
    return center * inverse, inverse


def norm_back(grad, normal, inverse, gain):
    scaled = grad * gain
    return inverse * (
        scaled
        - jnp.mean(scaled, axis=-1, keepdims=True)
        - normal * jnp.mean(scaled * normal, axis=-1, keepdims=True)
    )


def column_sum(x):
    return jnp.sum(x.reshape(x.shape[0] // CROPS, CROPS, x.shape[1]), axis=0)


def window_row_inside(orient):
    row = lax.broadcasted_iota(jnp.int32, (WIN, 128), 0)
    return row < 98 if orient == 0 else row % 8 < STRIPE


def key_bias(orient, window, height, width):
    row = lax.broadcasted_iota(jnp.int32, (WIN, 128), 0)
    if orient == 0:
        line, column = row // GRID + window * STRIPE, row % GRID
    else:
        line, column = row // 8, row % 8 + window * STRIPE
    valid = window_row_inside(orient) & (line < height) & (column < width)
    return jnp.where(valid, 0.0, masked_score)


def load_window(ref, block, crop, orient, window):
    if orient == 0:
        return ref[block, pl.ds(98 * CROPS * window + crop, WIN, stride=CROPS), :]
    parts = [
        ref[block, pl.ds((line * GRID + window * STRIPE) * CROPS + crop, 8, stride=CROPS), :]
        for line in range(GRID)
    ]
    return jnp.concatenate(parts, axis=0)


def store_window(ref, block, crop, orient, window, x):
    if orient == 0:
        ref[block, pl.ds(98 * CROPS * window + crop, 98, stride=CROPS), :] = x[:98]
        return
    for line in range(GRID):
        at = (line * GRID + window * STRIPE) * CROPS + crop
        ref[block, pl.ds(at, STRIPE, stride=CROPS), :] = x[line * 8 : line * 8 + STRIPE]


def heads_apart(x, inside=None):
    lane = lax.broadcasted_iota(jnp.int32, (WIN, 128), 1) // HEAD
    rest = jnp.zeros((128 - WIN, 128), bf16)
    blocks = []
    for head in range(HALF_HEADS):
        keep = lane == head
        if inside is not None:
            keep = keep & inside
        blocks.append(jnp.where(keep, x, 0.0).astype(bf16))
        blocks.append(rest)
    return jnp.concatenate(blocks, axis=0)


def by_head(flat_turned, probs):
    parts = []
    for head in range(HALF_HEADS):
        parts.append(
            dot(flat_turned[head * HEAD : (head + 1) * HEAD], probs[:, head * 128 : (head + 1) * 128])
        )
    return jnp.concatenate(parts, axis=0)


def attend(queries, keys, values, biases):
    apart = [heads_apart(x) for x in queries]
    value_turned = [x.T.astype(bf16) for x in values]
    scores = [dot_nt(k.astype(bf16), q) for k, q in zip(keys, apart)]
    scores = [s * (factor * log2_e) + jnp.concatenate([b] * HALF_HEADS, axis=1) for s, b in zip(scores, biases)]
    peaks = [jnp.max(s, axis=0, keepdims=True) for s in scores]
    raised = [jnp.exp2(s - p) for s, p in zip(scores, peaks)]
    shares = [1.0 / jnp.sum(r, axis=0, keepdims=True) for r in raised]
    probs = [(r * s).astype(bf16) for r, s in zip(raised, shares)]
    outs = [by_head(v, p) for v, p in zip(value_turned, probs)]
    return [o.T[:WIN] for o in outs], probs


def attend_back(grads, queries, keys, values, probs, insides):
    grad_apart = [heads_apart(x, i) for x, i in zip(grads, insides)]
    grad_probs = [dot_nt(v, g) for v, g in zip(values, grad_apart)]
    key_turned = [x.astype(f32).T.astype(bf16) for x in keys]
    grad_value = [dot(p, g) for p, g in zip(probs, grad_apart)]
    wide = [p.astype(f32) for p in probs]
    inner = [jnp.sum(g * w, axis=0, keepdims=True) for g, w in zip(grad_probs, wide)]
    grad_scores = [(w * (g - i)).astype(bf16) for w, g, i in zip(wide, grad_probs, inner)]
    apart = [heads_apart(x) for x in queries]
    grad_key = [dot(s, q) * factor for s, q in zip(grad_scores, apart)]
    grad_query = [by_head(k, s) for k, s in zip(key_turned, grad_scores)]
    grad_query = [g.T[:WIN] * factor for g in grad_query]
    return grad_query, grad_key, grad_value


WINDOWS = [(orient, window) for orient in range(2) for window in range(2)]


def steps_along(x, orient):
    zero = jnp.zeros((CROPS, x.shape[1]), x.dtype)
    if orient == 0:
        return {-1: jnp.concatenate([zero, x[:-CROPS]], axis=0), 0: x, 1: jnp.concatenate([x[CROPS:], zero], axis=0)}
    half = LINE // 2
    left, right = x[:half], x[half:]
    return {
        -1: jnp.concatenate([zero, left[:-CROPS], zero, right[:-CROPS]], axis=0),
        0: x,
        1: jnp.concatenate([left[CROPS:], zero, right[CROPS:], zero], axis=0),
    }


def line_reaches(line, step, orient):
    if step == 0:
        return None
    stops = (GRID, STRIPE) if orient == 0 else (GRID,)
    edges = [(stop - 1) if step == 1 else (stop % GRID) for stop in stops]
    ok = line != edges[0]
    for edge in edges[1:]:
        ok = ok & (line != edge)
    return jnp.where(ok, 1.0, 0.0).astype(f32)


def line_at(ref, block, line):
    held = jnp.clip(line, 0, GRID - 1)
    return ref[block, pl.ds(pl.multiple_of(held * LINE, LINE), LINE), :]


def stencil_line(ref, block, taps, line, orient, back):
    total = None
    for step in (-1, 0, 1):
        moved = steps_along(line_at(ref, block, line + (-step if back else step)).astype(f32), orient)
        reach = line_reaches(line, -step if back else step, orient)
        for side in (-1, 0, 1):
            tap = taps[3 * (step + 1) + side + 1]
            if reach is not None:
                tap = tap * reach
            term = moved[-side if back else side] * tap
            total = term if total is None else total + term
    return total


def stencil_line_taps(ref, block, grad, line, orient):
    sums = []
    for step in (-1, 0, 1):
        moved = steps_along(line_at(ref, block, line + step).astype(f32), orient)
        reach = line_reaches(line, step, orient)
        for side in (-1, 0, 1):
            part = column_sum(grad * moved[side])
            sums.append(part if reach is None else part * reach)
    sums.append(column_sum(grad))
    return sums


def assemble_attn(layer, me, core, own, near, far, wqkv, wm, sm):
    qkv, mixer_t, vec = own

    def put(shard, blocks, at, mixer_rows, mixer_at):
        orient, part = lax.div(shard, 2), lax.rem(shard, 2)
        for i, block in enumerate(blocks):
            j = at + i
            row = orient * 384 + lax.div(j, 2) * 128 + part * 64 + lax.rem(j, 2) * 32
            wqkv[pl.ds(pl.multiple_of(row, 32), 32), :] = block
        wm[pl.ds(pl.multiple_of(shard * 64 + mixer_at, 32), mixer_rows.shape[0]), :] = mixer_rows

    put(me, [qkv[0, 32 * i : 32 * (i + 1)] for i in range(6)], jnp.int32(0), mixer_t[0], 0)
    sm[...] = vec[layer].astype(f32)
    for halves, which in ((near, core), (far, 1 - core)):
        for k, half in enumerate(halves, 1):
            shard = lax.rem(me + 4 - k, 4)
            put(shard, [half[32 * i : 32 * (i + 1)] for i in range(3)], 3 * which, half[96:128], 32 * which)
            sm[pl.ds(pl.multiple_of(16 * which, 16), 16), :] += half[128:144].astype(f32)


def assemble_ff(first, me, core, own, near, far, we, wr):
    expand, reduce_t = own
    we[me] = expand[0]
    wr[pl.ds(pl.multiple_of(me * 64, 64), 64), :] = reduce_t[0]
    for halves, which in ((near, core), (far, 1 - core)):
        for k, half in enumerate(halves, 1):
            shard = lax.rem(me + 4 - k, 4)
            we[shard, pl.ds(pl.multiple_of(128 * which, 128), 128), :] = half[first : first + 128]
            row = pl.multiple_of(shard * 64 + 32 * which, 32)
            for c in range(4):
                at = first + 128 + 32 * c
                wr[pl.ds(row, 32), c * 256 : (c + 1) * 256] = half[at : at + 32]


def assemble_top(me, attn_own, ff_own, rest, wqkv, wm, sm, we, wr):
    qkv, mixer_t, vec = attn_own
    expand, reduce_t = ff_own

    def put(shard, row, value):
        orient, part = lax.div(shard, 2), lax.rem(shard, 2)
        n = value.shape[0]
        if row < 192:
            at = orient * 384 + row // 64 * 128 + part * 64 + row % 64
            wqkv[pl.ds(pl.multiple_of(at, 16), n), :] = value
        elif row < 256:
            wm[pl.ds(pl.multiple_of(shard * 64 + row - 192, 16), n), :] = value
        elif row < 288:
            sm[row - 256 : row - 256 + n, :] += value.astype(f32)
        elif row < 544:
            we[shard, row - 288 : row - 288 + n, :] = value
        else:
            c, at = divmod(row - 544, 64)
            wr[pl.ds(pl.multiple_of(shard * 64 + at, 16), n), c * 256 : (c + 1) * 256] = value

    for p in range(3):
        put(me, 64 * p, qkv[0, 64 * p : 64 * (p + 1)])
    put(me, 192, mixer_t[0])
    sm[...] = vec[1].astype(f32)
    put(me, 288, expand[0])
    for c in range(4):
        put(me, 544 + 64 * c, reduce_t[0, :, c * 256 : (c + 1) * 256])
    dp, _, r, _ = rest.shape
    edges = list(range(0, 257, 64)) + [288] + [544 + 64 * c for c in range(5)]
    for k in range(3):
        shard = lax.rem(me + 3 - k, 4)
        for d in range(dp):
            for lo, hi in zip(edges[:-1], edges[1:]):
                a, b = max(lo, d * r), min(hi, (d + 1) * r)
                if a < b:
                    put(shard, a, rest[d, k, a - d * r : b - d * r])


def chunks():
    return [slice(at, at + CHUNK) for at in range(0, ROWS, CHUNK)]


def put_blocks(ref, rows, x):
    for block in range(x.shape[1] // 128):
        ref[block, rows, :] = x[:, block * 128 : (block + 1) * 128]


def project(x, wqkv, sm, qkv):
    zero = jnp.zeros((1, 128), f32)
    query_bias, value_bias = sm[ENTRY : ENTRY + 1], sm[ENTRY + 1 : ENTRY + 2]
    bias = jnp.concatenate(
        [query_bias[:, :128], zero, value_bias[:, :128], query_bias[:, 128:], zero, value_bias[:, 128:]], axis=1
    )
    for rows in chunks():
        normal, _ = norm(x[rows, :].astype(f32))
        a = (normal * sm[GAIN : GAIN + 1] + sm[SHIFT : SHIFT + 1]).astype(bf16)
        put_blocks(qkv, rows, dot_nt(a, wqkv[...]) + bias)
    qkv[:, ROWS:HELD, :] = jnp.zeros((6, HELD - ROWS, 128), f32)


def attend_crops(place, crops, slots, qkv, packed, probs_ref, out):
    at, lists = [], ([], [], [], [])
    for crop, slot in zip(crops, slots):
        height, width = place[2 + 2 * crop], place[3 + 2 * crop]
        for n, (orient, window) in enumerate(WINDOWS):
            three = [load_window(qkv, orient * 3 + p, crop, orient, window) for p in range(3)]
            packed[slot, n] = jnp.concatenate(three, axis=1).astype(bf16)
            entries = (*three, key_bias(orient, window, height, width))
            for held, new in zip(lists, entries):
                held.append(new)
            at.append((crop, slot, n, orient, window))
    outs, probs = attend(*lists)
    for (crop, slot, n, orient, window), o, p in zip(at, outs, probs):
        probs_ref[slot, n] = p
        store_window(out, orient, crop, orient, window, o)


def attend_crops_back(crops, slots, em, packed, probs_ref, e):
    at, lists = [], ([], [], [], [], [], [])
    for crop, slot in zip(crops, slots):
        for n, (orient, window) in enumerate(WINDOWS):
            grad = load_window(em, orient, crop, orient, window)
            entries = (
                grad, packed[slot, n, :, :128], packed[slot, n, :, 128:256], packed[slot, n, :, 256:],
                probs_ref[slot, n], window_row_inside(orient),
            )
            for held, new in zip(lists, entries):
                held.append(new)
            at.append((crop, orient, window))
    for (crop, orient, window), dq, dk, dv in zip(at, *attend_back(*lists)):
        for p, part in enumerate((dq, dk, dv)):
            store_window(e, orient * 3 + p, crop, orient, window, part)


def taps_of(sm, orient):
    lanes = slice(orient * 128, (orient + 1) * 128)
    return [sm[TAPS + t : TAPS + t + 1, lanes] for t in range(10)]


def mix(out, value, value_at, sm, mixed):
    taps = [taps_of(sm, orient) for orient in range(2)]

    def line(i, _):
        rows = pl.ds(pl.multiple_of(i * LINE, LINE), LINE)
        for orient in range(2):
            e_v = stencil_line(value, value_at[orient], taps[orient], i, orient, False) + taps[orient][9]
            mixed[rows, orient * 128 : (orient + 1) * 128] = (out[orient, rows, :] + e_v).astype(bf16)
        return 0

    lax.fori_loop(0, GRID, line, 0)


def mixer(x, mixed, wm, sm, middle):
    for rows in chunks():
        middle[rows, :] = x[rows, :].astype(f32) + (dot_nt(mixed[rows, :], wm[...]) + sm[BRANCH : BRANCH + 1])


def hidden(a2, we, sm, s):
    u = dot(a2, we[s]) + sm[HIDDEN + s : HIDDEN + s + 1]
    phi = 0.5 + 0.5 * lax.erf(u * root_half)
    return u, phi


def slope_of(u, phi):
    return phi + u * jnp.exp(-0.5 * u * u) * inverse_root_tau


def second_norm(middle, sm):
    normal, inverse = norm(middle)
    a2 = (normal * sm[GAIN + 1 : GAIN + 2] + sm[SHIFT + 1 : SHIFT + 2]).astype(bf16)
    return normal, inverse, a2


def ff_forward(middle, we, wr, sm, g_out=None, slope_out=None):
    _, _, a2 = second_norm(middle, sm)
    gs = []
    for s in range(4):
        u, phi = hidden(a2, we, sm, s)
        gs.append((u * phi).astype(bf16))
        if g_out is not None:
            g_out[s], slope_out[s] = gs[-1], slope_of(u, phi).astype(bf16)
    return middle + (dot_nt(jnp.concatenate(gs, axis=1), wr[...]) + sm[BRANCH + 1 : BRANCH + 2])


def ff_backward(grad, middle, we, wr, sm, acc_e, acc_r, vec, held=None):
    ey = grad.astype(bf16)
    vec[BRANCH + 1] += column_sum(grad)
    normal, inverse, a2 = second_norm(middle, sm)
    eus = []
    for s in range(4):
        if held is None:
            u, phi = hidden(a2, we, sm, s)
            g, slope = (u * phi).astype(bf16), slope_of(u, phi)
        else:
            g, slope = held(s)
        acc_r[s] += dot_tn(ey, g)
        eu_wide = dot(ey, wr[:, s * 256 : (s + 1) * 256]) * slope.astype(f32)
        vec[HIDDEN + s] += column_sum(eu_wide)
        eu = eu_wide.astype(bf16)
        acc_e[s] += dot_tn(a2, eu)
        eus.append(eu)
    back = None
    for s in range(4):
        term = dot_nt(eus[s], we[s])
        back = term if back is None else back + term
    vec[GAIN + 1] += column_sum(back * normal)
    vec[SHIFT + 1] += column_sum(back)
    return grad + norm_back(back, normal, inverse, sm[GAIN + 1 : GAIN + 2])


def mixer_back(grad, mixed, wm, acc_m, vec, em):
    for rows in chunks():
        here = grad[rows, :]
        eo = here.astype(bf16)
        vec[BRANCH] += column_sum(here)
        acc_m[...] += dot_tn(eo, mixed[rows, :])
        put_blocks(em, rows, dot(eo, wm[...]))
    em[:, ROWS:HELD, :] = jnp.zeros((2, HELD - ROWS, 128), f32)


def mix_back(em, value, value_at, sm, e, e_low, vec):
    taps = [taps_of(sm, orient) for orient in range(2)]

    def line(i, _):
        rows = pl.ds(pl.multiple_of(i * LINE, LINE), LINE)
        for orient in range(2):
            lanes = slice(orient * 128, (orient + 1) * 128)
            base = orient * 384
            eq, ek, ev = [e[orient * 3 + p, rows, :] for p in range(3)]
            ev = ev + stencil_line(em, orient, taps[orient], i, orient, True)
            e_low[rows, base : base + 384] = jnp.concatenate([eq, ek, ev], axis=1).astype(bf16)
            vec[ENTRY, :, lanes] += column_sum(eq)
            vec[ENTRY + 1, :, lanes] += column_sum(ev)
            for t, part in enumerate(stencil_line_taps(value, value_at[orient], em[orient, rows, :], i, orient)):
                vec[TAPS + t, :, lanes] += part
        return 0

    lax.fori_loop(0, GRID, line, 0)


def project_back(grad, x, e_low, wqkv, sm, acc_q, vec, out):
    for rows in chunks():
        normal, inverse = norm(x[rows, :].astype(f32))
        a = (normal * sm[GAIN : GAIN + 1] + sm[SHIFT : SHIFT + 1]).astype(bf16)
        e = e_low[rows, :]
        acc_q[...] += dot_tn(e, a)
        back = dot(e, wqkv[...])
        vec[GAIN] += column_sum(back * normal)
        vec[SHIFT] += column_sum(back)
        out[rows, :] = (grad[rows, :] + norm_back(back, normal, inverse, sm[GAIN : GAIN + 1])).astype(out.dtype)


def attn_pieces(acc_q, acc_m, sums):
    def qkv(s, p, lo, hi):
        at = (s // 2) * 384 + p * 128 + (s % 2) * 64
        return acc_q[at + lo : at + hi]

    return [(64, lambda s, lo, hi, p=p: qkv(s, p, lo, hi)) for p in range(3)] + [
        (64, lambda s, lo, hi: acc_m[64 * s + lo : 64 * s + hi]),
        (32, lambda s, lo, hi: sums[lo:hi]),
    ]


def ff_pieces(acc_e, acc_r):
    return [(256, lambda s, lo, hi: acc_e[s, lo:hi])] + [
        (64, lambda s, lo, hi, c=c: acc_r[c, 64 * s + lo : 64 * s + hi]) for c in range(4)
    ]


def part_rows(rows, parts):
    return -(-rows // (16 * parts)) * 16


def write_parts(pieces, first, ref):
    parts, _, r, _ = ref.shape
    for s in range(4):
        at = -first
        for rows, get in pieces + [(first + parts * r, None)]:
            for part in range(parts):
                lo, hi = max(at, part * r), min(at + rows, (part + 1) * r)
                if lo < hi:
                    new = jnp.zeros((hi - lo, D), f32) if get is None else get(s, lo - at, hi - at)
                    ref[part, s, lo - part * r : hi - part * r] = new.astype(ref.dtype)
            at += rows


def write_halves(core, pieces, keep, give):
    half = keep.shape[0] * keep.shape[2]
    for mine in range(2):

        @pl.when(core == mine)
        def _(mine=mine):
            write_parts(pieces, mine * half, keep)
            write_parts(pieces, (1 - mine) * half, give)


def clear(*refs):
    for ref in refs:
        ref[...] = jnp.zeros_like(ref)


def first_step(fn):
    pl.when(pl.program_id(0) == 0)(fn)


def last_step(fn):
    pl.when(pl.program_id(0) == pl.num_programs(0) - 1)(fn)


def attn_fwd_kernel(place, x, *refs):
    own, near, far = refs[0:3], refs[3:6], refs[6:9]
    middle, packed, probs, mixed, value, wqkv, wm, sm, qkv, out = refs[9:]

    @first_step
    def _():
        assemble_attn(0, place[0], place[1], own, near, far, wqkv, wm, sm)
        project(x, wqkv, sm, qkv)

    crops = [pl.program_id(0) * STEP_CROPS + i for i in range(STEP_CROPS)]
    attend_crops(place, crops, range(STEP_CROPS), qkv, packed, probs, out)

    @last_step
    def _():
        mix(out, qkv, (2, 5), sm, mixed)
        for orient in range(2):
            value[orient] = qkv[orient * 3 + 2, :ROWS, :].astype(bf16)
        mixer(x, mixed, wm, sm, middle)


def ff_fwd_kernel(place, middle, sm, *refs):
    own, near, far = refs[0:2], refs[2:5], refs[5:8]
    out, we, wr = refs[8:]

    @first_step
    def _():
        assemble_ff(0, place[0], place[1], own, near, far, we, wr)

    out[...] = ff_forward(middle[...], we, wr, sm)


def top_kernel(place, x, cotangent, *refs):
    attn_own, ff_own, rest = refs[0:3], refs[3:5], refs[5]
    (output, grad_out, grads) = refs[6:9]
    (wqkv, wm, sm, we, wr, qkv, out, packed, probs, mixed, middle, g, slope, e, e_low,
     acc_e, acc_r, acc_q, acc_m, vec) = refs[9:]

    assemble_top(place[0], attn_own, ff_own, rest, wqkv, wm, sm, we, wr)
    clear(acc_e, acc_r, acc_q, acc_m, vec)
    project(x, wqkv, sm, qkv)

    def ahead(i, _):
        crops = [i * STEP_CROPS + j for j in range(STEP_CROPS)]
        attend_crops(place, crops, crops, qkv, packed, probs, out)
        return 0

    lax.fori_loop(0, CROPS // STEP_CROPS, ahead, 0)
    mix(out, qkv, (2, 5), sm, mixed)
    mixer(x, mixed, wm, sm, middle)
    for rows in chunks():
        gs, slopes = {}, {}
        output[rows, :] = ff_forward(middle[rows, :], we, wr, sm, gs, slopes).astype(bf16)
        for s in range(4):
            g[rows, s * 256 : (s + 1) * 256] = gs[s]
            slope[rows, s * 256 : (s + 1) * 256] = slopes[s]
    for rows in chunks():
        held = lambda s: (g[rows, s * 256 : (s + 1) * 256], slope[rows, s * 256 : (s + 1) * 256])
        middle_here = middle[rows, :]
        middle[rows, :] = ff_backward(cotangent[rows, :].astype(f32), middle_here, we, wr, sm, acc_e, acc_r, vec, held)
    em = out
    mixer_back(middle, mixed, wm, acc_m, vec, em)

    def behind(i, _):
        crops = [i * STEP_CROPS + j for j in range(STEP_CROPS)]
        attend_crops_back(crops, crops, em, packed, probs, e)
        return 0

    lax.fori_loop(0, CROPS // STEP_CROPS, behind, 0)
    mix_back(em, qkv, (2, 5), sm, e, e_low, vec)
    project_back(middle, x, e_low, wqkv, sm, acc_q, vec, grad_out)
    write_parts(attn_pieces(acc_q, acc_m, jnp.sum(vec[...], axis=1)) + ff_pieces(acc_e, acc_r), 0, grads)


def ff_bwd_kernel(place, grad, middle, we, wr, sm, grad_mid, keep, give, vec, acc_e, acc_r):
    @first_step
    def _():
        clear(acc_e, acc_r, vec)

    grad_mid[...] = ff_backward(grad[...], middle[...], we, wr, sm, acc_e, acc_r, vec)

    @last_step
    def _():
        write_halves(place[1], ff_pieces(acc_e, acc_r), keep, give)


def attn_bwd_kernel(place, grad, x, packed, probs, mixed, value, wqkv, wm, sm, vec_in, patch_grad, keep, give, em, e, e_low, acc_q, acc_m, vec):
    @first_step
    def _():
        clear(acc_q, acc_m)
        vec[...] = vec_in[...]
        mixer_back(grad, mixed, wm, acc_m, vec, em)

    crops = [pl.program_id(0) * STEP_CROPS + i for i in range(STEP_CROPS)]
    attend_crops_back(crops, range(STEP_CROPS), em, packed, probs, e)

    @last_step
    def _():
        mix_back(em, value, (0, 1), sm, e, e_low, vec)
        project_back(grad, x, e_low, wqkv, sm, acc_q, vec, patch_grad)
        write_halves(place[1], attn_pieces(acc_q, acc_m, jnp.sum(vec[...], axis=1)), keep, give)


def whole(shape):
    return pl.BlockSpec(shape, lambda i, *_: (0,) * len(shape))


def rows_of(lanes, rows=CHUNK):
    return pl.BlockSpec((rows, lanes), lambda i, *_: (i, 0))


def crop_spec(*dims):
    return pl.BlockSpec((STEP_CROPS, 4) + dims, lambda i, *_: (i, 0, 0, 0))


def of_layer(layer, *dims):
    return pl.BlockSpec((1,) + dims, lambda i, *_: (layer,) + (0,) * len(dims))


def attn_specs(layer):
    return [of_layer(layer, 192, D), of_layer(layer, 64, D), whole((2, 32, D))]


def ff_specs(layer):
    return [of_layer(layer, D, D), of_layer(layer, 64, FF)]


def half_specs(rows):
    return [whole((rows, D))] * 6


def shape(dims, dtype=bf16):
    return jax.ShapeDtypeStruct(dims, dtype)


def params(micros):
    return dict(
        compiler_params=pltpu.CompilerParams(
            vmem_limit_bytes=58 * 1024 * 1024, dimension_semantics=("arbitrary",)
        ),
        cost_estimate=pl.CostEstimate(flops=int(micros * 1e9), bytes_accessed=1 << 20, transcendentals=0),
    )


v = pltpu.VMEM


def attn_fwd_call(place, x, unit):
    rows = unit[-1].shape[0]
    return pl.pallas_call(
        attn_fwd_kernel,
        grid_spec=pltpu.PrefetchScalarGridSpec(
            num_scalar_prefetch=1,
            grid=(CROPS // STEP_CROPS,),
            in_specs=[whole((ROWS, D))] + attn_specs(0) + half_specs(rows),
            out_specs=[whole((ROWS, D)), crop_spec(WIN, 384), crop_spec(WIN, 512), whole((ROWS, D)), whole((2, ROWS, 128)), whole((768, D)), whole((D, D)), whole((32, D))],
            scratch_shapes=[v((6, HELD, 128), f32), v((2, HELD, 128), f32)],
        ),
        out_shape=[shape((ROWS, D), f32), shape((CROPS, 4, WIN, 384)), shape((CROPS, 4, WIN, 512)), shape((ROWS, D)), shape((2, ROWS, 128)), shape((768, D)), shape((D, D)), shape((32, D), f32)],
        name="attn_fwd",
        **params(10),
    )(place, x, *unit)


def ff_fwd_call(place, middle, sm, unit):
    return pl.pallas_call(
        ff_fwd_kernel,
        grid_spec=pltpu.PrefetchScalarGridSpec(
            num_scalar_prefetch=1,
            grid=(ROWS // CHUNK,),
            in_specs=[rows_of(D), whole((32, D))] + ff_specs(0) + half_specs(HALF_FF),
            out_specs=[rows_of(D), whole((4, D, D)), whole((D, FF))],
        ),
        out_shape=[shape((ROWS, D), f32), shape((4, D, D)), shape((D, FF))],
        name="ff_fwd",
        **params(6),
    )(place, middle, sm, *unit)


def top_call(place, x, cotangent, weights, parts, r):
    dp, _, rest_rows, _ = weights[-1].shape
    return pl.pallas_call(
        top_kernel,
        grid_spec=pltpu.PrefetchScalarGridSpec(
            num_scalar_prefetch=1,
            grid=(1,),
            in_specs=[whole((ROWS, D)), whole((ROWS, D))] + attn_specs(1) + ff_specs(1) + [whole((dp, 3, rest_rows, D))],
            out_specs=[whole((ROWS, D)), whole((ROWS, D)), whole((parts, 4, r, D))],
            scratch_shapes=[
                v((768, D), bf16), v((D, D), bf16), v((32, D), f32), v((4, D, D), bf16), v((D, FF), bf16),
                v((6, HELD, 128), f32), v((2, HELD, 128), f32), v((CROPS, 4, WIN, 384), bf16), v((CROPS, 4, WIN, 512), bf16),
                v((ROWS, D), bf16), v((ROWS, D), f32), v((ROWS, FF), bf16), v((ROWS, FF), bf16),
                v((6, HELD, 128), f32), v((ROWS, 768), bf16),
                v((4, D, D), f32), v((4, D, D), f32), v((768, D), f32), v((D, D), f32), v((32, CROPS, D), f32),
            ],
        ),
        out_shape=[shape((ROWS, D)), shape((ROWS, D), f32), shape((parts, 4, r, D))],
        name="top_block",
        **params(30),
    )(place, x, cotangent, *weights)


def ff_bwd_call(place, grad, middle, we, wr, sm, parts, r):
    return pl.pallas_call(
        ff_bwd_kernel,
        grid_spec=pltpu.PrefetchScalarGridSpec(
            num_scalar_prefetch=1,
            grid=(ROWS // CHUNK,),
            in_specs=[rows_of(D), rows_of(D), whole((4, D, D)), whole((D, FF)), whole((32, D))],
            out_specs=[rows_of(D)] + [whole((parts, 4, r, D))] * 2 + [whole((32, CROPS, D))],
            scratch_shapes=[v((4, D, D), f32), v((4, D, D), f32)],
        ),
        out_shape=[shape((ROWS, D), f32)] + [shape((parts, 4, r, D))] * 2 + [shape((32, CROPS, D), f32)],
        name="ff_bwd",
        **params(10),
    )(place, grad, middle, we, wr, sm)


def attn_bwd_call(place, grad, x, packed, probs, mixed, value, wqkv, wm, sm, vec):
    return pl.pallas_call(
        attn_bwd_kernel,
        grid_spec=pltpu.PrefetchScalarGridSpec(
            num_scalar_prefetch=1,
            grid=(CROPS // STEP_CROPS,),
            in_specs=[whole((ROWS, D)), whole((ROWS, D)), crop_spec(WIN, 384), crop_spec(WIN, 512), whole((ROWS, D)), whole((2, ROWS, 128)), whole((768, D)), whole((D, D)), whole((32, D)), whole((32, CROPS, D))],
            out_specs=[whole((ROWS, D))] + [whole((1, 4, LOW_ROWS // 2, D))] * 2,
            scratch_shapes=[v((2, HELD, 128), f32), v((6, HELD, 128), f32), v((ROWS, 768), bf16), v((768, D), f32), v((D, D), f32), v((32, CROPS, D), f32)],
        ),
        out_shape=[shape((ROWS, D))] + [shape((1, 4, LOW_ROWS // 2, D))] * 2,
        name="attn_bwd",
        **params(16),
    )(place, grad, x, packed, probs, mixed, value, wqkv, wm, sm, vec)


def to_rows(x):
    return jnp.transpose(x, (1, 2, 0, 3)).reshape(ROWS, D)


def from_rows(x):
    return jnp.transpose(x.reshape(GRID, GRID, CROPS, D), (2, 0, 1, 3))


def pack_kernel(place, qkv, mixer_t, gain, shift, entry, taps, branch, hidden_bias, expand, reduce_t, half_a, half_f, vec, unit):
    me, core = place[0], place[1]
    lane = lax.broadcasted_iota(jnp.int32, (18, D), 1)
    row = lax.broadcasted_iota(jnp.int32, (14, D), 0)
    for layer in range(2):
        rows = jnp.concatenate(
            [ref[layer].astype(f32) for ref in (gain, shift, entry)] + [taps[:, layer].astype(f32), branch[layer].astype(f32)], axis=0
        )
        vectors = jnp.where(lane // 64 == me, jnp.concatenate([rows] * 4, axis=1), 0.0)
        hidden_rows = jnp.where(row == me, hidden_bias[layer : layer + 1].astype(f32), 0.0)
        vec[layer] = jnp.concatenate([vectors, hidden_rows], axis=0).astype(bf16)
    half_a[0:96] = qkv[0, pl.ds(pl.multiple_of(96 * core, 32), 96)]
    half_a[96:128] = mixer_t[0, pl.ds(pl.multiple_of(32 * core, 32), 32)]
    half_a[128:144] = vec[0, pl.ds(pl.multiple_of(16 * core, 16), 16)]
    half_f[0:128] = expand[0, pl.ds(pl.multiple_of(128 * core, 128), 128)]
    for c in range(4):
        half_f[128 + 32 * c : 160 + 32 * c] = reduce_t[0, pl.ds(pl.multiple_of(32 * core, 32), 32), c * 256 : (c + 1) * 256]
    unit[0:192] = qkv[1]
    unit[192:256] = mixer_t[1]
    unit[256:288] = vec[1]
    unit[288:544] = expand[1]
    for c in range(4):
        unit[544 + 64 * c : 608 + 64 * c] = reduce_t[1, :, c * 256 : (c + 1) * 256]
    if unit.shape[0] > UNIT:
        unit[UNIT:] = jnp.zeros((unit.shape[0] - UNIT, D), bf16)
    r = half_a.shape[0] - HALF_ATTN
    half_a[HALF_ATTN:] = unit[pl.ds(pl.multiple_of(place[3] * r, 16), r)]


def local_call(kernel, name, place, arrays, outs, scratch=()):
    return pl.pallas_call(
        kernel,
        grid_spec=pltpu.PrefetchScalarGridSpec(
            num_scalar_prefetch=1,
            grid=(1,),
            in_specs=[whole(x.shape) for x in arrays],
            out_specs=[whole(dims) for dims, _ in outs],
            scratch_shapes=list(scratch),
        ),
        out_shape=[shape(dims, dtype) for dims, dtype in outs],
        name=name,
        **params(1),
    )(place, *arrays)


def turn_mp(x, k):
    n = lax.axis_size("mp")
    return lax.ppermute(x, "mp", [(i, (i + k) % n) for i in range(n)])


def swap_dp(x, bits):
    n = lax.axis_size("dp")
    return lax.ppermute(x, "dp", [(i, i ^ bits) for i in range(n)])


def turn_all(x):
    return [turn_mp(x, k) for k in (1, 2, 3)]


def swap_core(xs):
    return [swap_dp(x, 1) for x in xs]


def pick(x, at):
    return lax.dynamic_index_in_dim(x, at, 0, keepdims=False)


def add_up(xs):
    total = xs[0].astype(f32)
    for x in xs[1:]:
        total = total + x.astype(f32)
    return total


def to_planes(keep, got, at):
    total = add_up([keep, got]).astype(bf16)
    return [pick(total, at ^ b) for b in range(keep.shape[0])]


def swap_planes(parts):
    return [parts[0]] + [swap_dp(part, 2 * b) for b, part in enumerate(parts) if b]


def to_shards(xs, me):
    total = add_up(xs)
    low = total.astype(bf16)
    return [pick(total, me)] + [pick(low, (me + k) % 4) for k in (1, 2, 3)]


def turn_shards(parts):
    return [parts[0]] + [turn_mp(part, k) for k, part in enumerate(parts) if k]


def unpack_kernel(planes, cut_f, cut_t, place, *refs):
    mine, other = refs[:planes], refs[planes : 2 * planes]
    packed, mixer_g, expand, reduce_g, gain, shift, entry, taps, branch, hidden_g, held, held_t = refs[2 * planes :]
    me, core = place[0], place[1]
    r_f, r_t = cut_t - cut_f, mine[0].shape[0] - cut_t
    for which, parts in ((core, mine), (1 - core, other)):
        total = parts[0][:cut_f].astype(f32)
        for part in parts[1:]:
            total = total + part[:cut_f].astype(f32)
        held[which, :cut_f] = total
        for b in range(planes):
            at = place[2] ^ b
            held[which, pl.ds(pl.multiple_of(cut_f + at * r_f, 16), r_f)] = parts[b][cut_f:cut_t].astype(f32)
            held_t[pl.ds(pl.multiple_of((2 * at + which) * r_t, 16), r_t)] = parts[b][cut_t:].astype(f32)

    def rows(which, lo, hi):
        if which is None:
            return held_t[lo:hi]
        start, half = which
        out = []
        for c in range(2):
            a, b = max(lo, c * half), min(hi, (c + 1) * half)
            if a < b:
                out.append(held[c, start + a - c * half : start + b - c * half])
        return out[0] if len(out) == 1 else jnp.concatenate(out, axis=0)

    low_a, low_f = (0, cut_f), (cut_f, planes * r_f)
    for layer, attn, ff, ff_at in ((0, low_a, low_f, 0), (1, None, None, 288)):
        packed[layer] = rows(attn, 0, 192)
        mixer_g[layer] = rows(attn, 192, 256)
        expand[layer] = rows(ff, ff_at, ff_at + 256)
        for c in range(4):
            at = ff_at + 256 + 64 * c
            reduce_g[layer, :, c * 256 : (c + 1) * 256] = rows(ff, at, at + 64)
        vectors = rows(attn, 256, 288)
        mine_lanes = vectors[:, :64]
        for s in range(1, 4):
            mine_lanes = jnp.where(me == s, vectors[:, 64 * s : 64 * (s + 1)], mine_lanes)
        gain[layer] = mine_lanes[GAIN : GAIN + 2]
        shift[layer] = mine_lanes[SHIFT : SHIFT + 2]
        entry[layer] = mine_lanes[ENTRY : ENTRY + 2]
        branch[layer] = mine_lanes[BRANCH : BRANCH + 2]
        for t in range(10):
            taps[t, layer : layer + 1] = mine_lanes[TAPS + t : TAPS + t + 1]
        row = vectors[HIDDEN : HIDDEN + 1]
        for s in range(1, 4):
            row = jnp.where(me == s, vectors[HIDDEN + s : HIDDEN + s + 1], row)
        hidden_g[layer : layer + 1] = row


def body(patches, validity, norm_gain, norm_shift, qkv_weight, entry_bias, stencil, mixer_weight, branch_bias, expand_weight, hidden_bias, reduce_weight, cotangent):
    dp = lax.axis_size("dp")
    planes = dp // 2
    me, at_dp = lax.axis_index("mp"), lax.axis_index("dp")
    heights = jnp.sum(validity[:, :, 0], axis=1)
    widths = jnp.sum(validity[:, 0, :], axis=1)
    place = jnp.stack([me, at_dp % 2, at_dp // 2, at_dp]).astype(jnp.int32)
    sizes = jnp.concatenate([jnp.stack([me, at_dp % 2]), jnp.stack([heights, widths], axis=1).reshape(-1)]).astype(jnp.int32)

    qkv_t = jnp.transpose(qkv_weight, (0, 2, 3, 1)).reshape(2, 192, D)
    mixer_t = jnp.transpose(mixer_weight, (0, 2, 1))
    reduce_t = jnp.transpose(reduce_weight, (0, 2, 1))
    vectors = (norm_gain, norm_shift, entry_bias, jnp.transpose(stencil, (1, 0, 2)), branch_bias, hidden_bias)

    arrays = [qkv_t, mixer_t, norm_gain, norm_shift, entry_bias, jnp.transpose(stencil, (1, 0, 2)), branch_bias, hidden_bias, expand_weight, reduce_t]
    r_t, r_f = part_rows(UNIT, dp), part_rows(FF_ROWS, dp)
    outs = [(HALF_ATTN + r_t, D), (HALF_FF, D), (2, 32, D)]
    half_a0, half_f0, vec = local_call(
        pack_kernel, "pack", place, arrays, [(dims, bf16) for dims in outs], [v((dp * r_t, D), bf16)]
    )
    attn_own, ff_own = [qkv_t, mixer_t, vec], [expand_weight, reduce_t]

    near_a0 = turn_all(half_a0)
    near_1 = jnp.stack([x[HALF_ATTN:] for x in near_a0])
    near_f0 = turn_all(half_f0)
    far_a0 = swap_core(near_a0)
    x, top_grad = to_rows(patches), to_rows(cotangent)
    near_1, x = lax.optimization_barrier((near_1, x))
    rest_1 = lax.all_gather(near_1, "dp", axis=0, tiled=False)
    middle, packed, probs, mixed, value, wqkv, wm, sm = attn_fwd_call(sizes, x, attn_own + near_a0 + far_a0)
    near_f0, middle = lax.optimization_barrier((near_f0, middle))
    far_f0 = swap_core(near_f0)
    state, we, wr = ff_fwd_call(sizes, middle, sm, ff_own + near_f0 + far_f0)
    output, grad, grads_1 = top_call(sizes, state, top_grad, attn_own + ff_own + [rest_1], dp, r_t)
    sums_1 = lax.psum_scatter(grads_1, "dp", scatter_dimension=0, tiled=False)

    grad_mid, keep_f, give_f, vec = ff_bwd_call(place, grad, middle, we, wr, sm, planes, r_f)
    got_f = swap_dp(give_f, 1)
    patch_grad, keep_a, give_a = attn_bwd_call(place, grad_mid, x, packed, probs, mixed, value, wqkv, wm, sm, vec)
    got_f, keep_a, give_a = lax.optimization_barrier((got_f, keep_a, give_a))

    got_a = swap_dp(give_a, 1)
    planes_f = swap_planes(to_planes(keep_f, got_f, place[2]))
    shards_a = to_shards([keep_a[0], got_a[0]], me)
    mp_a = turn_shards(shards_a)
    planes_f, sums_1 = lax.optimization_barrier((planes_f, sums_1, shards_a))[:2]
    low = add_up(planes_f).astype(bf16)
    mp_f = turn_shards(to_shards([jnp.concatenate([low, sums_1], axis=1)], me))
    share = jnp.concatenate([add_up(mp_a), add_up(mp_f)], axis=0).astype(bf16)
    mine = swap_planes([share] * planes)
    other = swap_core(mine)
    outs = [(2, 192, D), (2, 64, D), (2, D, D), (2, 64, FF), (2, 2, 64), (2, 2, 64), (2, 2, 64), (10, 2, 64), (2, 2, 64), (2, D)]
    cut_f = LOW_ROWS // 2
    cut_t = cut_f + r_f
    held = [v((2, cut_f + planes * r_f, D), f32), v((dp * r_t, D), f32)]
    packed_g, mixer_g, expand_g, reduce_g, gain_g, shift_g, entry_g, taps_g, branch_g, hidden_g = local_call(
        functools.partial(unpack_kernel, planes, cut_f, cut_t), "unpack", place, mine + other, [(dims, f32) for dims in outs], held
    )
    return (
        from_rows(output), from_rows(patch_grad), gain_g, shift_g,
        jnp.transpose(packed_g.reshape(2, 3, 64, D), (0, 3, 1, 2)), entry_g, jnp.transpose(taps_g, (1, 0, 2)),
        jnp.transpose(mixer_g, (0, 2, 1)), branch_g, expand_g, hidden_g, jnp.transpose(reduce_g, (0, 2, 1)),
    )


def solution(mesh):
    crops = P(("dp", "mp"), None, None, None)
    lanes = P(None, None, "mp")
    deep = P(None, None, None, "mp")
    return jax.shard_map(
        body,
        mesh=mesh,
        in_specs=(crops, P(("dp", "mp"), None, None), lanes, lanes, deep, lanes, lanes, lanes, lanes, lanes, P(None, "mp"), lanes, crops),
        out_specs=(crops, crops, lanes, lanes, deep, lanes, lanes, lanes, lanes, lanes, P(None, "mp"), lanes),
        check_vma=False,
    )
```

```python
import functools

import jax
import jax.numpy as jnp
from jax import lax
from jax.experimental import pallas as pl
from jax.experimental.pallas import tpu as pltpu
from jax.sharding import PartitionSpec as P

GRID = 14
STRIPE = 7
CELLS = GRID * GRID
CROPS = 8
ROWS = CELLS * CROPS
LINE = GRID * CROPS
HELD = ROWS + 112
WIN = 112
HALF_HEADS = 4
HEAD = 32
D = 256
FF = 1024
STEP_CROPS = 2
CHUNK = 784

norm_eps = 1e-05
masked_score = -1e30
root_half = 0.7071067811865476
inverse_root_tau = 0.3989422804014327
log2_e = 1.4426950408889634
factor = HEAD**-0.5

f32 = jnp.float32
bf16 = jnp.bfloat16

HALF_ATTN = 144
HALF_FF = 256
FF_ROWS = 512
UNIT = 800
LOW_ROWS = 288
GAIN, SHIFT, ENTRY, TAPS, BRANCH, HIDDEN = 0, 2, 4, 6, 16, 18


def dot(a, b):
    return lax.dot_general(a, b, (((1,), (0,)), ((), ())), preferred_element_type=f32)


def dot_nt(a, b):
    return lax.dot_general(a, b, (((1,), (1,)), ((), ())), preferred_element_type=f32)


def dot_tn(a, b):
    return lax.dot_general(a, b, (((0,), (0,)), ((), ())), preferred_element_type=f32)


def norm(x):
    center = x - jnp.mean(x, axis=-1, keepdims=True)
    spread = jnp.mean(center * center, axis=-1, keepdims=True)
    inverse = lax.rsqrt(spread + norm_eps)
    return center * inverse, inverse


def norm_back(grad, normal, inverse, gain):
    scaled = grad * gain
    return inverse * (
        scaled
        - jnp.mean(scaled, axis=-1, keepdims=True)
        - normal * jnp.mean(scaled * normal, axis=-1, keepdims=True)
    )


def column_sum(x):
    return jnp.sum(x.reshape(x.shape[0] // CROPS, CROPS, x.shape[1]), axis=0)


def window_row_inside(orient):
    row = lax.broadcasted_iota(jnp.int32, (WIN, 128), 0)
    return row < 98 if orient == 0 else row % 8 < STRIPE


def key_bias(orient, window, height, width):
    row = lax.broadcasted_iota(jnp.int32, (WIN, 128), 0)
    if orient == 0:
        line, column = row // GRID + window * STRIPE, row % GRID
    else:
        line, column = row // 8, row % 8 + window * STRIPE
    valid = window_row_inside(orient) & (line < height) & (column < width)
    return jnp.where(valid, 0.0, masked_score)


def load_window(ref, block, crop, orient, window):
    if orient == 0:
        return ref[block, pl.ds(98 * CROPS * window + crop, WIN, stride=CROPS), :]
    parts = [
        ref[block, pl.ds((line * GRID + window * STRIPE) * CROPS + crop, 8, stride=CROPS), :]
        for line in range(GRID)
    ]
    return jnp.concatenate(parts, axis=0)


def store_window(ref, block, crop, orient, window, x):
    if orient == 0:
        ref[block, pl.ds(98 * CROPS * window + crop, 98, stride=CROPS), :] = x[:98]
        return
    for line in range(GRID):
        at = (line * GRID + window * STRIPE) * CROPS + crop
        ref[block, pl.ds(at, STRIPE, stride=CROPS), :] = x[line * 8 : line * 8 + STRIPE]


def fill_head_masks(masks):
    lane = lax.broadcasted_iota(jnp.int32, (WIN, 256), 1) % 128 // HEAD
    for head in range(HALF_HEADS):
        masks[head] = jnp.where(lane == head, 1.0, 0.0).astype(bf16)


def heads_down(x, masks):
    return jnp.concatenate([x * masks[head] for head in range(HALF_HEADS)], axis=0)


def fold_heads(x):
    head = lax.broadcasted_iota(jnp.int32, (WIN, 256), 1) % 128 // HEAD
    parts = [x[h * WIN : (h + 1) * WIN] for h in range(HALF_HEADS)]
    low, high = jnp.where(head == 0, parts[0], parts[1]), jnp.where(head == 2, parts[2], parts[3])
    return jnp.where(head < 2, low, high)


def windows_apart(x):
    none, rest = jnp.zeros((WIN, 128), x.dtype), jnp.zeros((128 - WIN, 256), x.dtype)
    first = jnp.concatenate([x[:, :128], none], axis=1)
    second = jnp.concatenate([none, x[:, 128:]], axis=1)
    return jnp.concatenate([first, rest, second, rest], axis=0)


def by_head(turned, probs):
    parts = []
    for head in range(HALF_HEADS):
        left = jnp.concatenate([turned[w * 128 + head * HEAD : w * 128 + (head + 1) * HEAD] for w in range(2)], axis=0)
        both = dot(left, probs[head * WIN : (head + 1) * WIN])
        parts.append((both[:HEAD, :128], both[HEAD:, 128:]))
    return [jnp.concatenate([part[w] for part in parts], axis=0).T[:WIN] for w in range(2)]


def head_probs(scores, bias):
    scores = scores * (factor * log2_e) + bias
    raised = jnp.exp2(scores - jnp.max(scores, axis=0, keepdims=True))
    return (raised * (1.0 / jnp.sum(raised, axis=0, keepdims=True))).astype(bf16)


def head_grad_scores(grad_probs, probs):
    wide = probs.astype(f32)
    inner = jnp.sum(grad_probs * wide, axis=0, keepdims=True)
    return (wide * (grad_probs - inner)).astype(bf16)


def each_head(fn, *arrays):
    parts = [fn(*(x[h * WIN : (h + 1) * WIN] for x in arrays)) for h in range(HALF_HEADS)]
    return jnp.concatenate(parts, axis=0)


def attend(queries, keys, values, biases, masks):
    apart = [windows_apart(x.astype(bf16)) for x in queries]
    scores = [dot_nt(heads_down(k.astype(bf16), masks), q) for k, q in zip(keys, apart)]
    value_turned = [x.T.astype(bf16) for x in values]
    probs = [each_head(lambda s, b=b: head_probs(s, b), s) for s, b in zip(scores, biases)]
    return [by_head(v, p) for v, p in zip(value_turned, probs)], probs


def attend_back(grads, queries, keys, values, probs, masks):
    grad_apart = [windows_apart(x) for x in grads]
    grad_probs = [dot_nt(heads_down(v, masks), g) for v, g in zip(values, grad_apart)]
    key_turned = [x.astype(f32).T.astype(bf16) for x in keys]
    grad_value = [fold_heads(dot(p, g)) for p, g in zip(probs, grad_apart)]
    grad_scores = [each_head(head_grad_scores, g, p) for g, p in zip(grad_probs, probs)]
    apart = [windows_apart(x) for x in queries]
    grad_key = [fold_heads(dot(s, q)) * factor for s, q in zip(grad_scores, apart)]
    grad_query = [[x * factor for x in by_head(k, s)] for k, s in zip(key_turned, grad_scores)]
    return grad_query, grad_key, grad_value


def steps_along(x, orient):
    zero = jnp.zeros((CROPS, x.shape[1]), x.dtype)
    if orient == 0:
        return {-1: jnp.concatenate([zero, x[:-CROPS]], axis=0), 0: x, 1: jnp.concatenate([x[CROPS:], zero], axis=0)}
    half = LINE // 2
    left, right = x[:half], x[half:]
    return {
        -1: jnp.concatenate([zero, left[:-CROPS], zero, right[:-CROPS]], axis=0),
        0: x,
        1: jnp.concatenate([left[CROPS:], zero, right[CROPS:], zero], axis=0),
    }


def line_reaches(line, step, orient):
    if step == 0:
        return None
    stops = (GRID, STRIPE) if orient == 0 else (GRID,)
    edges = [(stop - 1) if step == 1 else (stop % GRID) for stop in stops]
    ok = line != edges[0]
    for edge in edges[1:]:
        ok = ok & (line != edge)
    return jnp.where(ok, 1.0, 0.0).astype(f32)


def line_at(ref, block, line):
    held = jnp.clip(line, 0, GRID - 1)
    return ref[block, pl.ds(pl.multiple_of(held * LINE, LINE), LINE), :]


def stencil_line(ref, block, taps, line, orient, back):
    total = None
    for step in (-1, 0, 1):
        moved = steps_along(line_at(ref, block, line + (-step if back else step)).astype(f32), orient)
        reach = line_reaches(line, -step if back else step, orient)
        for side in (-1, 0, 1):
            tap = taps[3 * (step + 1) + side + 1]
            if reach is not None:
                tap = tap * reach
            term = moved[-side if back else side] * tap
            total = term if total is None else total + term
    return total


def stencil_line_taps(ref, block, grad, line, orient):
    sums = []
    for step in (-1, 0, 1):
        moved = steps_along(line_at(ref, block, line + step).astype(f32), orient)
        reach = line_reaches(line, step, orient)
        for side in (-1, 0, 1):
            part = column_sum(grad * moved[side])
            sums.append(part if reach is None else part * reach)
    sums.append(column_sum(grad))
    return sums


def assemble_attn(layer, me, core, own, near, far, wqkv, wm, sm):
    qkv, mixer_t, vec = own

    def put(shard, blocks, at, mixer_rows, mixer_at):
        orient, part = lax.div(shard, 2), lax.rem(shard, 2)
        for i, block in enumerate(blocks):
            j = at + i
            row = orient * 384 + lax.div(j, 2) * 128 + part * 64 + lax.rem(j, 2) * 32
            wqkv[pl.ds(pl.multiple_of(row, 32), 32), :] = block
        wm[pl.ds(pl.multiple_of(shard * 64 + mixer_at, 32), mixer_rows.shape[0]), :] = mixer_rows

    put(me, [qkv[0, 32 * i : 32 * (i + 1)] for i in range(6)], jnp.int32(0), mixer_t[0], 0)
    sm[...] = vec[layer].astype(f32)
    for halves, which in ((near, core), (far, 1 - core)):
        for k, half in enumerate(halves, 1):
            shard = lax.rem(me + 4 - k, 4)
            put(shard, [half[32 * i : 32 * (i + 1)] for i in range(3)], 3 * which, half[96:128], 32 * which)
            sm[pl.ds(pl.multiple_of(16 * which, 16), 16), :] += half[128:144].astype(f32)


def assemble_ff(first, me, core, own, near, far, we, wr):
    expand, reduce_t = own
    we[me] = expand[0]
    wr[pl.ds(pl.multiple_of(me * 64, 64), 64), :] = reduce_t[0]
    for halves, which in ((near, core), (far, 1 - core)):
        for k, half in enumerate(halves, 1):
            shard = lax.rem(me + 4 - k, 4)
            we[shard, pl.ds(pl.multiple_of(128 * which, 128), 128), :] = half[first : first + 128]
            row = pl.multiple_of(shard * 64 + 32 * which, 32)
            for c in range(4):
                at = first + 128 + 32 * c
                wr[pl.ds(row, 32), c * 256 : (c + 1) * 256] = half[at : at + 32]


def assemble_top(me, attn_own, ff_own, rest, wqkv, wm, sm, we, wr):
    qkv, mixer_t, vec = attn_own
    expand, reduce_t = ff_own

    def put(shard, row, value):
        orient, part = lax.div(shard, 2), lax.rem(shard, 2)
        n = value.shape[0]
        if row < 192:
            at = orient * 384 + row // 64 * 128 + part * 64 + row % 64
            wqkv[pl.ds(pl.multiple_of(at, 16), n), :] = value
        elif row < 256:
            wm[pl.ds(pl.multiple_of(shard * 64 + row - 192, 16), n), :] = value
        elif row < 288:
            sm[row - 256 : row - 256 + n, :] += value.astype(f32)
        elif row < 544:
            we[shard, row - 288 : row - 288 + n, :] = value
        else:
            c, at = divmod(row - 544, 64)
            wr[pl.ds(pl.multiple_of(shard * 64 + at, 16), n), c * 256 : (c + 1) * 256] = value

    for p in range(3):
        put(me, 64 * p, qkv[1, 64 * p : 64 * (p + 1)])
    put(me, 192, mixer_t[1])
    sm[...] = vec[1].astype(f32)
    put(me, 288, expand[1])
    for c in range(4):
        put(me, 544 + 64 * c, reduce_t[1, :, c * 256 : (c + 1) * 256])
    dp, _, r, _ = rest.shape
    edges = list(range(0, 257, 64)) + [288] + [544 + 64 * c for c in range(5)]
    for k in range(3):
        shard = lax.rem(me + 3 - k, 4)
        for d in range(dp):
            for lo, hi in zip(edges[:-1], edges[1:]):
                a, b = max(lo, d * r), min(hi, (d + 1) * r)
                if a < b:
                    put(shard, a, rest[d, k, a - d * r : b - d * r])


def chunks():
    return [slice(at, at + CHUNK) for at in range(0, ROWS, CHUNK)]


def put_blocks(ref, rows, x):
    for block in range(x.shape[1] // 128):
        ref[block, rows, :] = x[:, block * 128 : (block + 1) * 128]


def project(x, wqkv, sm, qkv):
    zero = jnp.zeros((1, 128), f32)
    query_bias, value_bias = sm[ENTRY : ENTRY + 1], sm[ENTRY + 1 : ENTRY + 2]
    bias = jnp.concatenate(
        [query_bias[:, :128], zero, value_bias[:, :128], query_bias[:, 128:], zero, value_bias[:, 128:]], axis=1
    )
    for rows in chunks():
        normal, _ = norm(x[rows, :].astype(f32))
        a = (normal * sm[GAIN : GAIN + 1] + sm[SHIFT : SHIFT + 1]).astype(bf16)
        put_blocks(qkv, rows, dot_nt(a, wqkv[...]) + bias)
    qkv[:, ROWS:HELD, :] = jnp.zeros((6, HELD - ROWS, 128), f32)


def load_pair(ref, block, crop, orient):
    return jnp.concatenate([load_window(ref, block, crop, orient, window) for window in range(2)], axis=1)


def attend_crops(place, crops, slots, masks, qkv, packed, probs_ref, out):
    at, lists = [], ([], [], [], [])
    for crop, slot in zip(crops, slots):
        height, width = place[2 + 2 * crop], place[3 + 2 * crop]
        for orient in range(2):
            three = [load_pair(qkv, orient * 3 + p, crop, orient) for p in range(3)]
            for p, x in enumerate(three):
                packed[slot, orient, p] = x.astype(bf16)
            bias = jnp.concatenate([key_bias(orient, window, height, width) for window in range(2)], axis=1)
            for held, new in zip(lists, (*three, bias)):
                held.append(new)
            at.append((crop, slot, orient))
    outs, probs = attend(*lists, masks)
    for (crop, slot, orient), both, p in zip(at, outs, probs):
        probs_ref[slot, orient] = p
        for window in range(2):
            store_window(out, orient, crop, orient, window, both[window])


def attend_crops_back(crops, slots, masks, em, packed, probs_ref, e_at):
    at, lists = [], ([], [], [], [], [])
    for crop, slot in zip(crops, slots):
        for orient in range(2):
            inside = jnp.concatenate([window_row_inside(orient)] * 2, axis=1)
            grad = jnp.where(inside, load_pair(em, orient, crop, orient), 0.0).astype(bf16)
            for held, new in zip(lists, (grad, *(packed[slot, orient, p] for p in range(3)), probs_ref[slot, orient])):
                held.append(new)
            at.append((crop, orient))
    for (crop, orient), dq, dk, dv in zip(at, *attend_back(*lists, masks)):
        for window in range(2):
            lanes = slice(window * 128, (window + 1) * 128)
            for p, part in enumerate((dq[window], dk[:, lanes], dv[:, lanes])):
                store_window(*e_at(orient, p), crop, orient, window, part)


def taps_of(sm, orient):
    lanes = slice(orient * 128, (orient + 1) * 128)
    return [sm[TAPS + t : TAPS + t + 1, lanes] for t in range(10)]


def mix(out, value, value_at, sm, mixed):
    taps = [taps_of(sm, orient) for orient in range(2)]

    def line(i, _):
        rows = pl.ds(pl.multiple_of(i * LINE, LINE), LINE)
        for orient in range(2):
            e_v = stencil_line(value, value_at[orient], taps[orient], i, orient, False) + taps[orient][9]
            mixed[rows, orient * 128 : (orient + 1) * 128] = (out[orient, rows, :] + e_v).astype(bf16)
        return 0

    lax.fori_loop(0, GRID, line, 0)


def mixer(x, mixed, wm, sm, middle):
    for rows in chunks():
        middle[rows, :] = x[rows, :].astype(f32) + (dot_nt(mixed[rows, :], wm[...]) + sm[BRANCH : BRANCH + 1])


def hidden(a2, we, sm, s):
    u = dot(a2, we[s]) + sm[HIDDEN + s : HIDDEN + s + 1]
    phi = 0.5 + 0.5 * lax.erf(u * root_half)
    return u, phi


def slope_of(u, phi):
    return phi + u * jnp.exp(-0.5 * u * u) * inverse_root_tau


def second_norm(middle, sm):
    normal, inverse = norm(middle)
    a2 = (normal * sm[GAIN + 1 : GAIN + 2] + sm[SHIFT + 1 : SHIFT + 2]).astype(bf16)
    return normal, inverse, a2


def ff_forward(middle, we, wr, sm, g_out=None, slope_out=None):
    _, _, a2 = second_norm(middle, sm)
    gs = []
    for s in range(4):
        u, phi = hidden(a2, we, sm, s)
        gs.append((u * phi).astype(bf16))
        if g_out is not None:
            g_out[s], slope_out[s] = gs[-1], slope_of(u, phi).astype(bf16)
    return middle + (dot_nt(jnp.concatenate(gs, axis=1), wr[...]) + sm[BRANCH + 1 : BRANCH + 2])


def ff_backward(grad, middle, we, wr, sm, acc_e, acc_r, vec, held=None):
    ey = grad.astype(bf16)
    vec[BRANCH + 1] += column_sum(grad)
    normal, inverse, a2 = second_norm(middle, sm)
    eus = []
    for s in range(4):
        if held is None:
            u, phi = hidden(a2, we, sm, s)
            g, slope = (u * phi).astype(bf16), slope_of(u, phi)
        else:
            g, slope = held(s)
        acc_r[s] += dot_tn(ey, g)
        eu_wide = dot(ey, wr[:, s * 256 : (s + 1) * 256]) * slope.astype(f32)
        vec[HIDDEN + s] += column_sum(eu_wide)
        eu = eu_wide.astype(bf16)
        acc_e[s] += dot_tn(a2, eu)
        eus.append(eu)
    back = None
    for s in range(4):
        term = dot_nt(eus[s], we[s])
        back = term if back is None else back + term
    vec[GAIN + 1] += column_sum(back * normal)
    vec[SHIFT + 1] += column_sum(back)
    return grad + norm_back(back, normal, inverse, sm[GAIN + 1 : GAIN + 2])


def mixer_back(grad, mixed, wm, acc_m, vec, em):
    for rows in chunks():
        here = grad[rows, :]
        eo = here.astype(bf16)
        vec[BRANCH] += column_sum(here)
        acc_m[...] += dot_tn(eo, mixed[rows, :])
        put_blocks(em, rows, dot(eo, wm[...]))
    em[:, ROWS:HELD, :] = jnp.zeros((2, HELD - ROWS, 128), f32)


def mix_back(em, value, value_at, sm, e_at, e_low, vec):
    taps = [taps_of(sm, orient) for orient in range(2)]

    def line(i, _):
        rows = pl.ds(pl.multiple_of(i * LINE, LINE), LINE)
        for orient in range(2):
            lanes = slice(orient * 128, (orient + 1) * 128)
            base = orient * 384
            eq, ek, ev = [ref[block, rows, :] for ref, block in (e_at(orient, p) for p in range(3))]
            ev = ev + stencil_line(em, orient, taps[orient], i, orient, True)
            e_low[rows, base : base + 384] = jnp.concatenate([eq, ek, ev], axis=1).astype(bf16)
            vec[ENTRY, :, lanes] += column_sum(eq)
            vec[ENTRY + 1, :, lanes] += column_sum(ev)
            for t, part in enumerate(stencil_line_taps(value, value_at[orient], em[orient, rows, :], i, orient)):
                vec[TAPS + t, :, lanes] += part
        return 0

    lax.fori_loop(0, GRID, line, 0)


def project_back(grad, x, e_low, wqkv, sm, acc_q, vec, out):
    for rows in chunks():
        normal, inverse = norm(x[rows, :].astype(f32))
        a = (normal * sm[GAIN : GAIN + 1] + sm[SHIFT : SHIFT + 1]).astype(bf16)
        e = e_low[rows, :]
        acc_q[...] += dot_tn(e, a)
        back = dot(e, wqkv[...])
        vec[GAIN] += column_sum(back * normal)
        vec[SHIFT] += column_sum(back)
        out[rows, :] = (grad[rows, :] + norm_back(back, normal, inverse, sm[GAIN : GAIN + 1])).astype(out.dtype)


def attn_pieces(acc_q, acc_m, sums):
    def qkv(s, p, lo, hi):
        at = (s // 2) * 384 + p * 128 + (s % 2) * 64
        return acc_q[at + lo : at + hi]

    return [(64, lambda s, lo, hi, p=p: qkv(s, p, lo, hi)) for p in range(3)] + [
        (64, lambda s, lo, hi: acc_m[64 * s + lo : 64 * s + hi]),
        (32, lambda s, lo, hi: sums[lo:hi]),
    ]


def ff_pieces(acc_e, acc_r):
    return [(256, lambda s, lo, hi: acc_e[s, lo:hi])] + [
        (64, lambda s, lo, hi, c=c: acc_r[c, 64 * s + lo : 64 * s + hi]) for c in range(4)
    ]


def part_rows(rows, parts):
    return -(-rows // (16 * parts)) * 16


def write_parts(pieces, first, ref):
    parts, _, r, _ = ref.shape
    for s in range(4):
        at = -first
        for rows, get in pieces + [(first + parts * r, None)]:
            for part in range(parts):
                lo, hi = max(at, part * r), min(at + rows, (part + 1) * r)
                if lo < hi:
                    new = jnp.zeros((hi - lo, D), f32) if get is None else get(s, lo - at, hi - at)
                    ref[part, s, lo - part * r : hi - part * r] = new.astype(ref.dtype)
            at += rows


def write_halves(core, pieces, keep, give):
    half = keep.shape[0] * keep.shape[2]
    for mine in range(2):

        @pl.when(core == mine)
        def _(mine=mine):
            write_parts(pieces, mine * half, keep)
            write_parts(pieces, (1 - mine) * half, give)


def clear(*refs):
    for ref in refs:
        ref[...] = jnp.zeros_like(ref)


def first_step(fn):
    pl.when(pl.program_id(0) == 0)(fn)


def last_step(fn):
    pl.when(pl.program_id(0) == pl.num_programs(0) - 1)(fn)


def attn_fwd_kernel(place, x, *refs):
    own, near, far = refs[0:3], refs[3:6], refs[6:9]
    middle, packed, probs, mixed, value, wqkv, wm, sm, qkv, out, masks = refs[9:]

    @first_step
    def _():
        assemble_attn(0, place[0], place[1], own, near, far, wqkv, wm, sm)
        fill_head_masks(masks)
        project(x, wqkv, sm, qkv)

    crops = [pl.program_id(0) * STEP_CROPS + i for i in range(STEP_CROPS)]
    attend_crops(place, crops, range(STEP_CROPS), masks, qkv, packed, probs, out)

    @last_step
    def _():
        mix(out, qkv, (2, 5), sm, mixed)
        for orient in range(2):
            value[orient] = qkv[orient * 3 + 2, :ROWS, :].astype(bf16)
        mixer(x, mixed, wm, sm, middle)


def ff_fwd_kernel(place, middle, sm, *refs):
    own, near, far = refs[0:2], refs[2:5], refs[5:8]
    out, we, wr = refs[8:]

    @first_step
    def _():
        assemble_ff(0, place[0], place[1], own, near, far, we, wr)

    out[...] = ff_forward(middle[...], we, wr, sm)


def top_kernel(place, x, cotangent, *refs):
    attn_own, ff_own, rest = refs[0:3], refs[3:5], refs[5]
    (output, grad_out, grads) = refs[6:9]
    (wqkv, wm, sm, we, wr, qkv, out, packed, probs, mixed, middle, g, slope, dv,
     acc_e, acc_r, acc_q, acc_m, vec, masks) = refs[9:]

    assemble_top(place[0], attn_own, ff_own, rest, wqkv, wm, sm, we, wr)
    clear(acc_e, acc_r, acc_q, acc_m, vec)
    fill_head_masks(masks)
    project(x, wqkv, sm, qkv)

    def ahead(i, _):
        crops = [i * STEP_CROPS + j for j in range(STEP_CROPS)]
        attend_crops(place, crops, crops, masks, qkv, packed, probs, out)
        return 0

    lax.fori_loop(0, CROPS // STEP_CROPS, ahead, 0)
    mix(out, qkv, (2, 5), sm, mixed)
    mixer(x, mixed, wm, sm, middle)
    for rows in chunks():
        gs, slopes = {}, {}
        output[rows, :] = ff_forward(middle[rows, :], we, wr, sm, gs, slopes).astype(bf16)
        for s in range(4):
            g[rows, s * 256 : (s + 1) * 256] = gs[s]
            slope[rows, s * 256 : (s + 1) * 256] = slopes[s]
    for rows in chunks():
        held = lambda s: (g[rows, s * 256 : (s + 1) * 256], slope[rows, s * 256 : (s + 1) * 256])
        middle_here = middle[rows, :]
        middle[rows, :] = ff_backward(cotangent[rows, :].astype(f32), middle_here, we, wr, sm, acc_e, acc_r, vec, held)
    em, e_low = out, g.at[:, 0:768]

    def e_at(orient, p):
        return (dv, orient) if p == 2 else (qkv, orient * 3 + p)

    mixer_back(middle, mixed, wm, acc_m, vec, em)

    def behind(i, _):
        crops = [i * STEP_CROPS + j for j in range(STEP_CROPS)]
        attend_crops_back(crops, crops, masks, em, packed, probs, e_at)
        return 0

    lax.fori_loop(0, CROPS // STEP_CROPS, behind, 0)
    mix_back(em, qkv, (2, 5), sm, e_at, e_low, vec)
    project_back(middle, x, e_low, wqkv, sm, acc_q, vec, grad_out)
    write_parts(attn_pieces(acc_q, acc_m, jnp.sum(vec[...], axis=1)) + ff_pieces(acc_e, acc_r), 0, grads)


def ff_bwd_kernel(place, grad, middle, we, wr, sm, grad_mid, keep, give, vec, acc_e, acc_r):
    @first_step
    def _():
        clear(acc_e, acc_r, vec)

    grad_mid[...] = ff_backward(grad[...], middle[...], we, wr, sm, acc_e, acc_r, vec)

    @last_step
    def _():
        write_halves(place[1], ff_pieces(acc_e, acc_r), keep, give)


def attn_bwd_kernel(place, grad, x, packed, probs, mixed, value, wqkv, wm, sm, vec_in, patch_grad, keep, give, em, e, e_low, acc_q, acc_m, vec, masks):
    @first_step
    def _():
        fill_head_masks(masks)
        clear(acc_q, acc_m)
        vec[...] = vec_in[...]
        mixer_back(grad, mixed, wm, acc_m, vec, em)

    crops = [pl.program_id(0) * STEP_CROPS + i for i in range(STEP_CROPS)]
    attend_crops_back(crops, range(STEP_CROPS), masks, em, packed, probs, lambda orient, p: (e, orient * 3 + p))

    @last_step
    def _():
        mix_back(em, value, (0, 1), sm, lambda orient, p: (e, orient * 3 + p), e_low, vec)
        project_back(grad, x, e_low, wqkv, sm, acc_q, vec, patch_grad)
        write_halves(place[1], attn_pieces(acc_q, acc_m, jnp.sum(vec[...], axis=1)), keep, give)


def whole(shape):
    return pl.BlockSpec(shape, lambda i, *_: (0,) * len(shape))


def rows_of(lanes, rows=CHUNK):
    return pl.BlockSpec((rows, lanes), lambda i, *_: (i, 0))


def crop_spec(*dims):
    return pl.BlockSpec((STEP_CROPS,) + dims, lambda i, *_: (i,) + (0,) * len(dims))


def of_layer(layer, *dims):
    return pl.BlockSpec((1,) + dims, lambda i, *_: (layer,) + (0,) * len(dims))


def attn_specs(layer):
    return [of_layer(layer, 192, D), of_layer(layer, 64, D), whole((2, 32, D))]


def ff_specs(layer):
    return [of_layer(layer, D, D), of_layer(layer, 64, FF)]


def half_specs(rows):
    return [whole((rows, D))] * 6


def shape(dims, dtype=bf16):
    return jax.ShapeDtypeStruct(dims, dtype)


def far(dims, dtype=bf16):
    return pltpu.HBM(dims, dtype)


def params(micros, mib=16, grid=True):
    steps = dict(dimension_semantics=("arbitrary",)) if grid else {}
    return dict(
        compiler_params=pltpu.CompilerParams(vmem_limit_bytes=mib * 1024 * 1024, **steps),
        cost_estimate=pl.CostEstimate(flops=int(micros * 1e9), bytes_accessed=1 << 20, transcendentals=0),
    )


def held_call(kernel, name, place, arrays, outs, scratch, micros, mib):
    there = pl.BlockSpec(memory_space=pltpu.VMEM)
    return pl.pallas_call(
        kernel,
        in_specs=[pl.BlockSpec(memory_space=pltpu.SMEM)] + [there] * len(arrays),
        out_specs=[there] * len(outs),
        out_shape=[shape(dims, dtype) for dims, dtype in outs],
        scratch_shapes=list(scratch),
        name=name,
        **params(micros, mib, False),
    )(place, *arrays)


v = pltpu.VMEM


def attn_fwd_call(place, x, unit):
    rows = unit[-1].shape[0]
    return pl.pallas_call(
        attn_fwd_kernel,
        grid_spec=pltpu.PrefetchScalarGridSpec(
            num_scalar_prefetch=1,
            grid=(CROPS // STEP_CROPS,),
            in_specs=[whole((ROWS, D))] + attn_specs(0) + half_specs(rows),
            out_specs=[whole((ROWS, D)), crop_spec(2, 3, WIN, 256), crop_spec(2, 4 * WIN, 256), whole((ROWS, D)), whole((2, ROWS, 128)), whole((768, D)), whole((D, D)), whole((32, D))],
            scratch_shapes=[v((6, HELD, 128), f32), v((2, HELD, 128), f32), v((HALF_HEADS, WIN, 256), bf16)],
        ),
        out_shape=[far((ROWS, D), f32), far((CROPS, 2, 3, WIN, 256)), far((CROPS, 2, 4 * WIN, 256)), far((ROWS, D)), far((2, ROWS, 128)), far((768, D)), far((D, D)), shape((32, D), f32)],
        name="attn_fwd",
        **params(10, 20),
    )(place, x, *unit)


def ff_fwd_call(place, middle, sm, unit):
    return pl.pallas_call(
        ff_fwd_kernel,
        grid_spec=pltpu.PrefetchScalarGridSpec(
            num_scalar_prefetch=1,
            grid=(ROWS // CHUNK,),
            in_specs=[rows_of(D), whole((32, D))] + ff_specs(0) + half_specs(HALF_FF),
            out_specs=[rows_of(D), whole((4, D, D)), whole((D, FF))],
        ),
        out_shape=[shape((ROWS, D), f32), far((4, D, D)), far((D, FF))],
        name="ff_fwd",
        **params(6, 16),
    )(place, middle, sm, *unit)


def top_call(place, x, cotangent, weights, parts, r):
    scratch = [
                v((768, D), bf16), v((D, D), bf16), v((32, D), f32), v((4, D, D), bf16), v((D, FF), bf16),
                v((6, HELD, 128), f32), v((2, HELD, 128), f32), v((CROPS, 2, 3, WIN, 256), bf16), v((CROPS, 2, 4 * WIN, 256), bf16),
                v((ROWS, D), bf16), v((ROWS, D), f32), v((ROWS, FF), bf16), v((ROWS, FF), bf16),
                v((2, HELD, 128), f32),
                v((4, D, D), f32), v((4, D, D), f32), v((768, D), f32), v((D, D), f32), v((32, CROPS, D), f32), v((HALF_HEADS, WIN, 256), bf16),
    ]
    outs = [((ROWS, D), bf16), ((ROWS, D), f32), ((parts, 4, r, D), bf16)]
    return held_call(top_kernel, "top_block", place, [x, cotangent, *weights], outs, scratch, 30, 49)


def ff_bwd_call(place, grad, middle, we, wr, sm, parts, r):
    return pl.pallas_call(
        ff_bwd_kernel,
        grid_spec=pltpu.PrefetchScalarGridSpec(
            num_scalar_prefetch=1,
            grid=(ROWS // CHUNK,),
            in_specs=[rows_of(D), rows_of(D), whole((4, D, D)), whole((D, FF)), whole((32, D))],
            out_specs=[rows_of(D)] + [whole((parts, 4, r, D))] * 2 + [whole((32, CROPS, D))],
            scratch_shapes=[v((4, D, D), f32), v((4, D, D), f32)],
        ),
        out_shape=[shape((ROWS, D), f32)] + [shape((parts, 4, r, D))] * 2 + [shape((32, CROPS, D), f32)],
        name="ff_bwd",
        **params(10, 20),
    )(place, grad, middle, we, wr, sm)


def attn_bwd_call(place, grad, x, packed, probs, mixed, value, wqkv, wm, sm, vec):
    return pl.pallas_call(
        attn_bwd_kernel,
        grid_spec=pltpu.PrefetchScalarGridSpec(
            num_scalar_prefetch=1,
            grid=(CROPS // STEP_CROPS,),
            in_specs=[whole((ROWS, D)), whole((ROWS, D)), crop_spec(2, 3, WIN, 256), crop_spec(2, 4 * WIN, 256), whole((ROWS, D)), whole((2, ROWS, 128)), whole((768, D)), whole((D, D)), whole((32, D)), whole((32, CROPS, D))],
            out_specs=[whole((ROWS, D))] + [whole((1, 4, LOW_ROWS // 2, D))] * 2,
            scratch_shapes=[v((2, HELD, 128), f32), v((6, HELD, 128), f32), v((ROWS, 768), bf16), v((768, D), f32), v((D, D), f32), v((32, CROPS, D), f32), v((HALF_HEADS, WIN, 256), bf16)],
        ),
        out_shape=[shape((ROWS, D))] + [shape((1, 4, LOW_ROWS // 2, D))] * 2,
        name="attn_bwd",
        **params(16, 36),
    )(place, grad, x, packed, probs, mixed, value, wqkv, wm, sm, vec)


def to_rows(x):
    return jnp.transpose(x, (1, 2, 0, 3)).reshape(ROWS, D)


def from_rows(x):
    return jnp.transpose(x.reshape(GRID, GRID, CROPS, D), (2, 0, 1, 3))


def pack_kernel(place, qkv, mixer_t, gain, shift, entry, taps, branch, hidden_bias, expand, reduce_t, half_a, half_f, vec, unit):
    me, core = place[0], place[1]
    lane = lax.broadcasted_iota(jnp.int32, (18, D), 1)
    row = lax.broadcasted_iota(jnp.int32, (14, D), 0)
    for layer in range(2):
        rows = jnp.concatenate(
            [ref[layer].astype(f32) for ref in (gain, shift, entry)] + [taps[:, layer].astype(f32), branch[layer].astype(f32)], axis=0
        )
        vectors = jnp.where(lane // 64 == me, jnp.concatenate([rows] * 4, axis=1), 0.0)
        hidden_rows = jnp.where(row == me, hidden_bias[layer : layer + 1].astype(f32), 0.0)
        vec[layer] = jnp.concatenate([vectors, hidden_rows], axis=0).astype(bf16)
    half_a[0:96] = qkv[0, pl.ds(pl.multiple_of(96 * core, 32), 96)]
    half_a[96:128] = mixer_t[0, pl.ds(pl.multiple_of(32 * core, 32), 32)]
    half_a[128:144] = vec[0, pl.ds(pl.multiple_of(16 * core, 16), 16)]
    half_f[0:128] = expand[0, pl.ds(pl.multiple_of(128 * core, 128), 128)]
    for c in range(4):
        half_f[128 + 32 * c : 160 + 32 * c] = reduce_t[0, pl.ds(pl.multiple_of(32 * core, 32), 32), c * 256 : (c + 1) * 256]
    unit[0:192] = qkv[1]
    unit[192:256] = mixer_t[1]
    unit[256:288] = vec[1]
    unit[288:544] = expand[1]
    for c in range(4):
        unit[544 + 64 * c : 608 + 64 * c] = reduce_t[1, :, c * 256 : (c + 1) * 256]
    if unit.shape[0] > UNIT:
        unit[UNIT:] = jnp.zeros((unit.shape[0] - UNIT, D), bf16)
    r = half_a.shape[0] - HALF_ATTN
    half_a[HALF_ATTN:] = unit[pl.ds(pl.multiple_of(place[3] * r, 16), r)]


def local_call(kernel, name, place, arrays, outs, scratch=()):
    return pl.pallas_call(
        kernel,
        grid_spec=pltpu.PrefetchScalarGridSpec(
            num_scalar_prefetch=1,
            grid=(1,),
            in_specs=[whole(x.shape) for x in arrays],
            out_specs=[whole(dims) for dims, _ in outs],
            scratch_shapes=list(scratch),
        ),
        out_shape=[shape(dims, dtype) for dims, dtype in outs],
        name=name,
        **params(1, 58),
    )(place, *arrays)


def turn_mp(x, k):
    n = lax.axis_size("mp")
    return lax.ppermute(x, "mp", [(i, (i + k) % n) for i in range(n)])


def swap_dp(x, bits):
    n = lax.axis_size("dp")
    return lax.ppermute(x, "dp", [(i, i ^ bits) for i in range(n)])


def turn_all(x):
    return [turn_mp(x, k) for k in (1, 2, 3)]


def swap_core(xs):
    return [swap_dp(x, 1) for x in xs]


def pick(x, at):
    return lax.dynamic_index_in_dim(x, at, 0, keepdims=False)


def add_up(xs):
    total = xs[0].astype(f32)
    for x in xs[1:]:
        total = total + x.astype(f32)
    return total


def to_planes(keep, got, at):
    total = add_up([keep, got]).astype(bf16)
    return [pick(total, at ^ b) for b in range(keep.shape[0])]


def swap_planes(parts):
    return [parts[0]] + [swap_dp(part, 2 * b) for b, part in enumerate(parts) if b]


def to_shards(xs, me):
    total = add_up(xs)
    low = total.astype(bf16)
    return [pick(total, me)] + [pick(low, (me + k) % 4) for k in (1, 2, 3)]


def turn_shards(parts):
    return [parts[0]] + [turn_mp(part, k) for k, part in enumerate(parts) if k]


def unpack_kernel(planes, cut_f, cut_t, place, *refs):
    mine, other = refs[:planes], refs[planes : 2 * planes]
    packed, mixer_g, expand, reduce_g, gain, shift, entry, taps, branch, hidden_g, held, held_t = refs[2 * planes :]
    me, core = place[0], place[1]
    r_f, r_t = cut_t - cut_f, mine[0].shape[0] - cut_t
    for which, parts in ((core, mine), (1 - core, other)):
        total = parts[0][:cut_f].astype(f32)
        for part in parts[1:]:
            total = total + part[:cut_f].astype(f32)
        held[which, :cut_f] = total
        for b in range(planes):
            at = place[2] ^ b
            held[which, pl.ds(pl.multiple_of(cut_f + at * r_f, 16), r_f)] = parts[b][cut_f:cut_t].astype(f32)
            held_t[pl.ds(pl.multiple_of((2 * at + which) * r_t, 16), r_t)] = parts[b][cut_t:].astype(f32)

    def rows(which, lo, hi):
        if which is None:
            return held_t[lo:hi]
        start, half = which
        out = []
        for c in range(2):
            a, b = max(lo, c * half), min(hi, (c + 1) * half)
            if a < b:
                out.append(held[c, start + a - c * half : start + b - c * half])
        return out[0] if len(out) == 1 else jnp.concatenate(out, axis=0)

    low_a, low_f = (0, cut_f), (cut_f, planes * r_f)
    for layer, attn, ff, ff_at in ((0, low_a, low_f, 0), (1, None, None, 288)):
        packed[layer] = rows(attn, 0, 192)
        mixer_g[layer] = rows(attn, 192, 256)
        expand[layer] = rows(ff, ff_at, ff_at + 256)
        for c in range(4):
            at = ff_at + 256 + 64 * c
            reduce_g[layer, :, c * 256 : (c + 1) * 256] = rows(ff, at, at + 64)
        vectors = rows(attn, 256, 288)
        mine_lanes = vectors[:, :64]
        for s in range(1, 4):
            mine_lanes = jnp.where(me == s, vectors[:, 64 * s : 64 * (s + 1)], mine_lanes)
        gain[layer] = mine_lanes[GAIN : GAIN + 2]
        shift[layer] = mine_lanes[SHIFT : SHIFT + 2]
        entry[layer] = mine_lanes[ENTRY : ENTRY + 2]
        branch[layer] = mine_lanes[BRANCH : BRANCH + 2]
        for t in range(10):
            taps[t, layer : layer + 1] = mine_lanes[TAPS + t : TAPS + t + 1]
        row = vectors[HIDDEN : HIDDEN + 1]
        for s in range(1, 4):
            row = jnp.where(me == s, vectors[HIDDEN + s : HIDDEN + s + 1], row)
        hidden_g[layer : layer + 1] = row


def body(patches, validity, norm_gain, norm_shift, qkv_weight, entry_bias, stencil, mixer_weight, branch_bias, expand_weight, hidden_bias, reduce_weight, cotangent):
    dp = lax.axis_size("dp")
    planes = dp // 2
    me, at_dp = lax.axis_index("mp"), lax.axis_index("dp")
    heights = jnp.sum(validity[:, :, 0], axis=1)
    widths = jnp.sum(validity[:, 0, :], axis=1)
    place = jnp.stack([me, at_dp % 2, at_dp // 2, at_dp]).astype(jnp.int32)
    sizes = jnp.concatenate([jnp.stack([me, at_dp % 2]), jnp.stack([heights, widths], axis=1).reshape(-1)]).astype(jnp.int32)

    qkv_t = jnp.transpose(qkv_weight, (0, 2, 3, 1)).reshape(2, 192, D)
    mixer_t = jnp.transpose(mixer_weight, (0, 2, 1))
    reduce_t = jnp.transpose(reduce_weight, (0, 2, 1))
    vectors = (norm_gain, norm_shift, entry_bias, jnp.transpose(stencil, (1, 0, 2)), branch_bias, hidden_bias)

    arrays = [qkv_t, mixer_t, norm_gain, norm_shift, entry_bias, jnp.transpose(stencil, (1, 0, 2)), branch_bias, hidden_bias, expand_weight, reduce_t]
    r_t, r_f = part_rows(UNIT, dp), part_rows(FF_ROWS, dp)
    outs = [(HALF_ATTN + r_t, D), (HALF_FF, D), (2, 32, D)]
    half_a0, half_f0, vec = local_call(
        pack_kernel, "pack", place, arrays, [(dims, bf16) for dims in outs], [v((dp * r_t, D), bf16)]
    )
    attn_own, ff_own = [qkv_t, mixer_t, vec], [expand_weight, reduce_t]

    near_a0 = turn_all(half_a0)
    near_1 = jnp.stack([x[HALF_ATTN:] for x in near_a0])
    near_f0 = turn_all(half_f0)
    far_a0 = swap_core(near_a0)
    x, top_grad = to_rows(patches), to_rows(cotangent)
    near_1, x = lax.optimization_barrier((near_1, x))
    rest_1 = lax.all_gather(near_1, "dp", axis=0, tiled=False)
    middle, packed, probs, mixed, value, wqkv, wm, sm = attn_fwd_call(sizes, x, attn_own + near_a0 + far_a0)
    near_f0, middle = lax.optimization_barrier((near_f0, middle))
    far_f0 = swap_core(near_f0)
    state, we, wr = ff_fwd_call(sizes, middle, sm, ff_own + near_f0 + far_f0)
    output, grad, grads_1 = top_call(sizes, state, top_grad, attn_own + ff_own + [rest_1], dp, r_t)
    sums_1 = lax.psum_scatter(grads_1, "dp", scatter_dimension=0, tiled=False)

    grad_mid, keep_f, give_f, vec = ff_bwd_call(place, grad, middle, we, wr, sm, planes, r_f)
    got_f = swap_dp(give_f, 1)
    patch_grad, keep_a, give_a = attn_bwd_call(place, grad_mid, x, packed, probs, mixed, value, wqkv, wm, sm, vec)
    got_f, keep_a, give_a = lax.optimization_barrier((got_f, keep_a, give_a))

    got_a = swap_dp(give_a, 1)
    planes_f = swap_planes(to_planes(keep_f, got_f, place[2]))
    shards_a = to_shards([keep_a[0], got_a[0]], me)
    mp_a = turn_shards(shards_a)
    planes_f, sums_1 = lax.optimization_barrier((planes_f, sums_1, shards_a))[:2]
    low = add_up(planes_f).astype(bf16)
    mp_f = turn_shards(to_shards([jnp.concatenate([low, sums_1], axis=1)], me))
    share = jnp.concatenate([add_up(mp_a), add_up(mp_f)], axis=0).astype(bf16)
    mine = swap_planes([share] * planes)
    other = swap_core(mine)
    outs = [(2, 192, D), (2, 64, D), (2, D, D), (2, 64, FF), (2, 2, 64), (2, 2, 64), (2, 2, 64), (10, 2, 64), (2, 2, 64), (2, D)]
    cut_f = LOW_ROWS // 2
    cut_t = cut_f + r_f
    held = [v((2, cut_f + planes * r_f, D), f32), v((dp * r_t, D), f32)]
    packed_g, mixer_g, expand_g, reduce_g, gain_g, shift_g, entry_g, taps_g, branch_g, hidden_g = held_call(
        functools.partial(unpack_kernel, planes, cut_f, cut_t), "unpack", place, mine + other, [(dims, f32) for dims in outs], held, 2, 16
    )
    return (
        from_rows(output), from_rows(patch_grad), gain_g, shift_g,
        jnp.transpose(packed_g.reshape(2, 3, 64, D), (0, 3, 1, 2)), entry_g, jnp.transpose(taps_g, (1, 0, 2)),
        jnp.transpose(mixer_g, (0, 2, 1)), branch_g, expand_g, hidden_g, jnp.transpose(reduce_g, (0, 2, 1)),
    )


def solution(mesh):
    crops = P(("dp", "mp"), None, None, None)
    lanes = P(None, None, "mp")
    deep = P(None, None, None, "mp")
    return jax.shard_map(
        body,
        mesh=mesh,
        in_specs=(crops, P(("dp", "mp"), None, None), lanes, lanes, deep, lanes, lanes, lanes, lanes, lanes, P(None, "mp"), lanes, crops),
        out_specs=(crops, crops, lanes, lanes, deep, lanes, lanes, lanes, lanes, lanes, P(None, "mp"), lanes),
        check_vma=False,
    )
```

```python
import functools

import jax
import jax.numpy as jnp
from jax import lax
from jax.experimental import pallas as pl
from jax.experimental.pallas import tpu as pltpu
from jax.sharding import PartitionSpec as P

GRID = 14
STRIPE = 7
CELLS = GRID * GRID
CROPS = 8
ROWS = CELLS * CROPS
LINE = GRID * CROPS
HELD = ROWS + 112
WIN = 112
HALF_HEADS = 4
HEAD = 32
D = 256
FF = 1024
STEP_CROPS = 2
CHUNK = 784

norm_eps = 1e-05
masked_score = -1e30
root_half = 0.7071067811865476
inverse_root_tau = 0.3989422804014327
log2_e = 1.4426950408889634
factor = HEAD**-0.5

f32 = jnp.float32
bf16 = jnp.bfloat16

HALF_ATTN = 144
HALF_FF = 256
FF_ROWS = 512
UNIT = 800
LOW_ROWS = 288
GAIN, SHIFT, ENTRY, TAPS, BRANCH, HIDDEN = 0, 2, 4, 6, 16, 18


def dot(a, b):
    return lax.dot_general(a, b, (((1,), (0,)), ((), ())), preferred_element_type=f32)


def dot_nt(a, b):
    return lax.dot_general(a, b, (((1,), (1,)), ((), ())), preferred_element_type=f32)


def dot_tn(a, b):
    return lax.dot_general(a, b, (((0,), (0,)), ((), ())), preferred_element_type=f32)


def norm(x):
    center = x - jnp.mean(x, axis=-1, keepdims=True)
    spread = jnp.mean(center * center, axis=-1, keepdims=True)
    inverse = lax.rsqrt(spread + norm_eps)
    return center * inverse, inverse


def norm_back(grad, normal, inverse, gain):
    scaled = grad * gain
    return inverse * (
        scaled
        - jnp.mean(scaled, axis=-1, keepdims=True)
        - normal * jnp.mean(scaled * normal, axis=-1, keepdims=True)
    )


def column_sum(x):
    return jnp.sum(x.reshape(x.shape[0] // CROPS, CROPS, x.shape[1]), axis=0)


def window_row_inside(orient):
    row = lax.broadcasted_iota(jnp.int32, (WIN, 128), 0)
    return row < 98 if orient == 0 else row % 8 < STRIPE


def key_bias(orient, window, height, width):
    row = lax.broadcasted_iota(jnp.int32, (WIN, 128), 0)
    if orient == 0:
        line, column = row // GRID + window * STRIPE, row % GRID
    else:
        line, column = row // 8, row % 8 + window * STRIPE
    valid = window_row_inside(orient) & (line < height) & (column < width)
    return jnp.where(valid, 0.0, masked_score)


def load_window(ref, block, crop, orient, window):
    if orient == 0:
        return ref[block, pl.ds(98 * CROPS * window + crop, WIN, stride=CROPS), :]
    parts = [
        ref[block, pl.ds((line * GRID + window * STRIPE) * CROPS + crop, 8, stride=CROPS), :]
        for line in range(GRID)
    ]
    return jnp.concatenate(parts, axis=0)


def store_window(ref, block, crop, orient, window, x):
    if orient == 0:
        ref[block, pl.ds(98 * CROPS * window + crop, 98, stride=CROPS), :] = x[:98]
        return
    for line in range(GRID):
        at = (line * GRID + window * STRIPE) * CROPS + crop
        ref[block, pl.ds(at, STRIPE, stride=CROPS), :] = x[line * 8 : line * 8 + STRIPE]


def fill_head_masks(masks):
    lane = lax.broadcasted_iota(jnp.int32, (WIN, 256), 1) % 128 // HEAD
    for head in range(HALF_HEADS):
        masks[head] = jnp.where(lane == head, 1.0, 0.0).astype(bf16)


def heads_down(x, masks):
    return jnp.concatenate([x * masks[head] for head in range(HALF_HEADS)], axis=0)


def fold_heads(x):
    head = lax.broadcasted_iota(jnp.int32, (WIN, 256), 1) % 128 // HEAD
    parts = [x[h * WIN : (h + 1) * WIN] for h in range(HALF_HEADS)]
    low, high = jnp.where(head == 0, parts[0], parts[1]), jnp.where(head == 2, parts[2], parts[3])
    return jnp.where(head < 2, low, high)


def windows_apart(x):
    none, rest = jnp.zeros((WIN, 128), x.dtype), jnp.zeros((128 - WIN, 256), x.dtype)
    first = jnp.concatenate([x[:, :128], none], axis=1)
    second = jnp.concatenate([none, x[:, 128:]], axis=1)
    return jnp.concatenate([first, rest, second, rest], axis=0)


def by_head(turned, probs):
    parts = []
    for head in range(HALF_HEADS):
        left = jnp.concatenate([turned[w * 128 + head * HEAD : w * 128 + (head + 1) * HEAD] for w in range(2)], axis=0)
        both = dot(left, probs[head * WIN : (head + 1) * WIN])
        parts.append((both[:HEAD, :128], both[HEAD:, 128:]))
    return [jnp.concatenate([part[w] for part in parts], axis=0).T[:WIN] for w in range(2)]


def head_probs(scores, bias):
    scores = scores * (factor * log2_e) + bias
    raised = jnp.exp2(scores - jnp.max(scores, axis=0, keepdims=True))
    return (raised * (1.0 / jnp.sum(raised, axis=0, keepdims=True))).astype(bf16)


def head_grad_scores(grad_probs, probs):
    wide = probs.astype(f32)
    inner = jnp.sum(grad_probs * wide, axis=0, keepdims=True)
    return (wide * (grad_probs - inner)).astype(bf16)


def each_head(fn, *arrays):
    parts = [fn(*(x[h * WIN : (h + 1) * WIN] for x in arrays)) for h in range(HALF_HEADS)]
    return jnp.concatenate(parts, axis=0)


def attend(queries, keys, values, biases, masks):
    apart = [windows_apart(x.astype(bf16)) for x in queries]
    scores = [dot_nt(heads_down(k.astype(bf16), masks), q) for k, q in zip(keys, apart)]
    value_turned = [x.T.astype(bf16) for x in values]
    probs = [each_head(lambda s, b=b: head_probs(s, b), s) for s, b in zip(scores, biases)]
    return [by_head(v, p) for v, p in zip(value_turned, probs)], probs


def attend_back(grads, queries, keys, values, probs, masks):
    grad_apart = [windows_apart(x) for x in grads]
    grad_probs = [dot_nt(heads_down(v, masks), g) for v, g in zip(values, grad_apart)]
    key_turned = [x.astype(f32).T.astype(bf16) for x in keys]
    grad_value = [fold_heads(dot(p, g)) for p, g in zip(probs, grad_apart)]
    grad_scores = [each_head(head_grad_scores, g, p) for g, p in zip(grad_probs, probs)]
    apart = [windows_apart(x) for x in queries]
    grad_key = [fold_heads(dot(s, q)) * factor for s, q in zip(grad_scores, apart)]
    grad_query = [[x * factor for x in by_head(k, s)] for k, s in zip(key_turned, grad_scores)]
    return grad_query, grad_key, grad_value


def steps_along(x, orient):
    zero = jnp.zeros((CROPS, x.shape[1]), x.dtype)
    if orient == 0:
        return {-1: jnp.concatenate([zero, x[:-CROPS]], axis=0), 0: x, 1: jnp.concatenate([x[CROPS:], zero], axis=0)}
    half = LINE // 2
    left, right = x[:half], x[half:]
    return {
        -1: jnp.concatenate([zero, left[:-CROPS], zero, right[:-CROPS]], axis=0),
        0: x,
        1: jnp.concatenate([left[CROPS:], zero, right[CROPS:], zero], axis=0),
    }


def line_reaches(line, step, orient):
    if step == 0:
        return None
    stops = (GRID, STRIPE) if orient == 0 else (GRID,)
    edges = [(stop - 1) if step == 1 else (stop % GRID) for stop in stops]
    ok = line != edges[0]
    for edge in edges[1:]:
        ok = ok & (line != edge)
    return jnp.where(ok, 1.0, 0.0).astype(f32)


def line_at(ref, block, line):
    held = jnp.clip(line, 0, GRID - 1)
    return ref[block, pl.ds(pl.multiple_of(held * LINE, LINE), LINE), :]


def stencil_line(ref, block, taps, line, orient, back):
    total = None
    for step in (-1, 0, 1):
        moved = steps_along(line_at(ref, block, line + (-step if back else step)).astype(f32), orient)
        reach = line_reaches(line, -step if back else step, orient)
        for side in (-1, 0, 1):
            tap = taps[3 * (step + 1) + side + 1]
            if reach is not None:
                tap = tap * reach
            term = moved[-side if back else side] * tap
            total = term if total is None else total + term
    return total


def stencil_line_taps(ref, block, grad, line, orient):
    sums = []
    for step in (-1, 0, 1):
        moved = steps_along(line_at(ref, block, line + step).astype(f32), orient)
        reach = line_reaches(line, step, orient)
        for side in (-1, 0, 1):
            part = column_sum(grad * moved[side])
            sums.append(part if reach is None else part * reach)
    sums.append(column_sum(grad))
    return sums


def assemble_attn(layer, me, core, own, near, far, wqkv, wm, sm):
    qkv, mixer_t, vec = own

    def put(shard, blocks, at, mixer_rows, mixer_at):
        orient, part = lax.div(shard, 2), lax.rem(shard, 2)
        for i, block in enumerate(blocks):
            j = at + i
            row = orient * 384 + lax.div(j, 2) * 128 + part * 64 + lax.rem(j, 2) * 32
            wqkv[pl.ds(pl.multiple_of(row, 32), 32), :] = block
        wm[pl.ds(pl.multiple_of(shard * 64 + mixer_at, 32), mixer_rows.shape[0]), :] = mixer_rows

    put(me, [qkv[0, 32 * i : 32 * (i + 1)] for i in range(6)], jnp.int32(0), mixer_t[0], 0)
    sm[...] = vec[layer].astype(f32)
    for halves, which in ((near, core), (far, 1 - core)):
        for k, half in enumerate(halves, 1):
            shard = lax.rem(me + 4 - k, 4)
            put(shard, [half[32 * i : 32 * (i + 1)] for i in range(3)], 3 * which, half[96:128], 32 * which)
            sm[pl.ds(pl.multiple_of(16 * which, 16), 16), :] += half[128:144].astype(f32)


def assemble_ff(first, me, core, own, near, far, we, wr):
    expand, reduce_t = own
    we[me] = expand[0]
    wr[pl.ds(pl.multiple_of(me * 64, 64), 64), :] = reduce_t[0]
    for halves, which in ((near, core), (far, 1 - core)):
        for k, half in enumerate(halves, 1):
            shard = lax.rem(me + 4 - k, 4)
            we[shard, pl.ds(pl.multiple_of(128 * which, 128), 128), :] = half[first : first + 128]
            row = pl.multiple_of(shard * 64 + 32 * which, 32)
            for c in range(4):
                at = first + 128 + 32 * c
                wr[pl.ds(row, 32), c * 256 : (c + 1) * 256] = half[at : at + 32]


def assemble_top(me, attn_own, ff_own, rest, wqkv, wm, sm, we, wr):
    qkv, mixer_t, vec = attn_own
    expand, reduce_t = ff_own

    def put(shard, row, value):
        orient, part = lax.div(shard, 2), lax.rem(shard, 2)
        n = value.shape[0]
        if row < 192:
            at = orient * 384 + row // 64 * 128 + part * 64 + row % 64
            wqkv[pl.ds(pl.multiple_of(at, 16), n), :] = value
        elif row < 256:
            wm[pl.ds(pl.multiple_of(shard * 64 + row - 192, 16), n), :] = value
        elif row < 288:
            sm[row - 256 : row - 256 + n, :] += value.astype(f32)
        elif row < 544:
            we[shard, row - 288 : row - 288 + n, :] = value
        else:
            c, at = divmod(row - 544, 64)
            wr[pl.ds(pl.multiple_of(shard * 64 + at, 16), n), c * 256 : (c + 1) * 256] = value

    for p in range(3):
        put(me, 64 * p, qkv[1, 64 * p : 64 * (p + 1)])
    put(me, 192, mixer_t[1])
    sm[...] = vec[1].astype(f32)
    put(me, 288, expand[1])
    for c in range(4):
        put(me, 544 + 64 * c, reduce_t[1, :, c * 256 : (c + 1) * 256])
    dp, _, r, _ = rest.shape
    edges = list(range(0, 257, 64)) + [288] + [544 + 64 * c for c in range(5)]
    for k in range(3):
        shard = lax.rem(me + 3 - k, 4)
        for d in range(dp):
            for lo, hi in zip(edges[:-1], edges[1:]):
                a, b = max(lo, d * r), min(hi, (d + 1) * r)
                if a < b:
                    put(shard, a, rest[d, k, a - d * r : b - d * r])


def chunks():
    return [slice(at, at + CHUNK) for at in range(0, ROWS, CHUNK)]


def put_blocks(ref, rows, x):
    for block in range(x.shape[1] // 128):
        ref[block, rows, :] = x[:, block * 128 : (block + 1) * 128]


def project(x, wqkv, sm, qkv):
    zero = jnp.zeros((1, 128), f32)
    query_bias, value_bias = sm[ENTRY : ENTRY + 1], sm[ENTRY + 1 : ENTRY + 2]
    bias = jnp.concatenate(
        [query_bias[:, :128], zero, value_bias[:, :128], query_bias[:, 128:], zero, value_bias[:, 128:]], axis=1
    )
    for rows in chunks():
        normal, _ = norm(x[rows, :].astype(f32))
        a = (normal * sm[GAIN : GAIN + 1] + sm[SHIFT : SHIFT + 1]).astype(bf16)
        put_blocks(qkv, rows, dot_nt(a, wqkv[...]) + bias)
    qkv[:, ROWS:HELD, :] = jnp.zeros((6, HELD - ROWS, 128), f32)


def load_pair(ref, block, crop, orient):
    return jnp.concatenate([load_window(ref, block, crop, orient, window) for window in range(2)], axis=1)


def attend_crops(place, crops, slots, masks, qkv, packed, probs_ref, out):
    at, lists = [], ([], [], [], [])
    for crop, slot in zip(crops, slots):
        height, width = place[2 + 2 * crop], place[3 + 2 * crop]
        for orient in range(2):
            three = [load_pair(qkv, orient * 3 + p, crop, orient) for p in range(3)]
            for p, x in enumerate(three):
                packed[slot, orient, p] = x.astype(bf16)
            bias = jnp.concatenate([key_bias(orient, window, height, width) for window in range(2)], axis=1)
            for held, new in zip(lists, (*three, bias)):
                held.append(new)
            at.append((crop, slot, orient))
    outs, probs = attend(*lists, masks)
    for (crop, slot, orient), both, p in zip(at, outs, probs):
        probs_ref[slot, orient] = p
        for window in range(2):
            store_window(out, orient, crop, orient, window, both[window])


def attend_crops_back(crops, slots, masks, em, packed, probs_ref, e_at):
    at, lists = [], ([], [], [], [], [])
    for crop, slot in zip(crops, slots):
        for orient in range(2):
            inside = jnp.concatenate([window_row_inside(orient)] * 2, axis=1)
            grad = jnp.where(inside, load_pair(em, orient, crop, orient), 0.0).astype(bf16)
            for held, new in zip(lists, (grad, *(packed[slot, orient, p] for p in range(3)), probs_ref[slot, orient])):
                held.append(new)
            at.append((crop, orient))
    for (crop, orient), dq, dk, dv in zip(at, *attend_back(*lists, masks)):
        for window in range(2):
            lanes = slice(window * 128, (window + 1) * 128)
            for p, part in enumerate((dq[window], dk[:, lanes], dv[:, lanes])):
                store_window(*e_at(orient, p), crop, orient, window, part)


def taps_of(sm, orient):
    lanes = slice(orient * 128, (orient + 1) * 128)
    return [sm[TAPS + t : TAPS + t + 1, lanes] for t in range(10)]


def mix(out, value, value_at, sm, mixed):
    taps = [taps_of(sm, orient) for orient in range(2)]

    def line(i, _):
        rows = pl.ds(pl.multiple_of(i * LINE, LINE), LINE)
        for orient in range(2):
            e_v = stencil_line(value, value_at[orient], taps[orient], i, orient, False) + taps[orient][9]
            mixed[rows, orient * 128 : (orient + 1) * 128] = (out[orient, rows, :] + e_v).astype(bf16)
        return 0

    lax.fori_loop(0, GRID, line, 0)


def mixer(x, mixed, wm, sm, *outs):
    for rows in chunks():
        middle = x[rows, :].astype(f32) + (dot_nt(mixed[rows, :], wm[...]) + sm[BRANCH : BRANCH + 1])
        for out in outs:
            out[rows, :] = middle


def hidden(a2, we, sm, s):
    u = dot(a2, we[s]) + sm[HIDDEN + s : HIDDEN + s + 1]
    phi = 0.5 + 0.5 * lax.erf(u * root_half)
    return u, phi


def slope_of(u, phi):
    return phi + u * jnp.exp(-0.5 * u * u) * inverse_root_tau


def second_norm(middle, sm):
    normal, inverse = norm(middle)
    a2 = (normal * sm[GAIN + 1 : GAIN + 2] + sm[SHIFT + 1 : SHIFT + 2]).astype(bf16)
    return normal, inverse, a2


def ff_forward(middle, we, wr, sm, g_out=None, slope_out=None):
    _, _, a2 = second_norm(middle, sm)
    gs = []
    for s in range(4):
        u, phi = hidden(a2, we, sm, s)
        gs.append((u * phi).astype(bf16))
        if g_out is not None:
            g_out[s], slope_out[s] = gs[-1], slope_of(u, phi).astype(bf16)
    return middle + (dot_nt(jnp.concatenate(gs, axis=1), wr[...]) + sm[BRANCH + 1 : BRANCH + 2])


def ff_backward(grad, middle, we, wr, sm, acc_e, acc_r, vec, held=None):
    ey = grad.astype(bf16)
    vec[BRANCH + 1] += column_sum(grad)
    normal, inverse, a2 = second_norm(middle, sm)
    eus = []
    for s in range(4):
        if held is None:
            u, phi = hidden(a2, we, sm, s)
            g, slope = (u * phi).astype(bf16), slope_of(u, phi)
        else:
            g, slope = held(s)
        acc_r[s] += dot_tn(ey, g)
        eu_wide = dot(ey, wr[:, s * 256 : (s + 1) * 256]) * slope.astype(f32)
        vec[HIDDEN + s] += column_sum(eu_wide)
        eu = eu_wide.astype(bf16)
        acc_e[s] += dot_tn(a2, eu)
        eus.append(eu)
    back = None
    for s in range(4):
        term = dot_nt(eus[s], we[s])
        back = term if back is None else back + term
    vec[GAIN + 1] += column_sum(back * normal)
    vec[SHIFT + 1] += column_sum(back)
    return grad + norm_back(back, normal, inverse, sm[GAIN + 1 : GAIN + 2])


def mixer_back(grad, mixed, wm, acc_m, vec, em):
    for rows in chunks():
        here = grad[rows, :]
        eo = here.astype(bf16)
        vec[BRANCH] += column_sum(here)
        acc_m[...] += dot_tn(eo, mixed[rows, :])
        put_blocks(em, rows, dot(eo, wm[...]))
    em[:, ROWS:HELD, :] = jnp.zeros((2, HELD - ROWS, 128), f32)


def mix_back(em, value, value_at, sm, e_at, e_low, vec):
    taps = [taps_of(sm, orient) for orient in range(2)]

    def line(i, _):
        rows = pl.ds(pl.multiple_of(i * LINE, LINE), LINE)
        for orient in range(2):
            lanes = slice(orient * 128, (orient + 1) * 128)
            base = orient * 384
            eq, ek, ev = [ref[block, rows, :] for ref, block in (e_at(orient, p) for p in range(3))]
            ev = ev + stencil_line(em, orient, taps[orient], i, orient, True)
            e_low[rows, base : base + 384] = jnp.concatenate([eq, ek, ev], axis=1).astype(bf16)
            vec[ENTRY, :, lanes] += column_sum(eq)
            vec[ENTRY + 1, :, lanes] += column_sum(ev)
            for t, part in enumerate(stencil_line_taps(value, value_at[orient], em[orient, rows, :], i, orient)):
                vec[TAPS + t, :, lanes] += part
        return 0

    lax.fori_loop(0, GRID, line, 0)


def project_back(grad, x, e_low, wqkv, sm, acc_q, vec, out):
    for rows in chunks():
        normal, inverse = norm(x[rows, :].astype(f32))
        a = (normal * sm[GAIN : GAIN + 1] + sm[SHIFT : SHIFT + 1]).astype(bf16)
        e = e_low[rows, :]
        acc_q[...] += dot_tn(e, a)
        back = dot(e, wqkv[...])
        vec[GAIN] += column_sum(back * normal)
        vec[SHIFT] += column_sum(back)
        out[rows, :] = (grad[rows, :] + norm_back(back, normal, inverse, sm[GAIN : GAIN + 1])).astype(out.dtype)


def attn_pieces(acc_q, acc_m, sums):
    def qkv(s, p, lo, hi):
        at = (s // 2) * 384 + p * 128 + (s % 2) * 64
        return acc_q[at + lo : at + hi]

    return [(64, lambda s, lo, hi, p=p: qkv(s, p, lo, hi)) for p in range(3)] + [
        (64, lambda s, lo, hi: acc_m[64 * s + lo : 64 * s + hi]),
        (32, lambda s, lo, hi: sums[lo:hi]),
    ]


def ff_pieces(acc_e, acc_r):
    return [(256, lambda s, lo, hi: acc_e[s, lo:hi])] + [
        (64, lambda s, lo, hi, c=c: acc_r[c, 64 * s + lo : 64 * s + hi]) for c in range(4)
    ]


def part_rows(rows, parts):
    return -(-rows // (16 * parts)) * 16


def write_parts(pieces, first, ref):
    parts, _, r, _ = ref.shape
    for s in range(4):
        at = -first
        for rows, get in pieces + [(first + parts * r, None)]:
            for part in range(parts):
                lo, hi = max(at, part * r), min(at + rows, (part + 1) * r)
                if lo < hi:
                    new = jnp.zeros((hi - lo, D), f32) if get is None else get(s, lo - at, hi - at)
                    ref[part, s, lo - part * r : hi - part * r] = new.astype(ref.dtype)
            at += rows


def write_halves(core, pieces, keep, give):
    half = keep.shape[0] * keep.shape[2]
    for mine in range(2):

        @pl.when(core == mine)
        def _(mine=mine):
            write_parts(pieces, mine * half, keep)
            write_parts(pieces, (1 - mine) * half, give)


def clear(*refs):
    for ref in refs:
        ref[...] = jnp.zeros_like(ref)


def first_step(fn):
    pl.when(pl.program_id(0) == 0)(fn)


def last_step(fn):
    pl.when(pl.program_id(0) == pl.num_programs(0) - 1)(fn)


def attn_fwd_kernel(place, x, *refs):
    own, near, far = refs[0:3], refs[3:6], refs[6:9]
    middle, again, packed, probs, mixed, value, wqkv, wm, sm, qkv, out, masks = refs[9:]

    @first_step
    def _():
        assemble_attn(0, place[0], place[1], own, near, far, wqkv, wm, sm)
        fill_head_masks(masks)
        project(x, wqkv, sm, qkv)

    crops = [pl.program_id(0) * STEP_CROPS + i for i in range(STEP_CROPS)]
    attend_crops(place, crops, range(STEP_CROPS), masks, qkv, packed, probs, out)

    @last_step
    def _():
        mix(out, qkv, (2, 5), sm, mixed)
        for orient in range(2):
            value[orient] = qkv[orient * 3 + 2, :ROWS, :].astype(bf16)
        mixer(x, mixed, wm, sm, middle, again)


def ff_fwd_kernel(place, middle, sm, *refs):
    own, near, far = refs[0:2], refs[2:5], refs[5:8]
    out, we, wr = refs[8:]

    @first_step
    def _():
        assemble_ff(0, place[0], place[1], own, near, far, we, wr)

    out[...] = ff_forward(middle[...], we, wr, sm)


def top_kernel(place, x, cotangent, *refs):
    attn_own, ff_own, rest = refs[0:3], refs[3:5], refs[5]
    (output, grad_out, grads) = refs[6:9]
    (wqkv, wm, sm, we, wr, qkv, out, packed, probs, mixed, middle, g, slope, dv,
     acc_e, acc_r, acc_q, acc_m, vec, masks) = refs[9:]

    assemble_top(place[0], attn_own, ff_own, rest, wqkv, wm, sm, we, wr)
    clear(acc_e, acc_r, acc_q, acc_m, vec)
    fill_head_masks(masks)
    project(x, wqkv, sm, qkv)

    def ahead(i, _):
        crops = [i * STEP_CROPS + j for j in range(STEP_CROPS)]
        attend_crops(place, crops, crops, masks, qkv, packed, probs, out)
        return 0

    lax.fori_loop(0, CROPS // STEP_CROPS, ahead, 0)
    mix(out, qkv, (2, 5), sm, mixed)
    mixer(x, mixed, wm, sm, middle)
    for rows in chunks():
        gs, slopes = {}, {}
        output[rows, :] = ff_forward(middle[rows, :], we, wr, sm, gs, slopes).astype(bf16)
        for s in range(4):
            g[rows, s * 256 : (s + 1) * 256] = gs[s]
            slope[rows, s * 256 : (s + 1) * 256] = slopes[s]
    for rows in chunks():
        held = lambda s: (g[rows, s * 256 : (s + 1) * 256], slope[rows, s * 256 : (s + 1) * 256])
        middle_here = middle[rows, :]
        middle[rows, :] = ff_backward(cotangent[rows, :].astype(f32), middle_here, we, wr, sm, acc_e, acc_r, vec, held)
    em, e_low = out, g.at[:, 0:768]

    def e_at(orient, p):
        return (dv, orient) if p == 2 else (qkv, orient * 3 + p)

    mixer_back(middle, mixed, wm, acc_m, vec, em)

    def behind(i, _):
        crops = [i * STEP_CROPS + j for j in range(STEP_CROPS)]
        attend_crops_back(crops, crops, masks, em, packed, probs, e_at)
        return 0

    lax.fori_loop(0, CROPS // STEP_CROPS, behind, 0)
    mix_back(em, qkv, (2, 5), sm, e_at, e_low, vec)
    project_back(middle, x, e_low, wqkv, sm, acc_q, vec, grad_out)
    write_parts(attn_pieces(acc_q, acc_m, jnp.sum(vec[...], axis=1)) + ff_pieces(acc_e, acc_r), 0, grads)


def ff_bwd_kernel(place, grad, middle, we, wr, sm, grad_mid, keep, give, vec, acc_e, acc_r):
    @first_step
    def _():
        clear(acc_e, acc_r, vec)

    grad_mid[...] = ff_backward(grad[...], middle[...], we, wr, sm, acc_e, acc_r, vec)

    @last_step
    def _():
        write_halves(place[1], ff_pieces(acc_e, acc_r), keep, give)


def attn_bwd_kernel(place, grad, x, packed, probs, mixed, value, wqkv, wm, sm, vec_in, patch_grad, keep, give, em, e, e_low, acc_q, acc_m, vec, masks):
    @first_step
    def _():
        fill_head_masks(masks)
        clear(acc_q, acc_m)
        vec[...] = vec_in[...]
        mixer_back(grad, mixed, wm, acc_m, vec, em)

    crops = [pl.program_id(0) * STEP_CROPS + i for i in range(STEP_CROPS)]
    attend_crops_back(crops, range(STEP_CROPS), masks, em, packed, probs, lambda orient, p: (e, orient * 3 + p))

    @last_step
    def _():
        mix_back(em, value, (0, 1), sm, lambda orient, p: (e, orient * 3 + p), e_low, vec)
        project_back(grad, x, e_low, wqkv, sm, acc_q, vec, patch_grad)
        write_halves(place[1], attn_pieces(acc_q, acc_m, jnp.sum(vec[...], axis=1)), keep, give)


def whole(shape):
    return pl.BlockSpec(shape, lambda i, *_: (0,) * len(shape))


def rows_of(lanes, rows=CHUNK):
    return pl.BlockSpec((rows, lanes), lambda i, *_: (i, 0))


def crop_spec(*dims):
    return pl.BlockSpec((STEP_CROPS,) + dims, lambda i, *_: (i,) + (0,) * len(dims))


def of_layer(layer, *dims):
    return pl.BlockSpec((1,) + dims, lambda i, *_: (layer,) + (0,) * len(dims))


def attn_specs(layer):
    return [of_layer(layer, 192, D), of_layer(layer, 64, D), whole((2, 32, D))]


def ff_specs(layer):
    return [of_layer(layer, D, D), of_layer(layer, 64, FF)]


def half_specs(rows):
    return [whole((rows, D))] * 6


def shape(dims, dtype=bf16):
    return jax.ShapeDtypeStruct(dims, dtype)


def far(dims, dtype=bf16):
    return pltpu.HBM(dims, dtype)


def params(micros, mib=16, grid=True):
    steps = dict(dimension_semantics=("arbitrary",)) if grid else {}
    return dict(
        compiler_params=pltpu.CompilerParams(vmem_limit_bytes=mib * 1024 * 1024, **steps),
        cost_estimate=pl.CostEstimate(flops=int(micros * 1e9), bytes_accessed=1 << 20, transcendentals=0),
    )


def held_call(kernel, name, place, arrays, outs, scratch, micros, mib):
    there = pl.BlockSpec(memory_space=pltpu.VMEM)
    return pl.pallas_call(
        kernel,
        in_specs=[pl.BlockSpec(memory_space=pltpu.SMEM)] + [there] * len(arrays),
        out_specs=[there] * len(outs),
        out_shape=[shape(dims, dtype) for dims, dtype in outs],
        scratch_shapes=list(scratch),
        name=name,
        **params(micros, mib, False),
    )(place, *arrays)


v = pltpu.VMEM


def attn_fwd_call(place, x, unit):
    rows = unit[-1].shape[0]
    return pl.pallas_call(
        attn_fwd_kernel,
        grid_spec=pltpu.PrefetchScalarGridSpec(
            num_scalar_prefetch=1,
            grid=(CROPS // STEP_CROPS,),
            in_specs=[whole((ROWS, D))] + attn_specs(0) + half_specs(rows),
            out_specs=[whole((ROWS, D)), whole((ROWS, D)), crop_spec(2, 3, WIN, 256), crop_spec(2, 4 * WIN, 256), whole((ROWS, D)), whole((2, ROWS, 128)), whole((768, D)), whole((D, D)), whole((32, D))],
            scratch_shapes=[v((6, HELD, 128), f32), v((2, HELD, 128), f32), v((HALF_HEADS, WIN, 256), bf16)],
        ),
        out_shape=[shape((ROWS, D), f32), far((ROWS, D), f32), far((CROPS, 2, 3, WIN, 256)), far((CROPS, 2, 4 * WIN, 256)), far((ROWS, D)), far((2, ROWS, 128)), far((768, D)), far((D, D)), shape((32, D), f32)],
        name="attn_fwd",
        **params(10, 20),
    )(place, x, *unit)


def ff_fwd_call(place, middle, sm, unit):
    return pl.pallas_call(
        ff_fwd_kernel,
        grid_spec=pltpu.PrefetchScalarGridSpec(
            num_scalar_prefetch=1,
            grid=(ROWS // CHUNK,),
            in_specs=[rows_of(D), whole((32, D))] + ff_specs(0) + half_specs(HALF_FF),
            out_specs=[rows_of(D), whole((4, D, D)), whole((D, FF))],
        ),
        out_shape=[shape((ROWS, D), f32), far((4, D, D)), far((D, FF))],
        name="ff_fwd",
        **params(6, 16),
    )(place, middle, sm, *unit)


def top_call(place, x, cotangent, weights, parts, r):
    scratch = [
                v((768, D), bf16), v((D, D), bf16), v((32, D), f32), v((4, D, D), bf16), v((D, FF), bf16),
                v((6, HELD, 128), f32), v((2, HELD, 128), f32), v((CROPS, 2, 3, WIN, 256), bf16), v((CROPS, 2, 4 * WIN, 256), bf16),
                v((ROWS, D), bf16), v((ROWS, D), f32), v((ROWS, FF), bf16), v((ROWS, FF), bf16),
                v((2, HELD, 128), f32),
                v((4, D, D), f32), v((4, D, D), f32), v((768, D), f32), v((D, D), f32), v((32, CROPS, D), f32), v((HALF_HEADS, WIN, 256), bf16),
    ]
    outs = [((ROWS, D), bf16), ((ROWS, D), f32), ((parts, 4, r, D), bf16)]
    return held_call(top_kernel, "top_block", place, [x, cotangent, *weights], outs, scratch, 30, 49)


def ff_bwd_call(place, grad, middle, we, wr, sm, parts, r):
    return pl.pallas_call(
        ff_bwd_kernel,
        grid_spec=pltpu.PrefetchScalarGridSpec(
            num_scalar_prefetch=1,
            grid=(ROWS // CHUNK,),
            in_specs=[rows_of(D), rows_of(D), whole((4, D, D)), whole((D, FF)), whole((32, D))],
            out_specs=[rows_of(D)] + [whole((parts, 4, r, D))] * 2 + [whole((32, CROPS, D))],
            scratch_shapes=[v((4, D, D), f32), v((4, D, D), f32)],
        ),
        out_shape=[shape((ROWS, D), f32)] + [shape((parts, 4, r, D))] * 2 + [shape((32, CROPS, D), f32)],
        name="ff_bwd",
        **params(10, 50),
    )(place, grad, middle, we, wr, sm)


def attn_bwd_call(place, grad, x, packed, probs, mixed, value, wqkv, wm, sm, vec):
    return pl.pallas_call(
        attn_bwd_kernel,
        grid_spec=pltpu.PrefetchScalarGridSpec(
            num_scalar_prefetch=1,
            grid=(CROPS // STEP_CROPS,),
            in_specs=[whole((ROWS, D)), whole((ROWS, D)), crop_spec(2, 3, WIN, 256), crop_spec(2, 4 * WIN, 256), whole((ROWS, D)), whole((2, ROWS, 128)), whole((768, D)), whole((D, D)), whole((32, D)), whole((32, CROPS, D))],
            out_specs=[whole((ROWS, D))] + [whole((1, 4, LOW_ROWS // 2, D))] * 2,
            scratch_shapes=[v((2, HELD, 128), f32), v((6, HELD, 128), f32), v((ROWS, 768), bf16), v((768, D), f32), v((D, D), f32), v((32, CROPS, D), f32), v((HALF_HEADS, WIN, 256), bf16)],
        ),
        out_shape=[shape((ROWS, D))] + [shape((1, 4, LOW_ROWS // 2, D))] * 2,
        name="attn_bwd",
        **params(16, 36),
    )(place, grad, x, packed, probs, mixed, value, wqkv, wm, sm, vec)


def to_rows(x):
    return jnp.transpose(x, (1, 2, 0, 3)).reshape(ROWS, D)


def from_rows(x):
    return jnp.transpose(x.reshape(GRID, GRID, CROPS, D), (2, 0, 1, 3))


def pack_kernel(place, qkv, mixer_t, gain, shift, entry, taps, branch, hidden_bias, expand, reduce_t, half_a, half_f, vec, unit):
    me, core = place[0], place[1]
    lane = lax.broadcasted_iota(jnp.int32, (18, D), 1)
    row = lax.broadcasted_iota(jnp.int32, (14, D), 0)
    for layer in range(2):
        rows = jnp.concatenate(
            [ref[layer].astype(f32) for ref in (gain, shift, entry)] + [taps[:, layer].astype(f32), branch[layer].astype(f32)], axis=0
        )
        vectors = jnp.where(lane // 64 == me, jnp.concatenate([rows] * 4, axis=1), 0.0)
        hidden_rows = jnp.where(row == me, hidden_bias[layer : layer + 1].astype(f32), 0.0)
        vec[layer] = jnp.concatenate([vectors, hidden_rows], axis=0).astype(bf16)
    half_a[0:96] = qkv[0, pl.ds(pl.multiple_of(96 * core, 32), 96)]
    half_a[96:128] = mixer_t[0, pl.ds(pl.multiple_of(32 * core, 32), 32)]
    half_a[128:144] = vec[0, pl.ds(pl.multiple_of(16 * core, 16), 16)]
    half_f[0:128] = expand[0, pl.ds(pl.multiple_of(128 * core, 128), 128)]
    for c in range(4):
        half_f[128 + 32 * c : 160 + 32 * c] = reduce_t[0, pl.ds(pl.multiple_of(32 * core, 32), 32), c * 256 : (c + 1) * 256]
    unit[0:192] = qkv[1]
    unit[192:256] = mixer_t[1]
    unit[256:288] = vec[1]
    unit[288:544] = expand[1]
    for c in range(4):
        unit[544 + 64 * c : 608 + 64 * c] = reduce_t[1, :, c * 256 : (c + 1) * 256]
    if unit.shape[0] > UNIT:
        unit[UNIT:] = jnp.zeros((unit.shape[0] - UNIT, D), bf16)
    r = half_a.shape[0] - HALF_ATTN
    half_a[HALF_ATTN:] = unit[pl.ds(pl.multiple_of(place[3] * r, 16), r)]


def local_call(kernel, name, place, arrays, outs, scratch=()):
    return pl.pallas_call(
        kernel,
        grid_spec=pltpu.PrefetchScalarGridSpec(
            num_scalar_prefetch=1,
            grid=(1,),
            in_specs=[whole(x.shape) for x in arrays],
            out_specs=[whole(dims) for dims, _ in outs],
            scratch_shapes=list(scratch),
        ),
        out_shape=[shape(dims, dtype) for dims, dtype in outs],
        name=name,
        **params(1, 58),
    )(place, *arrays)


def turn_mp(x, k):
    n = lax.axis_size("mp")
    return lax.ppermute(x, "mp", [(i, (i + k) % n) for i in range(n)])


def swap_dp(x, bits):
    n = lax.axis_size("dp")
    return lax.ppermute(x, "dp", [(i, i ^ bits) for i in range(n)])


def turn_all(x):
    return [turn_mp(x, k) for k in (1, 2, 3)]


def swap_core(xs):
    return [swap_dp(x, 1) for x in xs]


def pick(x, at):
    return lax.dynamic_index_in_dim(x, at, 0, keepdims=False)


def add_up(xs):
    total = xs[0].astype(f32)
    for x in xs[1:]:
        total = total + x.astype(f32)
    return total


def to_planes(keep, got, at):
    total = add_up([keep, got]).astype(bf16)
    return [pick(total, at ^ b) for b in range(keep.shape[0])]


def swap_planes(parts):
    return [parts[0]] + [swap_dp(part, 2 * b) for b, part in enumerate(parts) if b]


def to_shards(xs, me):
    total = add_up(xs)
    low = total.astype(bf16)
    return [pick(total, me)] + [pick(low, (me + k) % 4) for k in (1, 2, 3)]


def turn_shards(parts):
    return [parts[0]] + [turn_mp(part, k) for k, part in enumerate(parts) if k]


def unpack_kernel(planes, cut_f, cut_t, place, *refs):
    mine, other = refs[:planes], refs[planes : 2 * planes]
    packed, mixer_g, expand, reduce_g, gain, shift, entry, taps, branch, hidden_g, held, held_t = refs[2 * planes :]
    me, core = place[0], place[1]
    r_f, r_t = cut_t - cut_f, mine[0].shape[0] - cut_t
    for which, parts in ((core, mine), (1 - core, other)):
        total = parts[0][:cut_f].astype(f32)
        for part in parts[1:]:
            total = total + part[:cut_f].astype(f32)
        held[which, :cut_f] = total
        for b in range(planes):
            at = place[2] ^ b
            held[which, pl.ds(pl.multiple_of(cut_f + at * r_f, 16), r_f)] = parts[b][cut_f:cut_t].astype(f32)
            held_t[pl.ds(pl.multiple_of((2 * at + which) * r_t, 16), r_t)] = parts[b][cut_t:].astype(f32)

    def rows(which, lo, hi):
        if which is None:
            return held_t[lo:hi]
        start, half = which
        out = []
        for c in range(2):
            a, b = max(lo, c * half), min(hi, (c + 1) * half)
            if a < b:
                out.append(held[c, start + a - c * half : start + b - c * half])
        return out[0] if len(out) == 1 else jnp.concatenate(out, axis=0)

    low_a, low_f = (0, cut_f), (cut_f, planes * r_f)
    for layer, attn, ff, ff_at in ((0, low_a, low_f, 0), (1, None, None, 288)):
        packed[layer] = rows(attn, 0, 192)
        mixer_g[layer] = rows(attn, 192, 256)
        expand[layer] = rows(ff, ff_at, ff_at + 256)
        for c in range(4):
            at = ff_at + 256 + 64 * c
            reduce_g[layer, :, c * 256 : (c + 1) * 256] = rows(ff, at, at + 64)
        vectors = rows(attn, 256, 288)
        mine_lanes = vectors[:, :64]
        for s in range(1, 4):
            mine_lanes = jnp.where(me == s, vectors[:, 64 * s : 64 * (s + 1)], mine_lanes)
        gain[layer] = mine_lanes[GAIN : GAIN + 2]
        shift[layer] = mine_lanes[SHIFT : SHIFT + 2]
        entry[layer] = mine_lanes[ENTRY : ENTRY + 2]
        branch[layer] = mine_lanes[BRANCH : BRANCH + 2]
        for t in range(10):
            taps[t, layer : layer + 1] = mine_lanes[TAPS + t : TAPS + t + 1]
        row = vectors[HIDDEN : HIDDEN + 1]
        for s in range(1, 4):
            row = jnp.where(me == s, vectors[HIDDEN + s : HIDDEN + s + 1], row)
        hidden_g[layer : layer + 1] = row


def body(patches, validity, norm_gain, norm_shift, qkv_weight, entry_bias, stencil, mixer_weight, branch_bias, expand_weight, hidden_bias, reduce_weight, cotangent):
    dp = lax.axis_size("dp")
    planes = dp // 2
    me, at_dp = lax.axis_index("mp"), lax.axis_index("dp")
    heights = jnp.sum(validity[:, :, 0], axis=1)
    widths = jnp.sum(validity[:, 0, :], axis=1)
    place = jnp.stack([me, at_dp % 2, at_dp // 2, at_dp]).astype(jnp.int32)
    sizes = jnp.concatenate([jnp.stack([me, at_dp % 2]), jnp.stack([heights, widths], axis=1).reshape(-1)]).astype(jnp.int32)

    qkv_t = jnp.transpose(qkv_weight, (0, 2, 3, 1)).reshape(2, 192, D)
    mixer_t = jnp.transpose(mixer_weight, (0, 2, 1))
    reduce_t = jnp.transpose(reduce_weight, (0, 2, 1))
    vectors = (norm_gain, norm_shift, entry_bias, jnp.transpose(stencil, (1, 0, 2)), branch_bias, hidden_bias)

    arrays = [qkv_t, mixer_t, norm_gain, norm_shift, entry_bias, jnp.transpose(stencil, (1, 0, 2)), branch_bias, hidden_bias, expand_weight, reduce_t]
    r_t, r_f = part_rows(UNIT, dp), part_rows(FF_ROWS, dp)
    outs = [(HALF_ATTN + r_t, D), (HALF_FF, D), (2, 32, D)]
    half_a0, half_f0, vec = local_call(
        pack_kernel, "pack", place, arrays, [(dims, bf16) for dims in outs], [v((dp * r_t, D), bf16)]
    )
    attn_own, ff_own = [qkv_t, mixer_t, vec], [expand_weight, reduce_t]

    near_a0 = turn_all(half_a0)
    near_1 = jnp.stack([x[HALF_ATTN:] for x in near_a0])
    near_f0 = turn_all(half_f0)
    far_a0 = swap_core(near_a0)
    x, top_grad = to_rows(patches), to_rows(cotangent)
    near_1, x = lax.optimization_barrier((near_1, x))
    rest_1 = lax.all_gather(near_1, "dp", axis=0, tiled=False)
    middle, again, packed, probs, mixed, value, wqkv, wm, sm = attn_fwd_call(sizes, x, attn_own + near_a0 + far_a0)
    near_f0, middle = lax.optimization_barrier((near_f0, middle))
    far_f0 = swap_core(near_f0)
    state, we, wr = ff_fwd_call(sizes, middle, sm, ff_own + near_f0 + far_f0)
    output, grad, grads_1 = top_call(sizes, state, top_grad, attn_own + ff_own + [rest_1], dp, r_t)
    sums_1 = lax.psum_scatter(grads_1, "dp", scatter_dimension=0, tiled=False)

    grad_mid, keep_f, give_f, vec = ff_bwd_call(place, grad, again, we, wr, sm, planes, r_f)
    got_f = swap_dp(give_f, 1)
    patch_grad, keep_a, give_a = attn_bwd_call(place, grad_mid, x, packed, probs, mixed, value, wqkv, wm, sm, vec)
    got_f, keep_a, give_a = lax.optimization_barrier((got_f, keep_a, give_a))

    got_a = swap_dp(give_a, 1)
    planes_f = swap_planes(to_planes(keep_f, got_f, place[2]))
    shards_a = to_shards([keep_a[0], got_a[0]], me)
    mp_a = turn_shards(shards_a)
    planes_f, sums_1 = lax.optimization_barrier((planes_f, sums_1, shards_a))[:2]
    low = add_up(planes_f).astype(bf16)
    mp_f = turn_shards(to_shards([jnp.concatenate([low, sums_1], axis=1)], me))
    share = jnp.concatenate([add_up(mp_a), add_up(mp_f)], axis=0).astype(bf16)
    mine = swap_planes([share] * planes)
    other = swap_core(mine)
    outs = [(2, 192, D), (2, 64, D), (2, D, D), (2, 64, FF), (2, 2, 64), (2, 2, 64), (2, 2, 64), (10, 2, 64), (2, 2, 64), (2, D)]
    cut_f = LOW_ROWS // 2
    cut_t = cut_f + r_f
    held = [v((2, cut_f + planes * r_f, D), f32), v((dp * r_t, D), f32)]
    packed_g, mixer_g, expand_g, reduce_g, gain_g, shift_g, entry_g, taps_g, branch_g, hidden_g = held_call(
        functools.partial(unpack_kernel, planes, cut_f, cut_t), "unpack", place, mine + other, [(dims, f32) for dims in outs], held, 2, 16
    )
    return (
        from_rows(output), from_rows(patch_grad), gain_g, shift_g,
        jnp.transpose(packed_g.reshape(2, 3, 64, D), (0, 3, 1, 2)), entry_g, jnp.transpose(taps_g, (1, 0, 2)),
        jnp.transpose(mixer_g, (0, 2, 1)), branch_g, expand_g, hidden_g, jnp.transpose(reduce_g, (0, 2, 1)),
    )


def solution(mesh):
    crops = P(("dp", "mp"), None, None, None)
    lanes = P(None, None, "mp")
    deep = P(None, None, None, "mp")
    return jax.shard_map(
        body,
        mesh=mesh,
        in_specs=(crops, P(("dp", "mp"), None, None), lanes, lanes, deep, lanes, lanes, lanes, lanes, lanes, P(None, "mp"), lanes, crops),
        out_specs=(crops, crops, lanes, lanes, deep, lanes, lanes, lanes, lanes, lanes, P(None, "mp"), lanes),
        check_vma=False,
    )
```

```python
import functools

import jax
import jax.numpy as jnp
from jax import lax
from jax.experimental import pallas as pl
from jax.experimental.pallas import tpu as pltpu
from jax.sharding import PartitionSpec as P

GRID = 14
STRIPE = 7
CELLS = GRID * GRID
CROPS = 8
ROWS = CELLS * CROPS
LINE = GRID * CROPS
HELD = ROWS + 112
WIN = 112
HALF_HEADS = 4
HEAD = 32
D = 256
FF = 1024
STEP_CROPS = 2
CHUNK = 784

norm_eps = 1e-05
masked_score = -1e30
root_half = 0.7071067811865476
inverse_root_tau = 0.3989422804014327
log2_e = 1.4426950408889634
factor = HEAD**-0.5

f32 = jnp.float32
bf16 = jnp.bfloat16

HALF_ATTN = 144
HALF_FF = 256
FF_ROWS = 512
UNIT = 800
LOW_ROWS = 288
GAIN, SHIFT, ENTRY, TAPS, BRANCH, HIDDEN = 0, 2, 4, 6, 16, 18


def dot(a, b):
    return lax.dot_general(a, b, (((1,), (0,)), ((), ())), preferred_element_type=f32)


def dot_nt(a, b):
    return lax.dot_general(a, b, (((1,), (1,)), ((), ())), preferred_element_type=f32)


def dot_tn(a, b):
    return lax.dot_general(a, b, (((0,), (0,)), ((), ())), preferred_element_type=f32)


def norm(x):
    center = x - jnp.mean(x, axis=-1, keepdims=True)
    spread = jnp.mean(center * center, axis=-1, keepdims=True)
    inverse = lax.rsqrt(spread + norm_eps)
    return center * inverse, inverse


def norm_back(grad, normal, inverse, gain):
    scaled = grad * gain
    return inverse * (
        scaled
        - jnp.mean(scaled, axis=-1, keepdims=True)
        - normal * jnp.mean(scaled * normal, axis=-1, keepdims=True)
    )


def column_sum(x):
    return jnp.sum(x.reshape(x.shape[0] // CROPS, CROPS, x.shape[1]), axis=0)


def window_row_inside(orient):
    row = lax.broadcasted_iota(jnp.int32, (WIN, 128), 0)
    return row < 98 if orient == 0 else row % 8 < STRIPE


def key_bias(orient, window, height, width):
    row = lax.broadcasted_iota(jnp.int32, (WIN, 128), 0)
    if orient == 0:
        line, column = row // GRID + window * STRIPE, row % GRID
    else:
        line, column = row // 8, row % 8 + window * STRIPE
    valid = window_row_inside(orient) & (line < height) & (column < width)
    return jnp.where(valid, 0.0, masked_score)


def load_window(ref, block, crop, orient, window):
    if orient == 0:
        return ref[block, pl.ds(98 * CROPS * window + crop, WIN, stride=CROPS), :]
    parts = [
        ref[block, pl.ds((line * GRID + window * STRIPE) * CROPS + crop, 8, stride=CROPS), :]
        for line in range(GRID)
    ]
    return jnp.concatenate(parts, axis=0)


def store_window(ref, block, crop, orient, window, x):
    if orient == 0:
        ref[block, pl.ds(98 * CROPS * window + crop, 98, stride=CROPS), :] = x[:98]
        return
    for line in range(GRID):
        at = (line * GRID + window * STRIPE) * CROPS + crop
        ref[block, pl.ds(at, STRIPE, stride=CROPS), :] = x[line * 8 : line * 8 + STRIPE]


def fill_head_masks(masks):
    lane = lax.broadcasted_iota(jnp.int32, (WIN, 256), 1) % 128 // HEAD
    for head in range(HALF_HEADS):
        masks[head] = jnp.where(lane == head, 1.0, 0.0).astype(bf16)


def heads_down(x, masks):
    return jnp.concatenate([x * masks[head] for head in range(HALF_HEADS)], axis=0)


def fold_heads(x):
    head = lax.broadcasted_iota(jnp.int32, (WIN, 256), 1) % 128 // HEAD
    parts = [x[h * WIN : (h + 1) * WIN] for h in range(HALF_HEADS)]
    low, high = jnp.where(head == 0, parts[0], parts[1]), jnp.where(head == 2, parts[2], parts[3])
    return jnp.where(head < 2, low, high)


def windows_apart(x):
    none, rest = jnp.zeros((WIN, 128), x.dtype), jnp.zeros((128 - WIN, 256), x.dtype)
    first = jnp.concatenate([x[:, :128], none], axis=1)
    second = jnp.concatenate([none, x[:, 128:]], axis=1)
    return jnp.concatenate([first, rest, second, rest], axis=0)


def by_head(turned, probs):
    parts = []
    for head in range(HALF_HEADS):
        left = jnp.concatenate([turned[w * 128 + head * HEAD : w * 128 + (head + 1) * HEAD] for w in range(2)], axis=0)
        both = dot(left, probs[head * WIN : (head + 1) * WIN])
        parts.append((both[:HEAD, :128], both[HEAD:, 128:]))
    return [jnp.concatenate([part[w] for part in parts], axis=0).T[:WIN] for w in range(2)]


def head_probs(scores, bias):
    scores = scores * (factor * log2_e) + bias
    raised = jnp.exp2(scores - jnp.max(scores, axis=0, keepdims=True))
    return (raised * (1.0 / jnp.sum(raised, axis=0, keepdims=True))).astype(bf16)


def head_grad_scores(grad_probs, probs):
    wide = probs.astype(f32)
    inner = jnp.sum(grad_probs * wide, axis=0, keepdims=True)
    return (wide * (grad_probs - inner)).astype(bf16)


def each_head(fn, *arrays):
    parts = [fn(*(x[h * WIN : (h + 1) * WIN] for x in arrays)) for h in range(HALF_HEADS)]
    return jnp.concatenate(parts, axis=0)


def attend(queries, keys, values, biases, masks):
    apart = [windows_apart(x.astype(bf16)) for x in queries]
    scores = [dot_nt(heads_down(k.astype(bf16), masks), q) for k, q in zip(keys, apart)]
    value_turned = [x.T.astype(bf16) for x in values]
    probs = [each_head(lambda s, b=b: head_probs(s, b), s) for s, b in zip(scores, biases)]
    return [by_head(v, p) for v, p in zip(value_turned, probs)], probs


def attend_back(grads, queries, keys, values, probs, masks):
    grad_apart = [windows_apart(x) for x in grads]
    grad_probs = [dot_nt(heads_down(v, masks), g) for v, g in zip(values, grad_apart)]
    key_turned = [x.astype(f32).T.astype(bf16) for x in keys]
    grad_value = [fold_heads(dot(p, g)) for p, g in zip(probs, grad_apart)]
    grad_scores = [each_head(head_grad_scores, g, p) for g, p in zip(grad_probs, probs)]
    apart = [windows_apart(x) for x in queries]
    grad_key = [fold_heads(dot(s, q)) * factor for s, q in zip(grad_scores, apart)]
    grad_query = [[x * factor for x in by_head(k, s)] for k, s in zip(key_turned, grad_scores)]
    return grad_query, grad_key, grad_value


def steps_along(x, orient):
    zero = jnp.zeros((CROPS, x.shape[1]), x.dtype)
    if orient == 0:
        return {-1: jnp.concatenate([zero, x[:-CROPS]], axis=0), 0: x, 1: jnp.concatenate([x[CROPS:], zero], axis=0)}
    half = LINE // 2
    left, right = x[:half], x[half:]
    return {
        -1: jnp.concatenate([zero, left[:-CROPS], zero, right[:-CROPS]], axis=0),
        0: x,
        1: jnp.concatenate([left[CROPS:], zero, right[CROPS:], zero], axis=0),
    }


def line_reaches(line, step, orient):
    if step == 0:
        return None
    stops = (GRID, STRIPE) if orient == 0 else (GRID,)
    edges = [(stop - 1) if step == 1 else (stop % GRID) for stop in stops]
    ok = line != edges[0]
    for edge in edges[1:]:
        ok = ok & (line != edge)
    return jnp.where(ok, 1.0, 0.0).astype(f32)


def line_at(ref, block, line):
    held = jnp.clip(line, 0, GRID - 1)
    return ref[block, pl.ds(pl.multiple_of(held * LINE, LINE), LINE), :]


def stencil_line(ref, block, taps, line, orient, back):
    total = None
    for step in (-1, 0, 1):
        moved = steps_along(line_at(ref, block, line + (-step if back else step)).astype(f32), orient)
        reach = line_reaches(line, -step if back else step, orient)
        for side in (-1, 0, 1):
            tap = taps[3 * (step + 1) + side + 1]
            if reach is not None:
                tap = tap * reach
            term = moved[-side if back else side] * tap
            total = term if total is None else total + term
    return total


def stencil_line_taps(ref, block, grad, line, orient):
    sums = []
    for step in (-1, 0, 1):
        moved = steps_along(line_at(ref, block, line + step).astype(f32), orient)
        reach = line_reaches(line, step, orient)
        for side in (-1, 0, 1):
            part = column_sum(grad * moved[side])
            sums.append(part if reach is None else part * reach)
    sums.append(column_sum(grad))
    return sums


def assemble_attn(layer, me, core, own, near, far, wqkv, wm, sm):
    qkv, mixer_t, vec = own

    def put(shard, blocks, at, mixer_rows, mixer_at):
        orient, part = lax.div(shard, 2), lax.rem(shard, 2)
        for i, block in enumerate(blocks):
            j = at + i
            row = orient * 384 + lax.div(j, 2) * 128 + part * 64 + lax.rem(j, 2) * 32
            wqkv[pl.ds(pl.multiple_of(row, 32), 32), :] = block
        wm[pl.ds(pl.multiple_of(shard * 64 + mixer_at, 32), mixer_rows.shape[0]), :] = mixer_rows

    put(me, [qkv[0, 32 * i : 32 * (i + 1)] for i in range(6)], jnp.int32(0), mixer_t[0], 0)
    sm[...] = vec[layer].astype(f32)
    for halves, which in ((near, core), (far, 1 - core)):
        for k, half in enumerate(halves, 1):
            shard = lax.rem(me + 4 - k, 4)
            put(shard, [half[32 * i : 32 * (i + 1)] for i in range(3)], 3 * which, half[96:128], 32 * which)
            sm[pl.ds(pl.multiple_of(16 * which, 16), 16), :] += half[128:144].astype(f32)


def assemble_ff(first, me, core, own, near, far, we, wr):
    expand, reduce_t = own
    we[me] = expand[0]
    wr[pl.ds(pl.multiple_of(me * 64, 64), 64), :] = reduce_t[0]
    for halves, which in ((near, core), (far, 1 - core)):
        for k, half in enumerate(halves, 1):
            shard = lax.rem(me + 4 - k, 4)
            we[shard, pl.ds(pl.multiple_of(128 * which, 128), 128), :] = half[first : first + 128]
            row = pl.multiple_of(shard * 64 + 32 * which, 32)
            for c in range(4):
                at = first + 128 + 32 * c
                wr[pl.ds(row, 32), c * 256 : (c + 1) * 256] = half[at : at + 32]


def assemble_top(me, attn_own, ff_own, rest, wqkv, wm, sm, we, wr):
    qkv, mixer_t, vec = attn_own
    expand, reduce_t = ff_own

    def put(shard, row, value):
        orient, part = lax.div(shard, 2), lax.rem(shard, 2)
        n = value.shape[0]
        if row < 192:
            at = orient * 384 + row // 64 * 128 + part * 64 + row % 64
            wqkv[pl.ds(pl.multiple_of(at, 16), n), :] = value
        elif row < 256:
            wm[pl.ds(pl.multiple_of(shard * 64 + row - 192, 16), n), :] = value
        elif row < 288:
            sm[row - 256 : row - 256 + n, :] += value.astype(f32)
        elif row < 544:
            we[shard, row - 288 : row - 288 + n, :] = value
        else:
            c, at = divmod(row - 544, 64)
            wr[pl.ds(pl.multiple_of(shard * 64 + at, 16), n), c * 256 : (c + 1) * 256] = value

    for p in range(3):
        put(me, 64 * p, qkv[1, 64 * p : 64 * (p + 1)])
    put(me, 192, mixer_t[1])
    sm[...] = vec[1].astype(f32)
    put(me, 288, expand[1])
    for c in range(4):
        put(me, 544 + 64 * c, reduce_t[1, :, c * 256 : (c + 1) * 256])
    dp, _, r, _ = rest.shape
    edges = list(range(0, 257, 64)) + [288] + [544 + 64 * c for c in range(5)]
    for k in range(3):
        shard = lax.rem(me + 3 - k, 4)
        for d in range(dp):
            for lo, hi in zip(edges[:-1], edges[1:]):
                a, b = max(lo, d * r), min(hi, (d + 1) * r)
                if a < b:
                    put(shard, a, rest[d, k, a - d * r : b - d * r])


def chunks():
    return [slice(at, at + CHUNK) for at in range(0, ROWS, CHUNK)]


def put_blocks(ref, rows, x):
    for block in range(x.shape[1] // 128):
        ref[block, rows, :] = x[:, block * 128 : (block + 1) * 128]


def project(x, wqkv, sm, qkv):
    zero = jnp.zeros((1, 128), f32)
    query_bias, value_bias = sm[ENTRY : ENTRY + 1], sm[ENTRY + 1 : ENTRY + 2]
    bias = jnp.concatenate(
        [query_bias[:, :128], zero, value_bias[:, :128], query_bias[:, 128:], zero, value_bias[:, 128:]], axis=1
    )
    for rows in chunks():
        normal, _ = norm(x[rows, :].astype(f32))
        a = (normal * sm[GAIN : GAIN + 1] + sm[SHIFT : SHIFT + 1]).astype(bf16)
        put_blocks(qkv, rows, dot_nt(a, wqkv[...]) + bias)
    qkv[:, ROWS:HELD, :] = jnp.zeros((6, HELD - ROWS, 128), f32)


def load_pair(ref, block, crop, orient):
    return jnp.concatenate([load_window(ref, block, crop, orient, window) for window in range(2)], axis=1)


def attend_crops(place, crops, slots, masks, qkv, packed, probs_ref, out):
    at, lists = [], ([], [], [], [])
    for crop, slot in zip(crops, slots):
        height, width = place[2 + 2 * crop], place[3 + 2 * crop]
        for orient in range(2):
            three = [load_pair(qkv, orient * 3 + p, crop, orient) for p in range(3)]
            for p, x in enumerate(three):
                packed[slot, orient, p] = x.astype(bf16)
            bias = jnp.concatenate([key_bias(orient, window, height, width) for window in range(2)], axis=1)
            for held, new in zip(lists, (*three, bias)):
                held.append(new)
            at.append((crop, slot, orient))
    outs, probs = attend(*lists, masks)
    for (crop, slot, orient), both, p in zip(at, outs, probs):
        probs_ref[slot, orient] = p
        for window in range(2):
            store_window(out, orient, crop, orient, window, both[window])


def attend_crops_back(crops, slots, masks, em, packed, probs_ref, e_at):
    at, lists = [], ([], [], [], [], [])
    for crop, slot in zip(crops, slots):
        for orient in range(2):
            inside = jnp.concatenate([window_row_inside(orient)] * 2, axis=1)
            grad = jnp.where(inside, load_pair(em, orient, crop, orient), 0.0).astype(bf16)
            for held, new in zip(lists, (grad, *(packed[slot, orient, p] for p in range(3)), probs_ref[slot, orient])):
                held.append(new)
            at.append((crop, orient))
    for (crop, orient), dq, dk, dv in zip(at, *attend_back(*lists, masks)):
        for window in range(2):
            lanes = slice(window * 128, (window + 1) * 128)
            for p, part in enumerate((dq[window], dk[:, lanes], dv[:, lanes])):
                store_window(*e_at(orient, p), crop, orient, window, part)


def taps_of(sm, orient):
    lanes = slice(orient * 128, (orient + 1) * 128)
    return [sm[TAPS + t : TAPS + t + 1, lanes] for t in range(10)]


def mix(out, value, value_at, sm, mixed):
    taps = [taps_of(sm, orient) for orient in range(2)]

    def line(i, _):
        rows = pl.ds(pl.multiple_of(i * LINE, LINE), LINE)
        for orient in range(2):
            e_v = stencil_line(value, value_at[orient], taps[orient], i, orient, False) + taps[orient][9]
            mixed[rows, orient * 128 : (orient + 1) * 128] = (out[orient, rows, :] + e_v).astype(bf16)
        return 0

    lax.fori_loop(0, GRID, line, 0)


def mixer(x, mixed, wm, sm, *outs):
    for rows in chunks():
        middle = x[rows, :].astype(f32) + (dot_nt(mixed[rows, :], wm[...]) + sm[BRANCH : BRANCH + 1])
        for out in outs:
            out[rows, :] = middle


def hidden(a2, we, sm, s):
    u = dot(a2, we[s]) + sm[HIDDEN + s : HIDDEN + s + 1]
    phi = 0.5 + 0.5 * lax.erf(u * root_half)
    return u, phi


def slope_of(u, phi):
    return phi + u * jnp.exp(-0.5 * u * u) * inverse_root_tau


def second_norm(middle, sm):
    normal, inverse = norm(middle)
    a2 = (normal * sm[GAIN + 1 : GAIN + 2] + sm[SHIFT + 1 : SHIFT + 2]).astype(bf16)
    return normal, inverse, a2


def ff_forward(middle, we, wr, sm, g_out=None, slope_out=None):
    _, _, a2 = second_norm(middle, sm)
    gs = []
    for s in range(4):
        u, phi = hidden(a2, we, sm, s)
        gs.append((u * phi).astype(bf16))
        if g_out is not None:
            g_out[s], slope_out[s] = gs[-1], slope_of(u, phi).astype(bf16)
    return middle + (dot_nt(jnp.concatenate(gs, axis=1), wr[...]) + sm[BRANCH + 1 : BRANCH + 2])


def ff_backward(grad, middle, we, wr, sm, acc_e, acc_r, vec, held=None):
    ey = grad.astype(bf16)
    vec[BRANCH + 1] += column_sum(grad)
    normal, inverse, a2 = second_norm(middle, sm)
    eus = []
    for s in range(4):
        if held is None:
            u, phi = hidden(a2, we, sm, s)
            g, slope = (u * phi).astype(bf16), slope_of(u, phi)
        else:
            g, slope = held(s)
        acc_r[s] += dot_tn(ey, g)
        eu_wide = dot(ey, wr[:, s * 256 : (s + 1) * 256]) * slope.astype(f32)
        vec[HIDDEN + s] += column_sum(eu_wide)
        eu = eu_wide.astype(bf16)
        acc_e[s] += dot_tn(a2, eu)
        eus.append(eu)
    back = None
    for s in range(4):
        term = dot_nt(eus[s], we[s])
        back = term if back is None else back + term
    vec[GAIN + 1] += column_sum(back * normal)
    vec[SHIFT + 1] += column_sum(back)
    return grad + norm_back(back, normal, inverse, sm[GAIN + 1 : GAIN + 2])


def mixer_back(grad, mixed, wm, acc_m, vec, em):
    for rows in chunks():
        here = grad[rows, :]
        eo = here.astype(bf16)
        vec[BRANCH] += column_sum(here)
        acc_m[...] += dot_tn(eo, mixed[rows, :])
        put_blocks(em, rows, dot(eo, wm[...]))
    em[:, ROWS:HELD, :] = jnp.zeros((2, HELD - ROWS, 128), f32)


def mix_back(em, value, value_at, sm, e_at, e_low, vec):
    taps = [taps_of(sm, orient) for orient in range(2)]

    def line(i, _):
        rows = pl.ds(pl.multiple_of(i * LINE, LINE), LINE)
        for orient in range(2):
            lanes = slice(orient * 128, (orient + 1) * 128)
            base = orient * 384
            eq, ek, ev = [ref[block, rows, :] for ref, block in (e_at(orient, p) for p in range(3))]
            ev = ev + stencil_line(em, orient, taps[orient], i, orient, True)
            e_low[rows, base : base + 384] = jnp.concatenate([eq, ek, ev], axis=1).astype(bf16)
            vec[ENTRY, :, lanes] += column_sum(eq)
            vec[ENTRY + 1, :, lanes] += column_sum(ev)
            for t, part in enumerate(stencil_line_taps(value, value_at[orient], em[orient, rows, :], i, orient)):
                vec[TAPS + t, :, lanes] += part
        return 0

    lax.fori_loop(0, GRID, line, 0)


def project_back(grad, x, e_low, wqkv, sm, acc_q, vec, out):
    for rows in chunks():
        normal, inverse = norm(x[rows, :].astype(f32))
        a = (normal * sm[GAIN : GAIN + 1] + sm[SHIFT : SHIFT + 1]).astype(bf16)
        e = e_low[rows, :]
        acc_q[...] += dot_tn(e, a)
        back = dot(e, wqkv[...])
        vec[GAIN] += column_sum(back * normal)
        vec[SHIFT] += column_sum(back)
        out[rows, :] = (grad[rows, :] + norm_back(back, normal, inverse, sm[GAIN : GAIN + 1])).astype(out.dtype)


def attn_pieces(acc_q, acc_m, sums):
    def qkv(s, p, lo, hi):
        at = (s // 2) * 384 + p * 128 + (s % 2) * 64
        return acc_q[at + lo : at + hi]

    return [(64, lambda s, lo, hi, p=p: qkv(s, p, lo, hi)) for p in range(3)] + [
        (64, lambda s, lo, hi: acc_m[64 * s + lo : 64 * s + hi]),
        (32, lambda s, lo, hi: sums[lo:hi]),
    ]


def ff_pieces(acc_e, acc_r):
    return [(256, lambda s, lo, hi: acc_e[s, lo:hi])] + [
        (64, lambda s, lo, hi, c=c: acc_r[c, 64 * s + lo : 64 * s + hi]) for c in range(4)
    ]


def part_rows(rows, parts):
    return -(-rows // (16 * parts)) * 16


def write_parts(pieces, first, ref):
    parts, _, r, _ = ref.shape
    for s in range(4):
        at = -first
        for rows, get in pieces + [(first + parts * r, None)]:
            for part in range(parts):
                lo, hi = max(at, part * r), min(at + rows, (part + 1) * r)
                if lo < hi:
                    new = jnp.zeros((hi - lo, D), f32) if get is None else get(s, lo - at, hi - at)
                    ref[part, s, lo - part * r : hi - part * r] = new.astype(ref.dtype)
            at += rows


def write_halves(core, pieces, keep, give):
    half = keep.shape[0] * keep.shape[2]
    for mine in range(2):

        @pl.when(core == mine)
        def _(mine=mine):
            write_parts(pieces, mine * half, keep)
            write_parts(pieces, (1 - mine) * half, give)


def clear(*refs):
    for ref in refs:
        ref[...] = jnp.zeros_like(ref)


def first_step(fn):
    pl.when(pl.program_id(0) == 0)(fn)


def last_step(fn):
    pl.when(pl.program_id(0) == pl.num_programs(0) - 1)(fn)


def attn_fwd_kernel(place, x, *refs):
    own, near, far = refs[0:3], refs[3:6], refs[6:9]
    middle, again, packed, probs, mixed, value, wqkv, wm, sm, qkv, out, masks = refs[9:]

    @first_step
    def _():
        assemble_attn(0, place[0], place[1], own, near, far, wqkv, wm, sm)
        fill_head_masks(masks)
        project(x, wqkv, sm, qkv)

    crops = [pl.program_id(0) * STEP_CROPS + i for i in range(STEP_CROPS)]
    attend_crops(place, crops, range(STEP_CROPS), masks, qkv, packed, probs, out)

    @last_step
    def _():
        mix(out, qkv, (2, 5), sm, mixed)
        for orient in range(2):
            value[orient] = qkv[orient * 3 + 2, :ROWS, :].astype(bf16)
        mixer(x, mixed, wm, sm, middle, again)


def ff_fwd_kernel(place, middle, sm, *refs):
    own, near, far = refs[0:2], refs[2:5], refs[5:8]
    out, we, wr = refs[8:]

    @first_step
    def _():
        assemble_ff(0, place[0], place[1], own, near, far, we, wr)

    out[...] = ff_forward(middle[...], we, wr, sm)


def top_kernel(place, x, cotangent, *refs):
    attn_own, ff_own, rest = refs[0:3], refs[3:5], refs[5]
    (output, grad_out, grads) = refs[6:9]
    (wqkv, wm, sm, we, wr, qkv, out, packed, probs, mixed, middle, g, slope, dv,
     acc_e, acc_r, acc_q, acc_m, vec, masks) = refs[9:]

    assemble_top(place[0], attn_own, ff_own, rest, wqkv, wm, sm, we, wr)
    clear(acc_e, acc_r, acc_q, acc_m, vec)
    fill_head_masks(masks)
    project(x, wqkv, sm, qkv)

    def ahead(i, _):
        crops = [i * STEP_CROPS + j for j in range(STEP_CROPS)]
        attend_crops(place, crops, crops, masks, qkv, packed, probs, out)
        return 0

    lax.fori_loop(0, CROPS // STEP_CROPS, ahead, 0)
    mix(out, qkv, (2, 5), sm, mixed)
    mixer(x, mixed, wm, sm, middle)
    for rows in chunks():
        gs, slopes = {}, {}
        output[rows, :] = ff_forward(middle[rows, :], we, wr, sm, gs, slopes).astype(bf16)
        for s in range(4):
            g[rows, s * 256 : (s + 1) * 256] = gs[s]
            slope[rows, s * 256 : (s + 1) * 256] = slopes[s]
    for rows in chunks():
        held = lambda s: (g[rows, s * 256 : (s + 1) * 256], slope[rows, s * 256 : (s + 1) * 256])
        middle_here = middle[rows, :]
        middle[rows, :] = ff_backward(cotangent[rows, :].astype(f32), middle_here, we, wr, sm, acc_e, acc_r, vec, held)
    em, e_low = out, g.at[:, 0:768]

    def e_at(orient, p):
        return (dv, orient) if p == 2 else (qkv, orient * 3 + p)

    mixer_back(middle, mixed, wm, acc_m, vec, em)

    def behind(i, _):
        crops = [i * STEP_CROPS + j for j in range(STEP_CROPS)]
        attend_crops_back(crops, crops, masks, em, packed, probs, e_at)
        return 0

    lax.fori_loop(0, CROPS // STEP_CROPS, behind, 0)
    mix_back(em, qkv, (2, 5), sm, e_at, e_low, vec)
    project_back(middle, x, e_low, wqkv, sm, acc_q, vec, grad_out)
    write_parts(attn_pieces(acc_q, acc_m, jnp.sum(vec[...], axis=1)) + ff_pieces(acc_e, acc_r), 0, grads)


def ff_bwd_kernel(place, grad, middle, we, wr, sm, grad_mid, keep, give, vec, acc_e, acc_r):
    @first_step
    def _():
        clear(acc_e, acc_r, vec)

    grad_mid[...] = ff_backward(grad[...], middle[...], we, wr, sm, acc_e, acc_r, vec)

    @last_step
    def _():
        write_halves(place[1], ff_pieces(acc_e, acc_r), keep, give)


def attn_bwd_kernel(place, grad, x, packed, probs, mixed, value, wqkv, wm, sm, vec_in, patch_grad, keep, give, em, e, e_low, acc_q, acc_m, vec, masks):
    @first_step
    def _():
        fill_head_masks(masks)
        clear(acc_q, acc_m)
        vec[...] = vec_in[...]
        mixer_back(grad, mixed, wm, acc_m, vec, em)

    crops = [pl.program_id(0) * STEP_CROPS + i for i in range(STEP_CROPS)]
    attend_crops_back(crops, range(STEP_CROPS), masks, em, packed, probs, lambda orient, p: (e, orient * 3 + p))

    @last_step
    def _():
        mix_back(em, value, (0, 1), sm, lambda orient, p: (e, orient * 3 + p), e_low, vec)
        project_back(grad, x, e_low, wqkv, sm, acc_q, vec, patch_grad)
        write_halves(place[1], attn_pieces(acc_q, acc_m, jnp.sum(vec[...], axis=1)), keep, give)


def whole(shape):
    return pl.BlockSpec(shape, lambda i, *_: (0,) * len(shape))


def rows_of(lanes, rows=CHUNK):
    return pl.BlockSpec((rows, lanes), lambda i, *_: (i, 0))


def crop_spec(*dims):
    return pl.BlockSpec((STEP_CROPS,) + dims, lambda i, *_: (i,) + (0,) * len(dims))


def of_layer(layer, *dims):
    return pl.BlockSpec((1,) + dims, lambda i, *_: (layer,) + (0,) * len(dims))


def attn_specs(layer):
    return [of_layer(layer, 192, D), of_layer(layer, 64, D), whole((2, 32, D))]


def ff_specs(layer):
    return [of_layer(layer, D, D), of_layer(layer, 64, FF)]


def half_specs(rows):
    return [whole((rows, D))] * 6


def shape(dims, dtype=bf16):
    return jax.ShapeDtypeStruct(dims, dtype)


def far(dims, dtype=bf16):
    return pltpu.HBM(dims, dtype)


def params(micros, mib=16, grid=True):
    steps = dict(dimension_semantics=("arbitrary",)) if grid else {}
    return dict(
        compiler_params=pltpu.CompilerParams(vmem_limit_bytes=mib * 1024 * 1024, **steps),
        cost_estimate=pl.CostEstimate(flops=int(micros * 1e9), bytes_accessed=1 << 20, transcendentals=0),
    )


def held_call(kernel, name, place, arrays, outs, scratch, micros, mib):
    there = pl.BlockSpec(memory_space=pltpu.VMEM)
    return pl.pallas_call(
        kernel,
        in_specs=[pl.BlockSpec(memory_space=pltpu.SMEM)] + [there] * len(arrays),
        out_specs=[there] * len(outs),
        out_shape=[shape(dims, dtype) for dims, dtype in outs],
        scratch_shapes=list(scratch),
        name=name,
        **params(micros, mib, False),
    )(place, *arrays)


v = pltpu.VMEM


def attn_fwd_call(place, x, unit):
    rows = unit[-1].shape[0]
    return pl.pallas_call(
        attn_fwd_kernel,
        grid_spec=pltpu.PrefetchScalarGridSpec(
            num_scalar_prefetch=1,
            grid=(CROPS // STEP_CROPS,),
            in_specs=[whole((ROWS, D))] + attn_specs(0) + half_specs(rows),
            out_specs=[whole((ROWS, D)), whole((ROWS, D)), crop_spec(2, 3, WIN, 256), crop_spec(2, 4 * WIN, 256), whole((ROWS, D)), whole((2, ROWS, 128)), whole((768, D)), whole((D, D)), whole((32, D))],
            scratch_shapes=[v((6, HELD, 128), f32), v((2, HELD, 128), f32), v((HALF_HEADS, WIN, 256), bf16)],
        ),
        out_shape=[shape((ROWS, D), f32), far((ROWS, D), f32), far((CROPS, 2, 3, WIN, 256)), far((CROPS, 2, 4 * WIN, 256)), far((ROWS, D)), far((2, ROWS, 128)), far((768, D)), far((D, D)), shape((32, D), f32)],
        name="attn_fwd",
        **params(10, 20),
    )(place, x, *unit)


def ff_fwd_call(place, middle, sm, unit):
    return pl.pallas_call(
        ff_fwd_kernel,
        grid_spec=pltpu.PrefetchScalarGridSpec(
            num_scalar_prefetch=1,
            grid=(ROWS // CHUNK,),
            in_specs=[rows_of(D), whole((32, D))] + ff_specs(0) + half_specs(HALF_FF),
            out_specs=[rows_of(D), whole((4, D, D)), whole((D, FF))],
        ),
        out_shape=[shape((ROWS, D), f32), far((4, D, D)), far((D, FF))],
        name="ff_fwd",
        **params(6, 16),
    )(place, middle, sm, *unit)


def top_call(place, x, cotangent, weights, parts, r):
    scratch = [
                v((768, D), bf16), v((D, D), bf16), v((32, D), f32), v((4, D, D), bf16), v((D, FF), bf16),
                v((6, HELD, 128), f32), v((2, HELD, 128), f32), v((CROPS, 2, 3, WIN, 256), bf16), v((CROPS, 2, 4 * WIN, 256), bf16),
                v((ROWS, D), bf16), v((ROWS, D), f32), v((ROWS, FF), bf16), v((ROWS, FF), bf16),
                v((2, HELD, 128), f32),
                v((4, D, D), f32), v((4, D, D), f32), v((768, D), f32), v((D, D), f32), v((32, CROPS, D), f32), v((HALF_HEADS, WIN, 256), bf16),
    ]
    outs = [((ROWS, D), bf16), ((ROWS, D), f32), ((parts, 4, r, D), bf16)]
    return held_call(top_kernel, "top_block", place, [x, cotangent, *weights], outs, scratch, 30, 49)


def ff_bwd_call(place, grad, middle, we, wr, sm, parts, r):
    return pl.pallas_call(
        ff_bwd_kernel,
        grid_spec=pltpu.PrefetchScalarGridSpec(
            num_scalar_prefetch=1,
            grid=(ROWS // CHUNK,),
            in_specs=[rows_of(D), rows_of(D), whole((4, D, D)), whole((D, FF)), whole((32, D))],
            out_specs=[rows_of(D)] + [whole((parts, 4, r, D))] * 2 + [whole((32, CROPS, D))],
            scratch_shapes=[v((4, D, D), f32), v((4, D, D), f32)],
        ),
        out_shape=[shape((ROWS, D), f32)] + [shape((parts, 4, r, D))] * 2 + [shape((32, CROPS, D), f32)],
        name="ff_bwd",
        **params(10, 50),
    )(place, grad, middle, we, wr, sm)


def attn_bwd_call(place, grad, x, packed, probs, mixed, value, wqkv, wm, sm, vec):
    return pl.pallas_call(
        attn_bwd_kernel,
        grid_spec=pltpu.PrefetchScalarGridSpec(
            num_scalar_prefetch=1,
            grid=(CROPS // STEP_CROPS,),
            in_specs=[whole((ROWS, D)), whole((ROWS, D)), crop_spec(2, 3, WIN, 256), crop_spec(2, 4 * WIN, 256), whole((ROWS, D)), whole((2, ROWS, 128)), whole((768, D)), whole((D, D)), whole((32, D)), whole((32, CROPS, D))],
            out_specs=[whole((ROWS, D))] + [whole((1, 4, LOW_ROWS // 2, D))] * 2,
            scratch_shapes=[v((2, HELD, 128), f32), v((6, HELD, 128), f32), v((ROWS, 768), bf16), v((768, D), f32), v((D, D), f32), v((32, CROPS, D), f32), v((HALF_HEADS, WIN, 256), bf16)],
        ),
        out_shape=[shape((ROWS, D))] + [shape((1, 4, LOW_ROWS // 2, D))] * 2,
        name="attn_bwd",
        **params(16, 36),
    )(place, grad, x, packed, probs, mixed, value, wqkv, wm, sm, vec)


def to_rows(x):
    return jnp.transpose(x, (1, 2, 0, 3)).reshape(ROWS, D)


def from_rows(x):
    return jnp.transpose(x.reshape(GRID, GRID, CROPS, D), (2, 0, 1, 3))


def pack_kernel(place, qkv, mixer_t, gain, shift, entry, taps, branch, hidden_bias, expand, reduce_t, half_a, half_f, vec, unit):
    me, core = place[0], place[1]
    lane = lax.broadcasted_iota(jnp.int32, (18, D), 1)
    row = lax.broadcasted_iota(jnp.int32, (14, D), 0)
    for layer in range(2):
        rows = jnp.concatenate(
            [ref[layer].astype(f32) for ref in (gain, shift, entry)] + [taps[:, layer].astype(f32), branch[layer].astype(f32)], axis=0
        )
        vectors = jnp.where(lane // 64 == me, jnp.concatenate([rows] * 4, axis=1), 0.0)
        hidden_rows = jnp.where(row == me, hidden_bias[layer : layer + 1].astype(f32), 0.0)
        vec[layer] = jnp.concatenate([vectors, hidden_rows], axis=0).astype(bf16)
    half_a[0:96] = qkv[0, pl.ds(pl.multiple_of(96 * core, 32), 96)]
    half_a[96:128] = mixer_t[0, pl.ds(pl.multiple_of(32 * core, 32), 32)]
    half_a[128:144] = vec[0, pl.ds(pl.multiple_of(16 * core, 16), 16)]
    half_f[0:128] = expand[0, pl.ds(pl.multiple_of(128 * core, 128), 128)]
    for c in range(4):
        half_f[128 + 32 * c : 160 + 32 * c] = reduce_t[0, pl.ds(pl.multiple_of(32 * core, 32), 32), c * 256 : (c + 1) * 256]
    unit[0:192] = qkv[1]
    unit[192:256] = mixer_t[1]
    unit[256:288] = vec[1]
    unit[288:544] = expand[1]
    for c in range(4):
        unit[544 + 64 * c : 608 + 64 * c] = reduce_t[1, :, c * 256 : (c + 1) * 256]
    if unit.shape[0] > UNIT:
        unit[UNIT:] = jnp.zeros((unit.shape[0] - UNIT, D), bf16)
    r = half_a.shape[0] - HALF_ATTN
    half_a[HALF_ATTN:] = unit[pl.ds(pl.multiple_of(place[3] * r, 16), r)]


def local_call(kernel, name, place, arrays, outs, scratch=()):
    return pl.pallas_call(
        kernel,
        grid_spec=pltpu.PrefetchScalarGridSpec(
            num_scalar_prefetch=1,
            grid=(1,),
            in_specs=[whole(x.shape) for x in arrays],
            out_specs=[whole(dims) for dims, _ in outs],
            scratch_shapes=list(scratch),
        ),
        out_shape=[shape(dims, dtype) for dims, dtype in outs],
        name=name,
        **params(1, 58),
    )(place, *arrays)


def turn_mp(x, k):
    n = lax.axis_size("mp")
    return lax.ppermute(x, "mp", [(i, (i + k) % n) for i in range(n)])


def swap_dp(x, bits):
    n = lax.axis_size("dp")
    return lax.ppermute(x, "dp", [(i, i ^ bits) for i in range(n)])


def turn_all(x):
    return [turn_mp(x, k) for k in (1, 2, 3)]


def swap_core(xs):
    return [swap_dp(x, 1) for x in xs]


def pick(x, at):
    return lax.dynamic_index_in_dim(x, at, 0, keepdims=False)


def add_up(xs):
    total = xs[0].astype(f32)
    for x in xs[1:]:
        total = total + x.astype(f32)
    return total


def to_planes(keep, got, at):
    total = add_up([keep, got]).astype(bf16)
    return [pick(total, at ^ b) for b in range(keep.shape[0])]


def swap_planes(parts):
    return [parts[0]] + [swap_dp(part, 2 * b) for b, part in enumerate(parts) if b]


def to_shards(xs, me):
    total = add_up(xs)
    low = total.astype(bf16)
    return [pick(total, me)] + [pick(low, (me + k) % 4) for k in (1, 2, 3)]


def turn_shards(parts):
    return [parts[0]] + [turn_mp(part, k) for k, part in enumerate(parts) if k]


def unpack_kernel(planes, cut_f, cut_t, place, *refs):
    mine, other = refs[:planes], refs[planes : 2 * planes]
    packed, mixer_g, expand, reduce_g, gain, shift, entry, taps, branch, hidden_g, held, held_t = refs[2 * planes :]
    me, core = place[0], place[1]
    r_f, r_t = cut_t - cut_f, mine[0].shape[0] - cut_t
    for which, parts in ((core, mine), (1 - core, other)):
        total = parts[0][:cut_f].astype(f32)
        for part in parts[1:]:
            total = total + part[:cut_f].astype(f32)
        held[which, :cut_f] = total
        for b in range(planes):
            at = place[2] ^ b
            held[which, pl.ds(pl.multiple_of(cut_f + at * r_f, 16), r_f)] = parts[b][cut_f:cut_t].astype(f32)
            held_t[pl.ds(pl.multiple_of((2 * at + which) * r_t, 16), r_t)] = parts[b][cut_t:].astype(f32)

    def rows(which, lo, hi):
        if which is None:
            return held_t[lo:hi]
        start, half = which
        out = []
        for c in range(2):
            a, b = max(lo, c * half), min(hi, (c + 1) * half)
            if a < b:
                out.append(held[c, start + a - c * half : start + b - c * half])
        return out[0] if len(out) == 1 else jnp.concatenate(out, axis=0)

    low_a, low_f = (0, cut_f), (cut_f, planes * r_f)
    for layer, attn, ff, ff_at in ((0, low_a, low_f, 0), (1, None, None, 288)):
        packed[layer] = rows(attn, 0, 192)
        mixer_g[layer] = rows(attn, 192, 256)
        expand[layer] = rows(ff, ff_at, ff_at + 256)
        for c in range(4):
            at = ff_at + 256 + 64 * c
            reduce_g[layer, :, c * 256 : (c + 1) * 256] = rows(ff, at, at + 64)
        vectors = rows(attn, 256, 288)
        mine_lanes = vectors[:, :64]
        for s in range(1, 4):
            mine_lanes = jnp.where(me == s, vectors[:, 64 * s : 64 * (s + 1)], mine_lanes)
        gain[layer] = mine_lanes[GAIN : GAIN + 2]
        shift[layer] = mine_lanes[SHIFT : SHIFT + 2]
        entry[layer] = mine_lanes[ENTRY : ENTRY + 2]
        branch[layer] = mine_lanes[BRANCH : BRANCH + 2]
        for t in range(10):
            taps[t, layer : layer + 1] = mine_lanes[TAPS + t : TAPS + t + 1]
        row = vectors[HIDDEN : HIDDEN + 1]
        for s in range(1, 4):
            row = jnp.where(me == s, vectors[HIDDEN + s : HIDDEN + s + 1], row)
        hidden_g[layer : layer + 1] = row


def body(patches, validity, norm_gain, norm_shift, qkv_weight, entry_bias, stencil, mixer_weight, branch_bias, expand_weight, hidden_bias, reduce_weight, cotangent):
    dp = lax.axis_size("dp")
    planes = dp // 2
    me, at_dp = lax.axis_index("mp"), lax.axis_index("dp")
    heights = jnp.sum(validity[:, :, 0], axis=1)
    widths = jnp.sum(validity[:, 0, :], axis=1)
    place = jnp.stack([me, at_dp % 2, at_dp // 2, at_dp]).astype(jnp.int32)
    sizes = jnp.concatenate([jnp.stack([me, at_dp % 2]), jnp.stack([heights, widths], axis=1).reshape(-1)]).astype(jnp.int32)

    qkv_t = jnp.transpose(qkv_weight, (0, 2, 3, 1)).reshape(2, 192, D)
    mixer_t = jnp.transpose(mixer_weight, (0, 2, 1))
    reduce_t = jnp.transpose(reduce_weight, (0, 2, 1))
    vectors = (norm_gain, norm_shift, entry_bias, jnp.transpose(stencil, (1, 0, 2)), branch_bias, hidden_bias)

    arrays = [qkv_t, mixer_t, norm_gain, norm_shift, entry_bias, jnp.transpose(stencil, (1, 0, 2)), branch_bias, hidden_bias, expand_weight, reduce_t]
    r_t, r_f = part_rows(UNIT, dp), part_rows(FF_ROWS, dp)
    outs = [(HALF_ATTN + r_t, D), (HALF_FF, D), (2, 32, D)]
    half_a0, half_f0, vec = local_call(
        pack_kernel, "pack", place, arrays, [(dims, bf16) for dims in outs], [v((dp * r_t, D), bf16)]
    )
    attn_own, ff_own = [qkv_t, mixer_t, vec], [expand_weight, reduce_t]

    near_a0 = turn_all(half_a0)
    near_1 = jnp.stack([x[HALF_ATTN:] for x in near_a0])
    near_f0 = turn_all(half_f0)
    far_a0 = swap_core(near_a0)
    x, top_grad = to_rows(patches), to_rows(cotangent)
    near_1, x = lax.optimization_barrier((near_1, x))
    rest_1 = lax.all_gather(near_1, "dp", axis=0, tiled=False)
    middle, again, packed, probs, mixed, value, wqkv, wm, sm = attn_fwd_call(sizes, x, attn_own + near_a0 + far_a0)
    near_f0, middle = lax.optimization_barrier((near_f0, middle))
    far_f0 = swap_core(near_f0)
    state, we, wr = ff_fwd_call(sizes, middle, sm, ff_own + near_f0 + far_f0)
    output, grad, grads_1 = top_call(sizes, state, top_grad, attn_own + ff_own + [rest_1], dp, r_t)
    sums_1 = lax.psum_scatter(grads_1, "dp", scatter_dimension=0, tiled=False)

    grad_mid, keep_f, give_f, vec = ff_bwd_call(place, grad, again, we, wr, sm, planes, r_f)
    got_f = swap_dp(give_f, 1)
    parts_f = to_planes(keep_f, got_f, place[2])
    grad_mid, parts_f = lax.optimization_barrier((grad_mid, parts_f))
    planes_f = swap_planes(parts_f)
    patch_grad, keep_a, give_a = attn_bwd_call(place, grad_mid, x, packed, probs, mixed, value, wqkv, wm, sm, vec)
    planes_f, keep_a, give_a = lax.optimization_barrier((planes_f, keep_a, give_a))

    got_a = swap_dp(give_a, 1)
    shards_a = to_shards([keep_a[0], got_a[0]], me)
    mp_a = turn_shards(shards_a)
    planes_f, sums_1 = lax.optimization_barrier((planes_f, sums_1, shards_a))[:2]
    low = add_up(planes_f).astype(bf16)
    mp_f = turn_shards(to_shards([jnp.concatenate([low, sums_1], axis=1)], me))
    share = jnp.concatenate([add_up(mp_a), add_up(mp_f)], axis=0).astype(bf16)
    mine = swap_planes([share] * planes)
    other = swap_core(mine)
    outs = [(2, 192, D), (2, 64, D), (2, D, D), (2, 64, FF), (2, 2, 64), (2, 2, 64), (2, 2, 64), (10, 2, 64), (2, 2, 64), (2, D)]
    cut_f = LOW_ROWS // 2
    cut_t = cut_f + r_f
    held = [v((2, cut_f + planes * r_f, D), f32), v((dp * r_t, D), f32)]
    packed_g, mixer_g, expand_g, reduce_g, gain_g, shift_g, entry_g, taps_g, branch_g, hidden_g = held_call(
        functools.partial(unpack_kernel, planes, cut_f, cut_t), "unpack", place, mine + other, [(dims, f32) for dims in outs], held, 2, 16
    )
    return (
        from_rows(output), from_rows(patch_grad), gain_g, shift_g,
        jnp.transpose(packed_g.reshape(2, 3, 64, D), (0, 3, 1, 2)), entry_g, jnp.transpose(taps_g, (1, 0, 2)),
        jnp.transpose(mixer_g, (0, 2, 1)), branch_g, expand_g, hidden_g, jnp.transpose(reduce_g, (0, 2, 1)),
    )


def solution(mesh):
    crops = P(("dp", "mp"), None, None, None)
    lanes = P(None, None, "mp")
    deep = P(None, None, None, "mp")
    return jax.shard_map(
        body,
        mesh=mesh,
        in_specs=(crops, P(("dp", "mp"), None, None), lanes, lanes, deep, lanes, lanes, lanes, lanes, lanes, P(None, "mp"), lanes, crops),
        out_specs=(crops, crops, lanes, lanes, deep, lanes, lanes, lanes, lanes, lanes, P(None, "mp"), lanes),
        check_vma=False,
    )
```
